32 devices in a mesh: section: 4 (over y, x), dom: 8 (over z, core).
Axes of the slice: x: 2, y: 2, z: 4, core: 2. Of those that a mesh axis runs over, the one named last changes fastest.
Arguments:
- layer_inputs: bfloat16 [4, 1, 3072, 512], P('section', None, 'dom'), may hold values from -6 to 6
- top_grad: bfloat16 [1, 3072, 512], P(None, 'dom'), may hold values from -6 to 6
- w_qkv: bfloat16 [4, 512, 1536], P('section')
- w_out: bfloat16 [4, 512, 512], P('section'), may hold values from -0.25 to 0.25
- neighbours: int32 [24, 3], P('dom'), may hold values from -1 to 23, as said below
Outputs:
- input_grads: bfloat16 [4, 1, 3072, 512], P('section', None, 'dom')
- qkv_grad: float32 [4, 512, 1536], P('section', 'dom')
- out_grad: float32 [4, 512, 512], P('section', 'dom')
The draws below stay inside these ranges and needn't reach their ends.
Inputs may be any that keep to these rules, and one draw needn't show every extreme that they name: `neighbours`: entry 0 of block b is b; the other entries name distinct blocks (b + o) mod 24 with 0 < |o| <= 1, then -1 to the end of the row. The first block of every index of dom lists 3 blocks.
All inputs are finite; a program needn't handle non-finite values.
Results may differ from the reference program's by a relative error of at most 0.017.
Values may be sent and summed in bfloat16 or wider, within the bound.
No kernel may reach another device: no remote copies, remote signals or barrier semaphores. Data moves between devices by JAX's collectives and lax.ppermute only.
A program may use at most 128 MiB of HBM per device.

```python
import jax
import jax.numpy as jnp
from jax import lax

D = 512
HEADS = 8
TILE = 128
KMAX = 3
HALO = 1
BLK_DEV = 3
MICRO = 1
LAYERS = 4
BLOCKS = 24
NODES = 3072
N_DOM = 8


def draw_w_qkv(key, part):
    first = jax.random.fold_in(key, 0)
    base = jax.random.normal(first, (LAYERS, D, 3 * D), jnp.float32) * D ** (-0.5)
    return base.astype(jnp.bfloat16)


def draw_neighbours(key, part):
    first, second, third = jax.random.split(key, 3)
    devices = BLOCKS // BLK_DEV
    level = jax.random.randint(first, (devices,), 1, KMAX + 1)
    level = jnp.repeat(level, BLK_DEV)
    jitter = jax.random.randint(second, (BLOCKS,), -1, 2)
    count = jnp.clip(level + jitter, 1, KMAX)
    place = jnp.arange(BLOCKS)
    count = jnp.where(place % BLK_DEV == 0, KMAX, count)
    count = count.at[1].set(1)
    offsets = jnp.concatenate([jnp.arange(-HALO, 0), jnp.arange(1, HALO + 1)])
    scores = jax.random.randint(third, (BLOCKS, 2 * HALO), 0, 1 << 20) * (2 * HALO) + jnp.arange(2 * HALO)[None, :]
    order = jnp.argsort(scores, axis=1)
    chosen = offsets[order[:, :KMAX - 1]]
    ids = (place[:, None] + chosen) % BLOCKS
    keep = jnp.arange(1, KMAX)[None, :] < count[:, None]
    rest = jnp.where(keep, ids, -1)
    return jnp.concatenate([place[:, None], rest], axis=1).astype(jnp.int32)


def block_scale(rng, shape, cuts, low, top_value):
    factor_of, own = 1.0, jax.random.fold_in(rng, 6)
    for position, blocks in cuts:
        heights = jnp.exp(jax.random.uniform(jax.random.fold_in(own, position), (blocks,), jnp.float32, low / len(cuts), top_value / len(cuts)))
        factor_of = factor_of * jnp.repeat(heights, shape[position] // blocks).reshape([-1 if axis == position else 1 for axis in range(len(shape))])
    return factor_of


def gaussian(rng, shape, deviation, limit, cuts=(), dtype=jnp.bfloat16):
    result = jax.random.normal(rng, shape, jnp.float32) * deviation
    if len(cuts) > 0:
        result = block_scale(rng, shape, cuts, -0.22, 0.18) * result
    return jnp.clip(result, min=-limit, max=limit).astype(dtype)


def setup_inputs(seed: int = 0) -> dict:
    arg_keys = jax.random.split(jax.random.key(seed), 6)
    return {
        "layer_inputs": gaussian(arg_keys[0], (LAYERS, MICRO, NODES, D), 1.0, 6.0, ((0, 4), (2, 8))),
        "top_grad": gaussian(arg_keys[1], (MICRO, NODES, D), 1.0, 6.0, ((1, 8),)),
        "w_qkv": draw_w_qkv(jax.random.fold_in(arg_keys[5], 71), 0),
        "w_out": gaussian(arg_keys[3], (LAYERS, D, D), D ** -0.5, 0.25, ((0, 4),)),
        "neighbours": draw_neighbours(jax.random.fold_in(arg_keys[5], 71), 0),
    }


def layer_reference(x, g, w_qkv, w_out, neighbours):
    blocks = x.shape[0] // TILE
    width = x.shape[1]
    hdim = width // HEADS
    scale = 1.0 / hdim ** 0.5
    xf = x.astype(jnp.float32)
    mean_value = lax.optimization_barrier(jnp.mean(xf, axis=-1, keepdims=True))
    centered_input = xf - mean_value
    inverse_deviation = jax.lax.rsqrt(lax.optimization_barrier(jnp.mean(centered_input * centered_input, axis=-1, keepdims=True)) + 1e-05)
    normalized_input = centered_input * inverse_deviation
    normed_rows = normalized_input.astype(jnp.bfloat16)
    qkv = jnp.dot(normed_rows, w_qkv, preferred_element_type=jnp.float32).astype(jnp.bfloat16)
    qkv = qkv.reshape(blocks, TILE, 3 * width)
    query = qkv[..., :width].reshape(blocks, TILE, HEADS, hdim)
    keyval = qkv[..., width:]
    valid = neighbours >= 0
    where_at = jnp.where(valid, neighbours, 0).astype(jnp.int32)
    tiles = keyval[where_at]
    keys = tiles[..., :width].reshape(blocks, KMAX * TILE, HEADS, hdim)
    values = tiles[..., width:].reshape(blocks, KMAX * TILE, HEADS, hdim)
    mask = jnp.repeat(valid, TILE, axis=1)[:, None, None, :]
    scores = jnp.einsum('bqhd,bkhd->bhqk', query.astype(jnp.float32), keys.astype(jnp.float32)) * scale
    scores = jnp.where(mask, scores, -1e+30)
    top = lax.optimization_barrier(jnp.max(scores, axis=-1, keepdims=True))
    expo = jnp.exp(scores - top)
    probs = expo / lax.optimization_barrier(jnp.sum(expo, axis=-1, keepdims=True))
    probs_b = probs.astype(jnp.bfloat16)
    attn = jnp.einsum('bhqk,bkhd->bqhd', probs_b.astype(jnp.float32), values.astype(jnp.float32)).astype(jnp.bfloat16)
    attn = attn.reshape(blocks * TILE, width)
    out_term = jnp.dot(attn.T, g, preferred_element_type=jnp.float32)
    d_attn = jnp.dot(g, w_out.T, preferred_element_type=jnp.float32).astype(jnp.bfloat16)
    d_attn = d_attn.reshape(blocks, TILE, HEADS, hdim)
    d_prob = jnp.einsum('bqhd,bkhd->bhqk', d_attn.astype(jnp.float32), values.astype(jnp.float32))
    d_score = (probs * (d_prob - lax.optimization_barrier(jnp.sum(d_prob * probs, axis=-1, keepdims=True))) * scale).astype(jnp.bfloat16)
    d_query = jnp.einsum('bhqk,bkhd->bqhd', d_score.astype(jnp.float32), keys.astype(jnp.float32))
    d_keys = jnp.einsum('bhqk,bqhd->bkhd', d_score.astype(jnp.float32), query.astype(jnp.float32))
    d_values = jnp.einsum('bhqk,bqhd->bkhd', probs_b.astype(jnp.float32), d_attn.astype(jnp.float32))
    d_tiles = jnp.concatenate([d_keys.reshape(blocks, KMAX, TILE, width), d_values.reshape(blocks, KMAX, TILE, width)], axis=-1)
    source = (jnp.arange(blocks) // BLK_DEV).astype(jnp.int32)[:, None]
    target = (where_at // BLK_DEV).astype(jnp.int32)
    same = valid & (source == target)
    from_next = valid & (source == (target + 1) % N_DOM)
    from_prev = valid & (source == (target - 1) % N_DOM)

    def collect(select):
        terms = (d_tiles * select[:, :, None, None].astype(jnp.float32)).reshape(blocks * KMAX, TILE, 2 * width)
        return jax.ops.segment_sum(terms, where_at.reshape(-1), num_segments=blocks)
    d_keyval = collect(same) + collect(from_next).astype(jnp.bfloat16).astype(jnp.float32)
    d_keyval = d_keyval + collect(from_prev).astype(jnp.bfloat16).astype(jnp.float32)
    d_qkv = jnp.concatenate([d_query.reshape(blocks, TILE, width), d_keyval], axis=-1).astype(jnp.bfloat16)
    d_qkv = d_qkv.reshape(blocks * TILE, 3 * width)
    qkv_term = jnp.dot(normed_rows.T, d_qkv, preferred_element_type=jnp.float32)
    normed_gradient = jnp.dot(d_qkv, w_qkv.T, preferred_element_type=jnp.float32)
    layernorm_gradient = inverse_deviation * (normed_gradient - lax.optimization_barrier(jnp.mean(normed_gradient, axis=-1, keepdims=True)) - normalized_input * lax.optimization_barrier(jnp.mean(normed_gradient * normalized_input, axis=-1, keepdims=True)))
    d_input = (g.astype(jnp.float32) + layernorm_gradient).astype(jnp.bfloat16)
    return (d_input, qkv_term, out_term)

def reference(layer_inputs, top_grad, w_qkv, w_out, neighbours):
    grads = [[None] * MICRO for layer in range(LAYERS)]
    qkv_sums = [jnp.zeros(w_qkv.shape[1:], jnp.float32) for layer in range(LAYERS)]
    out_sums = [jnp.zeros(w_out.shape[1:], jnp.float32) for layer in range(LAYERS)]
    for micro_idx in range(MICRO):
        g = top_grad[micro_idx]
        for layer in range(LAYERS - 1, -1, -1):
            g, qkv_term, out_term = layer_reference(layer_inputs[layer, micro_idx], g, w_qkv[layer], w_out[layer], neighbours)
            grads[layer][micro_idx] = g
            qkv_sums[layer] = qkv_sums[layer] + qkv_term
            out_sums[layer] = out_sums[layer] + out_term
    input_grads = jnp.stack([jnp.stack(row) for row in grads])
    return (input_grads, jnp.stack(qkv_sums), jnp.stack(out_sums))
```

```python
import functools

import jax
import jax.numpy as jnp
from jax import lax
from jax.experimental import pallas as pl
from jax.experimental.pallas import tpu as pltpu
from jax.sharding import PartitionSpec as P

HEADS = 8
EPS = 1e-05
F32 = jnp.float32
BF16 = jnp.bfloat16
NN = (((1,), (0,)), ((), ()))
NT = (((1,), (1,)), ((), ()))
VMEM_LIMIT = 40 * 1024 * 1024


def mm(a, b, dims=NN):
    return lax.dot_general(a, b, dims, preferred_element_type=F32)


def prelude_kernel(
    blk, tile, flags, x_lo, x, x_hi, top, w_qkv,
    xn_t, inv, v_nat, k_t, q_t, probs, attn_t, g_t, k_nat, v_t,
):
    width = x.shape[1]
    hdim = width // HEADS
    scale = 1.0 / hdim**0.5
    for t in range(blk + 2):
        if t == 0:
            rows = x_lo[...]
        elif t == blk + 1:
            rows = x_hi[...]
        else:
            rows = x[(t - 1) * tile : t * tile, :]
        here = slice(t * tile, (t + 1) * tile)
        xf = rows.astype(F32)
        cent = xf - jnp.mean(xf, axis=-1, keepdims=True)
        rstd = lax.rsqrt(jnp.mean(cent * cent, axis=-1, keepdims=True) + EPS)
        xhat = cent * rstd
        xn = xhat.astype(BF16)
        xn_t[:, here] = xhat.T.astype(BF16)
        inv[:, here] = jnp.broadcast_to(rstd, (tile, 128)).T[0:8, :]
        keyval = mm(xn, w_qkv[:, width:])
        k_t[:, here] = (keyval[:, :width].T * scale).astype(BF16)
        v_t[:, here] = keyval[:, width:].T.astype(BF16)
        keyval = keyval.astype(BF16)
        for h in range(HEADS):
            k_nat[h, here, :] = keyval[:, h * hdim : (h + 1) * hdim]
            v_nat[h, here, :] = keyval[:, width + h * hdim : width + (h + 1) * hdim]
        if 0 < t <= blk:
            own = slice((t - 1) * tile, t * tile)
            query = mm(xn, w_qkv[:, :width])
            q_t[:, own] = (query.T * scale).astype(BF16)
            g_t[:, own] = jnp.where(
                flags[2 * blk] > 0, top[own, :].astype(F32).T, 0.0
            ).astype(BF16)
    for b in range(blk):
        own = slice(b * tile, (b + 1) * tile)
        near = slice(b * tile, (b + 3) * tile)
        for h in range(HEADS):
            head = slice(h * hdim, (h + 1) * hdim)
            s = mm(k_nat[h, near, :], q_t[head, own])
            s = jnp.concatenate(
                [
                    jnp.where(flags[b] > 0, s[:tile], -1e30),
                    s[tile : 2 * tile],
                    jnp.where(flags[blk + b] > 0, s[2 * tile :], -1e30),
                ],
                axis=0,
            )
            e = jnp.exp(s - jnp.max(s, axis=0, keepdims=True))
            p = (e * (1.0 / jnp.sum(e, axis=0, keepdims=True))).astype(BF16)
            probs[h, b] = p
            attn_t[head, own] = mm(v_t[head, near], p).astype(BF16)


def prelude(flags, x_lo, x, x_hi, top, w_qkv, blk):
    rows, width = x.shape
    tile = rows // blk
    hdim = width // HEADS
    ext = rows + 2 * tile
    vmem = pl.BlockSpec(memory_space=pltpu.VMEM)
    return pl.pallas_call(
        functools.partial(prelude_kernel, blk, tile),
        in_specs=[pl.BlockSpec(memory_space=pltpu.SMEM)] + [vmem] * 5,
        out_specs=[vmem] * 8,
        out_shape=[
            jax.ShapeDtypeStruct((width, ext), BF16),
            jax.ShapeDtypeStruct((8, ext), F32),
            jax.ShapeDtypeStruct((HEADS, ext, hdim), BF16),
            jax.ShapeDtypeStruct((width, ext), BF16),
            jax.ShapeDtypeStruct((width, rows), BF16),
            jax.ShapeDtypeStruct((HEADS, blk, 3 * tile, tile), BF16),
            jax.ShapeDtypeStruct((width, rows), BF16),
            jax.ShapeDtypeStruct((width, rows), BF16),
        ],
        scratch_shapes=[
            pltpu.VMEM((HEADS, ext, hdim), BF16),
            pltpu.VMEM((width, ext), BF16),
        ],
        compiler_params=pltpu.CompilerParams(vmem_limit_bytes=VMEM_LIMIT),
        name="prelude",
    )(flags, x_lo, x, x_hi, top, w_qkv)


def stage_kernel(
    blk, tile, g_prev, arrived, w_qkv, w_out, xn_t, inv, v_nat, k_t, q_t, probs, attn_t,
    g_t, y, c, d_qkv, da_t, d_own,
):
    width = g_prev.shape[0]
    rows = blk * tile
    hdim = width // HEADS
    g = (g_prev[...].astype(F32) + arrived[...].astype(F32)).astype(BF16)
    g_t[...] = g
    da_t[...] = mm(w_out[...], g).astype(BF16)
    for h in range(HEADS):
        head = slice(h * hdim, (h + 1) * hdim)
        dk = [None] * (blk + 2)
        dv = [None] * (blk + 2)
        for b in range(blk):
            own = slice(b * tile, (b + 1) * tile)
            near = slice(b * tile, (b + 3) * tile)
            da = da_t[head, own]
            total = jnp.sum(da.astype(F32) * attn_t[head, own].astype(F32), axis=0, keepdims=True)
            p = probs[h, b]
            dp = mm(v_nat[h, near, :], da)
            ds = (p.astype(F32) * (dp - total)).astype(BF16)
            d_own[head, own] = mm(k_t[head, near], ds).astype(BF16)
            key_part = mm(q_t[head, own], ds, NT)
            value_part = mm(da, p, NT)
            for j in range(3):
                cols = slice(j * tile, (j + 1) * tile)
                t = b + j
                dk[t] = key_part[:, cols] if dk[t] is None else dk[t] + key_part[:, cols]
                dv[t] = value_part[:, cols] if dv[t] is None else dv[t] + value_part[:, cols]
        for t in range(blk + 2):
            here = slice(t * tile, (t + 1) * tile)
            d_qkv[width + h * hdim : width + (h + 1) * hdim, here] = dk[t].astype(BF16)
            d_qkv[2 * width + h * hdim : 2 * width + (h + 1) * hdim, here] = dv[t].astype(BF16)
    for t in (0, blk + 1):
        here = slice(t * tile, (t + 1) * tile)
        d_qkv[:width, here] = jnp.zeros((width, tile), BF16)
    d_qkv[:width, tile : tile + rows] = d_own[...]
    for t in range(blk + 2):
        here = slice(t * tile, (t + 1) * tile)
        dn = mm(w_qkv[...], d_qkv[:, here])
        xhat = xn_t[:, here].astype(F32)
        first = jnp.mean(dn, axis=0, keepdims=True)
        second = jnp.mean(dn * xhat, axis=0, keepdims=True)
        out = inv[0:1, here] * (dn - first - xhat * second)
        if t == 0:
            c[0] = out.astype(BF16)
        elif t == blk + 1:
            c[1] = out.astype(BF16)
        else:
            own = slice((t - 1) * tile, t * tile)
            y[:, own] = (g[:, own].astype(F32) + out).astype(BF16)


def stage(g_prev, arrived, w_qkv, w_out, saved, blk):
    xn_t, inv, v_nat, k_t, q_t, probs, attn_t = saved
    width, rows = g_prev.shape
    tile = rows // blk
    ext = rows + 2 * tile
    vmem = pl.BlockSpec(memory_space=pltpu.VMEM)
    return pl.pallas_call(
        functools.partial(stage_kernel, blk, tile),
        in_specs=[vmem] * 11,
        out_specs=[vmem] * 4,
        out_shape=[
            jax.ShapeDtypeStruct((width, rows), BF16),
            jax.ShapeDtypeStruct((width, rows), BF16),
            jax.ShapeDtypeStruct((2, width, tile), BF16),
            jax.ShapeDtypeStruct((3 * width, ext), BF16),
        ],
        scratch_shapes=[pltpu.VMEM((width, rows), BF16), pltpu.VMEM((width, rows), BF16)],
        compiler_params=pltpu.CompilerParams(vmem_limit_bytes=VMEM_LIMIT),
        name="stage",
    )(g_prev, arrived, w_qkv, w_out, xn_t, inv, v_nat, k_t, q_t, probs, attn_t)


def weights_kernel(xn_t, d_qkv, attn_t, g_t, out):
    wide = d_qkv.shape[0]
    out[:, :wide] = mm(xn_t[...], d_qkv[...], NT).astype(BF16)
    out[:, wide:] = mm(attn_t[...], g_t[...], NT).astype(BF16)


def weights(xn_t, d_qkv, attn_t, g_t):
    width = g_t.shape[0]
    wide = d_qkv.shape[0]
    vmem = pl.BlockSpec(memory_space=pltpu.VMEM)
    return pl.pallas_call(
        weights_kernel,
        in_specs=[vmem] * 4,
        out_specs=vmem,
        out_shape=jax.ShapeDtypeStruct((width, wide + width), BF16),
        compiler_params=pltpu.CompilerParams(vmem_limit_bytes=VMEM_LIMIT),
        name="weights",
    )(xn_t, d_qkv, attn_t, g_t)


def ring(parts, distance):
    return [(i, (i + distance) % parts) for i in range(parts)]


def sum_scatter(term):
    parts = lax.axis_size("dom")
    if parts != 8:
        return lax.psum_scatter(term.astype(F32), "dom", scatter_dimension=0, tiled=True)
    me = lax.axis_index("dom")
    core, chip = me % 2, me // 2
    split = term.reshape(parts // 2, 2, term.shape[0] // parts, term.shape[1])
    keep = lax.dynamic_index_in_dim(split, core, 1, keepdims=False)
    give = lax.dynamic_index_in_dim(split, 1 - core, 1, keepdims=False)
    got = lax.ppermute(give, "dom", [(i, i ^ 1) for i in range(parts)])
    both = keep.astype(F32) + got.astype(F32)
    rounded = both.astype(BF16)
    total = lax.dynamic_index_in_dim(both, chip, 0, keepdims=False)
    pieces = []
    for k in range(1, parts // 2):
        give = lax.dynamic_index_in_dim(rounded, chip ^ k, 0, keepdims=False)
        pieces.append(lax.ppermute(give, "dom", [(i, i ^ (2 * k)) for i in range(parts)]))
    for piece in pieces:
        total = total + piece.astype(F32)
    return total


def local(layer_inputs, top_grad, w_qkv, w_out, neighbours):
    sections = lax.axis_size("section")
    section_me = lax.axis_index("section")
    parts = lax.axis_size("dom")
    me = lax.axis_index("dom")
    blk = neighbours.shape[0]
    rows, width = top_grad.shape[1:]
    tile = rows // blk
    x = layer_inputs[0, 0]
    w_in, w_back = w_qkv[0], w_out[0]
    x_lo = lax.ppermute(x[rows - tile :], "dom", ring(parts, 1))
    x_hi = lax.ppermute(x[:tile], "dom", ring(parts, -1))
    blocks = blk * parts
    mine = (me * blk + jnp.arange(blk))[:, None]
    others = neighbours[:, 1:]
    has_lo = jnp.any(others == (mine - 1) % blocks, axis=1)
    has_hi = jnp.any(others == (mine + 1) % blocks, axis=1)
    is_last = (section_me == sections - 1)[None]
    flags = jnp.concatenate([has_lo, has_hi, is_last]).astype(jnp.int32)
    *saved, g = prelude(flags, x_lo, x, x_hi, top_grad[0], w_in, blk)
    arrived = jnp.zeros_like(g)
    for k in range(sections):
        g, y, c, d_qkv = stage(g, arrived, w_in, w_back, saved, blk)
        if k == sections - 1:
            term = weights(saved[0], d_qkv, saved[6], g)
            summed = sum_scatter(term)
        from_prev = lax.ppermute(c[1], "dom", ring(parts, 1))
        from_next = lax.ppermute(c[0], "dom", ring(parts, -1))
        rims = jnp.concatenate(
            [from_prev, jnp.zeros((width, rows - 2 * tile), BF16), from_next], axis=1
        )
        y = (y.astype(F32) + rims.astype(F32)).astype(BF16)
        if k < sections - 1:
            arrived = lax.ppermute(y, "section", [(sections - 1 - k, sections - 2 - k)])
    return (y.T[None, None], summed[None, :, : 3 * width], summed[None, :, 3 * width :])


def solution(mesh):
    placed = (
        P("section", None, "dom", None),
        P(None, "dom", None),
        P("section", None, None),
        P("section", None, None),
        P("dom", None),
    )
    return jax.shard_map(
        local,
        mesh=mesh,
        in_specs=placed,
        out_specs=(
            P("section", None, "dom", None),
            P("section", "dom", None),
            P("section", "dom", None),
        ),
        check_vma=False,
    )
```

```python
import functools

import jax
import jax.numpy as jnp
from jax import lax
from jax.experimental import pallas as pl
from jax.experimental.pallas import tpu as pltpu
from jax.sharding import PartitionSpec as P

HEADS = 8
EPS = 1e-05
F32 = jnp.float32
BF16 = jnp.bfloat16
NN = (((1,), (0,)), ((), ()))
NT = (((1,), (1,)), ((), ()))
VMEM_LIMIT = 20 * 1024 * 1024


def mm(a, b, dims=NN):
    return lax.dot_general(a, b, dims, preferred_element_type=F32)


def cols(start, count=1, tile=128):
    return slice(start * tile, (start + count) * tile)


def call(kernel, name, outs, args, scratch=(), smem=0):
    vmem = pl.BlockSpec(memory_space=pltpu.VMEM)
    scalars = pl.BlockSpec(memory_space=pltpu.SMEM)
    return pl.pallas_call(
        kernel,
        in_specs=[scalars] * smem + [vmem] * (len(args) - smem),
        out_specs=[vmem] * len(outs),
        out_shape=[jax.ShapeDtypeStruct(shape, dtype) for shape, dtype in outs],
        scratch_shapes=[pltpu.VMEM(shape, dtype) for shape, dtype in scratch],
        compiler_params=pltpu.CompilerParams(vmem_limit_bytes=VMEM_LIMIT),
        name=name,
    )(*args)


def halves(pair, hdim):
    zero = jnp.zeros((hdim, pair.shape[1]), pair.dtype)
    return jnp.concatenate(
        [
            jnp.concatenate([pair[:hdim], zero], axis=0),
            jnp.concatenate([zero, pair[hdim:]], axis=0),
        ],
        axis=1,
    )


def normalize(rows):
    xf = rows.astype(F32)
    cent = xf - jnp.mean(xf, axis=-1, keepdims=True)
    rstd = lax.rsqrt(jnp.mean(cent * cent, axis=-1, keepdims=True) + EPS)
    return cent * rstd, rstd


def project_tile(t, tile, scale, rows, w_qkv, xn_t, inv, k_nat, v_nat, k_t, v_t):
    width = rows.shape[1]
    here = cols(t, tile=tile)
    xhat, rstd = normalize(rows)
    xn = xhat.astype(BF16)
    xn_t[:, here] = xhat.T.astype(BF16)
    inv[:, here] = jnp.broadcast_to(rstd, (tile, 128)).T[0:8, :]
    keyval = mm(xn, w_qkv[:, width:])
    k_t[:, here] = (keyval[:, :width].T * scale).astype(BF16)
    v_t[:, here] = keyval[:, width:].T.astype(BF16)
    k_nat[here, :] = keyval[:, :width].astype(BF16)
    v_nat[here, :] = keyval[:, width:].astype(BF16)
    return xn


def prelude_own_kernel(
    blk, tile, scale, x, top, w_qkv, xn_t, inv, k_nat, v_nat, k_t, v_t, q_t, g_t
):
    width = x.shape[1]
    is_last = lax.axis_index("section") == lax.axis_size("section") - 1
    for b in range(blk):
        own = cols(b, tile=tile)
        xn = project_tile(
            b, tile, scale, x[own, :], w_qkv, xn_t, inv, k_nat, v_nat, k_t, v_t
        )
        q_t[:, own] = (mm(xn, w_qkv[:, :width]).T * scale).astype(BF16)
        g_t[:, own] = jnp.where(is_last, top[own, :].astype(F32).T, 0.0).astype(BF16)


def prelude_kernel(
    blk, tile, scale, neighbours, x_lo, x_hi, w_qkv, xn_own, inv_own, k_own, v_own, kt_own, vt_own, q_t,
    xn_t, inv, v_nat, k_t, probs, attn_t, k_nat, v_t, scores,
):
    width = x_lo.shape[1]
    hdim = width // HEADS
    ours = cols(1, blk, tile)
    xn_t[:, ours] = xn_own[...]
    inv[:, ours] = inv_own[...]
    k_nat[ours, :] = k_own[...]
    v_nat[ours, :] = v_own[...]
    k_t[:, ours] = kt_own[...]
    v_t[:, ours] = vt_own[...]
    for t, rows in ((0, x_lo), (blk + 1, x_hi)):
        project_tile(t, tile, scale, rows[...], w_qkv, xn_t, inv, k_nat, v_nat, k_t, v_t)
    blocks = blk * lax.axis_size("dom")
    for b in range(blk):
        mine = lax.axis_index("dom") * blk + b
        below, above = lax.rem(mine + blocks - 1, blocks), lax.rem(mine + 1, blocks)
        has_lo = has_hi = False
        for j in range(1, neighbours.shape[1]):
            has_lo |= neighbours[b, j] == below
            has_hi |= neighbours[b, j] == above
        for i in range(HEADS // 2):
            lanes = cols(i, tile=2 * hdim)
            q = halves(q_t[lanes, cols(b, tile=tile)], hdim)
            s = mm(k_nat[cols(b, 3, tile), lanes], q)
            scores[i, b] = jnp.concatenate(
                [
                    jnp.where(has_lo, s[:tile], -1e30),
                    s[tile : 2 * tile],
                    jnp.where(has_hi, s[2 * tile :], -1e30),
                ],
                axis=0,
            )
    for b in range(blk):
        for i in range(HEADS // 2):
            s = scores[i, b]
            e = jnp.exp(s - jnp.max(s, axis=0, keepdims=True))
            probs[i, b] = (e * (1.0 / jnp.sum(e, axis=0, keepdims=True))).astype(BF16)
    for b in range(blk):
        for h in range(HEADS):
            head = cols(h, tile=hdim)
            p = probs[h // 2, b, :, cols(h % 2, tile=tile)]
            attn_t[head, cols(b, tile=tile)] = mm(v_t[head, cols(b, 3, tile)], p).astype(BF16)


def score_grads(blk, tile, hdim, g, w_out, v_nat, probs, attn_t, da_t, ds):
    da_t[...] = mm(w_out[...], g).astype(BF16)
    for b in range(blk):
        own = cols(b, tile=tile)
        for i in range(HEADS // 2):
            lanes = cols(i, tile=2 * hdim)
            da = da_t[lanes, own]
            prod = da.astype(F32) * attn_t[lanes, own].astype(F32)
            total = jnp.concatenate(
                [
                    jnp.sum(prod[:hdim], axis=0, keepdims=True),
                    jnp.sum(prod[hdim:], axis=0, keepdims=True),
                ],
                axis=1,
            )
            dp = mm(v_nat[cols(b, 3, tile), lanes], halves(da, hdim))
            ds[i, b] = (probs[i, b].astype(F32) * (dp - total)).astype(BF16)


def rim_terms(blk, tile, hdim, q_t, da_t, probs, ds, d_qkv):
    width = q_t.shape[0]
    for side, b, j in ((0, 0, 0), (1, blk - 1, 2)):
        own, near, here = cols(b, tile=tile), cols(j, tile=tile), cols(side, tile=tile)
        for i in range(HEADS // 2):
            lanes = cols(i, tile=2 * hdim)
            after = slice(width + i * 2 * hdim, width + (i + 1) * 2 * hdim)
            d_qkv[lanes, here] = mm(halves(q_t[lanes, own], hdim), ds[i, b, near, :], NT).astype(BF16)
            d_qkv[after, here] = mm(
                halves(da_t[lanes, own], hdim), probs[i, b, near, :], NT
            ).astype(BF16)


def own_terms(blk, tile, hdim, first, last, q_t, k_t, da_t, probs, ds, d_qkv):
    width = q_t.shape[0]
    for i in range(HEADS // 2):
        lanes = cols(i, tile=2 * hdim)
        dk = [None] * (blk + 2)
        dv = [None] * (blk + 2)
        for b in range(blk):
            own = cols(b, tile=tile)
            low, high = max(b, first), min(b + 3, last + 1)
            near = slice((low - b) * tile, (high - b) * tile)
            key_part = mm(halves(q_t[lanes, own], hdim), ds[i, b, near, :], NT)
            value_part = mm(halves(da_t[lanes, own], hdim), probs[i, b, near, :], NT)
            for t in range(low, high):
                part = cols(t - low, tile=tile)
                dk[t] = key_part[:, part] if dk[t] is None else dk[t] + key_part[:, part]
                dv[t] = value_part[:, part] if dv[t] is None else dv[t] + value_part[:, part]
            for h in (2 * i, 2 * i + 1):
                head = cols(h, tile=hdim)
                d_qkv[head, cols(b + 1 - first, tile=tile)] = mm(
                    k_t[head, cols(b, 3, tile)], ds[i, b, :, cols(h % 2, tile=tile)]
                ).astype(BF16)
        for t in range(first, last + 1):
            here = cols(t - first, tile=tile)
            d_qkv[width + i * 2 * hdim : width + (i + 1) * 2 * hdim, here] = dk[t].astype(BF16)
            d_qkv[2 * width + i * 2 * hdim : 2 * width + (i + 1) * 2 * hdim, here] = dv[t].astype(
                BF16
            )


def norm_grad(dn, xn, rstd):
    xhat = xn.astype(F32)
    first = jnp.mean(dn, axis=0, keepdims=True)
    second = jnp.mean(dn * xhat, axis=0, keepdims=True)
    return rstd * (dn - first - xhat * second)


def stage_first_kernel(
    blk, tile, g_prev, arrived, w_qkv, w_out, xn_t, inv, v_nat, q_t, probs, attn_t,
    g_t, da_t, ds, c_lo, c_hi, d_rim,
):
    width = g_prev.shape[0]
    hdim = width // HEADS
    g = (g_prev[...].astype(F32) + arrived[...].astype(F32)).astype(BF16)
    g_t[...] = g
    score_grads(blk, tile, hdim, g, w_out, v_nat, probs, attn_t, da_t, ds)
    rim_terms(blk, tile, hdim, q_t, da_t, probs, ds, d_rim)
    dn = mm(w_qkv[:, width:], d_rim[...])
    for side, t, c in ((0, 0, c_lo), (1, blk + 1, c_hi)):
        here = cols(t, tile=tile)
        c[...] = norm_grad(
            dn[:, cols(side, tile=tile)], xn_t[:, here], inv[0:1, here]
        ).astype(BF16)


def stage_second_kernel(
    blk, tile, g_t, da_t, ds, w_qkv, xn_t, inv, k_t, q_t, probs, y, d_qkv
):
    width = g_t.shape[0]
    hdim = width // HEADS
    own_terms(blk, tile, hdim, 1, blk, q_t, k_t, da_t, probs, ds, d_qkv)
    dn = mm(w_qkv[...], d_qkv[...])
    for b in range(blk):
        own, here = cols(b, tile=tile), cols(b + 1, tile=tile)
        out = norm_grad(dn[:, own], xn_t[:, here], inv[0:1, here])
        y[:, own] = (g_t[:, own].astype(F32) + out).astype(BF16)


def last_terms_kernel(
    blk, tile, g_prev, arrived, w_out, v_nat, k_t, q_t, probs, attn_t, g_t, d_qkv, da_t, ds
):
    width = g_prev.shape[0]
    hdim = width // HEADS
    g = (g_prev[...].astype(F32) + arrived[...].astype(F32)).astype(BF16)
    g_t[...] = g
    score_grads(blk, tile, hdim, g, w_out, v_nat, probs, attn_t, da_t, ds)
    for t in (0, blk + 1):
        d_qkv[:width, cols(t, tile=tile)] = jnp.zeros((width, tile), BF16)
    own_terms(blk, tile, hdim, 0, blk + 1, q_t, k_t, da_t, probs, ds, d_qkv)


def last_input_kernel(blk, tile, after, g_t, d_qkv, w_qkv, xn_t, inv, y, c_lo, c_hi):
    dn = mm(w_qkv[...], d_qkv[...])
    for t in range(blk + 2):
        here = cols(t, tile=tile)
        out = norm_grad(dn[:, here], xn_t[:, here], inv[0:1, here])
        if t == 0:
            c_lo[...] = out.astype(BF16)
        elif t == blk + 1:
            c_hi[...] = out.astype(BF16)
        else:
            own = cols(t - 1, tile=tile)
            y[:, own] = (g_t[:, own].astype(F32) + out).astype(BF16)


def finish_input_kernel(blk, tile, y_t, from_prev, from_next, out):
    for b in range(blk):
        own = cols(b, tile=tile)
        part = y_t[:, own].astype(F32)
        if b == 0:
            part = part + from_prev[...].astype(F32)
        if b == blk - 1:
            part = part + from_next[...].astype(F32)
        out[own, :] = part.T.astype(BF16)


def add_rims(blk, tile, y, from_prev, from_next, out):
    own = cols(0, tile=tile)
    out[...] = y[...]
    out[:, own] = (y[:, own].astype(F32) + from_prev[...].astype(F32)).astype(BF16)
    own = cols(blk - 1, tile=tile)
    out[:, own] = (out[:, own].astype(F32) + from_next[...].astype(F32)).astype(BF16)


def weight_rows(core, chips, rows, xn_t, d_qkv, attn_t, g_t):
    def picked(ref):
        starts = [pl.multiple_of((2 * z + core) * rows, rows) for z in range(chips)]
        return jnp.concatenate([ref[pl.ds(s, rows), :] for s in starts], axis=0)

    return mm(picked(xn_t), d_qkv[...], NT), mm(picked(attn_t), g_t[...], NT)


def give_kernel(chips, core, xn_t, d_qkv, attn_t, g_t, out):
    rows = xn_t.shape[0] // (2 * chips)
    wide = d_qkv.shape[0]
    if core is None:
        core = 1 - lax.rem(lax.axis_index("dom"), 2)
    a, b = weight_rows(core, chips, rows, xn_t, d_qkv, attn_t, g_t)
    for z in range(chips):
        out[z, :, :wide] = a[z * rows : (z + 1) * rows].astype(BF16)
        out[z, :, wide:] = b[z * rows : (z + 1) * rows].astype(BF16)


def keep_kernel(chips, xn_t, d_qkv, attn_t, g_t, got, *outs):
    *pieces, own, both = outs
    rows = xn_t.shape[0] // (2 * chips)
    wide = d_qkv.shape[0]
    me = lax.axis_index("dom")
    chip = me // 2
    a, b = weight_rows(lax.rem(me, 2), chips, rows, xn_t, d_qkv, attn_t, g_t)
    for z in range(chips):
        here = slice(z * rows, (z + 1) * rows)
        both[z, :, :wide] = a[here] + got[z, :, :wide].astype(F32)
        both[z, :, wide:] = b[here] + got[z, :, wide:].astype(F32)
    own[...] = both[chip]
    for k in range(1, chips):
        pieces[k - 1][...] = both[lax.bitwise_xor(chip, k)].astype(BF16)


def total_kernel(own, *refs):
    *pieces, first, second = refs
    total = own[...]
    for piece in pieces:
        total = total + piece[...].astype(F32)
    wide = first.shape[1]
    first[...] = total[:, :wide]
    second[...] = total[:, wide:]


def ring(parts, distance):
    return [(i, (i + distance) % parts) for i in range(parts)]


def weight_grads(xn_t, d_qkv, attn_t, g_t):
    parts = lax.axis_size("dom")
    width, wide = g_t.shape[0], d_qkv.shape[0]
    every = wide + width
    if parts != 8:
        rows = width // 2
        halves_of = []
        for core in (0, 1):
            out = call(
                functools.partial(give_kernel, 1, core), "weight_rows", [((1, rows, every), BF16)],
                [xn_t, d_qkv, attn_t, g_t],
            )[0]
            halves_of.append(out[0])
        term = jnp.concatenate(halves_of, axis=0).astype(F32)
        total = lax.psum_scatter(term, "dom", scatter_dimension=0, tiled=True)
        return total[:, :wide], total[:, wide:], g_t
    chips = parts // 2
    rows = width // parts
    give = call(
        functools.partial(give_kernel, chips, None), "give", [((chips, rows, every), BF16)],
        [xn_t, d_qkv, attn_t, g_t],
    )[0]
    got = lax.ppermute(give, "dom", [(i, i ^ 1) for i in range(parts)])
    *pieces, own = call(
        functools.partial(keep_kernel, chips), "keep",
        [((rows, every), BF16)] * (chips - 1) + [((rows, every), F32)],
        [xn_t, d_qkv, attn_t, g_t, got],
        scratch=[((chips, rows, every), F32)],
    )
    pieces = [
        lax.ppermute(piece, "dom", [(i, i ^ (2 * k)) for i in range(parts)])
        for k, piece in enumerate(pieces, 1)
    ]
    first, second = call(
        total_kernel, "total", [((rows, wide), F32), ((rows, width), F32)], [own, *pieces]
    )
    return first, second, own


def local(layer_inputs, top_grad, w_qkv, w_out, neighbours):
    sections = lax.axis_size("section")
    parts = lax.axis_size("dom")
    blk = neighbours.shape[0]
    rows, width = top_grad.shape[1:]
    tile = rows // blk
    ext = rows + 2 * tile
    hdim = width // HEADS
    scale = 1.0 / hdim**0.5
    x = layer_inputs[0, 0]
    w_in, w_back = w_qkv[0], w_out[0]
    x_lo = lax.ppermute(x[rows - tile :], "dom", ring(parts, 1))
    x_hi = lax.ppermute(x[:tile], "dom", ring(parts, -1))
    *kept, q_t, g_t = call(
        functools.partial(prelude_own_kernel, blk, tile, scale), "prelude_own",
        [
            ((width, rows), BF16), ((8, rows), F32), ((rows, width), BF16), ((rows, width), BF16),
            ((width, rows), BF16), ((width, rows), BF16), ((width, rows), BF16), ((width, rows), BF16),
        ],
        [x, top_grad[0], w_in],
    )
    pair_shape = (HEADS // 2, blk, 3 * tile, 2 * tile)
    xn_t, inv, v_nat, k_t, probs, attn_t = call(
        functools.partial(prelude_kernel, blk, tile, scale), "prelude",
        [
            ((width, ext), BF16), ((8, ext), F32), ((ext, width), BF16), ((width, ext), BF16),
            (pair_shape, BF16), ((width, rows), BF16),
        ],
        [neighbours, x_lo, x_hi, w_in, *kept, q_t],
        scratch=[((ext, width), BF16), ((width, ext), BF16), (pair_shape, F32)], smem=1,
    )
    arrived = jnp.zeros_like(g_t)
    for k in range(sections - 1):
        g_t, da_t, ds, c_lo, c_hi = call(
            functools.partial(stage_first_kernel, blk, tile), "stage_first",
            [((width, rows), BF16), ((width, rows), BF16), (pair_shape, BF16), ((width, tile), BF16), ((width, tile), BF16)],
            [g_t, arrived, w_in, w_back, xn_t, inv, v_nat, q_t, probs, attn_t],
            scratch=[((2 * width, 2 * tile), BF16)],
        )
        from_prev = lax.ppermute(c_hi, "dom", ring(parts, 1))
        from_next = lax.ppermute(c_lo, "dom", ring(parts, -1))
        y = call(
            functools.partial(stage_second_kernel, blk, tile), "stage_second",
            [((width, rows), BF16)],
            [g_t, da_t, ds, w_in, xn_t, inv, k_t, q_t, probs],
            scratch=[((3 * width, rows), BF16)],
        )[0]
        y = call(
            functools.partial(add_rims, blk, tile), "add_rims", [((width, rows), BF16)],
            [y, from_prev, from_next],
        )[0]
        arrived = lax.ppermute(y, "section", [(sections - 1 - k, sections - 2 - k)])
    g_t, d_qkv = call(
        functools.partial(last_terms_kernel, blk, tile), "last_terms",
        [((width, rows), BF16), ((3 * width, ext), BF16)],
        [g_t, arrived, w_back, v_nat, k_t, q_t, probs, attn_t],
        scratch=[((width, rows), BF16), (pair_shape, BF16)],
    )
    qkv_grad, out_grad, after = weight_grads(xn_t, d_qkv, attn_t, g_t)
    y, c_lo, c_hi = call(
        functools.partial(last_input_kernel, blk, tile), "last_input",
        [((width, rows), BF16), ((width, tile), BF16), ((width, tile), BF16)],
        [after, g_t, d_qkv, w_in, xn_t, inv],
    )
    from_prev = lax.ppermute(c_hi, "dom", ring(parts, 1))
    from_next = lax.ppermute(c_lo, "dom", ring(parts, -1))
    y = call(
        functools.partial(finish_input_kernel, blk, tile), "finish_input", [((rows, width), BF16)],
        [y, from_prev, from_next],
    )[0]
    return (y[None, None], qkv_grad[None], out_grad[None])


def solution(mesh):
    placed = (
        P("section", None, "dom", None),
        P(None, "dom", None),
        P("section", None, None),
        P("section", None, None),
        P("dom", None),
    )
    return jax.shard_map(
        local,
        mesh=mesh,
        in_specs=placed,
        out_specs=(
            P("section", None, "dom", None),
            P("section", "dom", None),
            P("section", "dom", None),
        ),
        check_vma=False,
    )
```

```python
import functools

import jax
import jax.numpy as jnp
from jax import lax
from jax.experimental import pallas as pl
from jax.experimental.pallas import tpu as pltpu
from jax.sharding import PartitionSpec as P

HEADS = 8
EPS = 1e-05
F32 = jnp.float32
BF16 = jnp.bfloat16
NN = (((1,), (0,)), ((), ()))
NT = (((1,), (1,)), ((), ()))
VMEM_LIMIT = 20 * 1024 * 1024


def mm(a, b, dims=NN):
    return lax.dot_general(a, b, dims, preferred_element_type=F32)


def cols(start, count=1, tile=128):
    return slice(start * tile, (start + count) * tile)


def call(kernel, name, outs, args, scratch=(), smem=0):
    vmem = pl.BlockSpec(memory_space=pltpu.VMEM)
    scalars = pl.BlockSpec(memory_space=pltpu.SMEM)
    return pl.pallas_call(
        kernel,
        in_specs=[scalars] * smem + [vmem] * (len(args) - smem),
        out_specs=[vmem] * len(outs),
        out_shape=[jax.ShapeDtypeStruct(shape, dtype) for shape, dtype in outs],
        scratch_shapes=[pltpu.VMEM(shape, dtype) for shape, dtype in scratch],
        compiler_params=pltpu.CompilerParams(vmem_limit_bytes=VMEM_LIMIT),
        cost_estimate=pl.CostEstimate(flops=1, bytes_accessed=1, transcendentals=0),
        name=name,
    )(*args)


def odd_device():
    return lax.rem(lax.axis_index("dom"), 2) == 1


def halves(pair, hdim):
    zero = jnp.zeros((hdim, pair.shape[1]), pair.dtype)
    return jnp.concatenate(
        [
            jnp.concatenate([pair[:hdim], zero], axis=0),
            jnp.concatenate([zero, pair[hdim:]], axis=0),
        ],
        axis=1,
    )


def normalize(rows):
    xf = rows.astype(F32)
    cent = xf - jnp.mean(xf, axis=-1, keepdims=True)
    rstd = lax.rsqrt(jnp.mean(cent * cent, axis=-1, keepdims=True) + EPS)
    return cent * rstd, rstd


def project_tile(t, tile, scale, rows, w_qkv, xn_t, inv, k_nat, v_nat, k_t, v_t):
    width = rows.shape[1]
    here = cols(t, tile=tile)
    xhat, rstd = normalize(rows)
    xn = xhat.astype(BF16)
    xn_t[:, here] = xhat.T.astype(BF16)
    inv[:, here] = jnp.broadcast_to(rstd, (tile, 128)).T[0:8, :]
    keyval = mm(xn, w_qkv[:, width:])
    k_t[:, here] = (keyval[:, :width].T * scale).astype(BF16)
    v_t[:, here] = keyval[:, width:].T.astype(BF16)
    k_nat[here, :] = keyval[:, :width].astype(BF16)
    v_nat[here, :] = keyval[:, width:].astype(BF16)
    return xn


def pick_kernel(tile, x, x_on, x_off):
    odd = odd_device()
    low, high = x[:tile, :].astype(F32), x[x.shape[0] - tile :, :].astype(F32)
    x_on[...] = jnp.where(odd, low, high).astype(BF16)
    x_off[...] = jnp.where(odd, high, low).astype(BF16)


def prelude_own_kernel(blk, tile, scale, x, w_qkv, xn_t, inv, k_nat, v_nat, k_t, v_t, q_t):
    width = x.shape[1]
    for b in range(blk):
        own = cols(b, tile=tile)
        xn = project_tile(
            b, tile, scale, x[own, :], w_qkv, xn_t, inv, k_nat, v_nat, k_t, v_t
        )
        q_t[:, own] = (mm(xn, w_qkv[:, :width]).T * scale).astype(BF16)


def prelude_kernel(
    blk, tile, scale, neighbours, x_on, x_off, w_qkv, xn_own, inv_own, k_own, v_own, kt_own, vt_own, q_t,
    top, xn_t, inv, v_nat, k_t, probs, attn_t, g_t, k_nat, v_t, scores,
):
    width = x_on.shape[1]
    hdim = width // HEADS
    ours = cols(1, blk, tile)
    xn_t[:, ours] = xn_own[...]
    inv[:, ours] = inv_own[...]
    k_nat[ours, :] = k_own[...]
    v_nat[ours, :] = v_own[...]
    k_t[:, ours] = kt_own[...]
    v_t[:, ours] = vt_own[...]
    is_last = lax.axis_index("section") == lax.axis_size("section") - 1
    for b in range(blk):
        own = cols(b, tile=tile)
        g_t[:, own] = jnp.where(is_last, top[own, :].astype(F32).T, 0.0).astype(BF16)
    odd = odd_device()
    x_lo = jnp.where(odd, x_on[...], x_off[...])
    x_hi = jnp.where(odd, x_off[...], x_on[...])
    for t, rows in ((0, x_lo), (blk + 1, x_hi)):
        project_tile(t, tile, scale, rows, w_qkv, xn_t, inv, k_nat, v_nat, k_t, v_t)
    blocks = blk * lax.axis_size("dom")
    for b in range(blk):
        mine = lax.axis_index("dom") * blk + b
        below, above = lax.rem(mine + blocks - 1, blocks), lax.rem(mine + 1, blocks)
        has_lo = has_hi = False
        for j in range(1, neighbours.shape[1]):
            has_lo |= neighbours[b, j] == below
            has_hi |= neighbours[b, j] == above
        for i in range(HEADS // 2):
            lanes = cols(i, tile=2 * hdim)
            q = halves(q_t[lanes, cols(b, tile=tile)], hdim)
            s = mm(k_nat[cols(b, 3, tile), lanes], q)
            scores[i, b] = jnp.concatenate(
                [
                    jnp.where(has_lo, s[:tile], -1e30),
                    s[tile : 2 * tile],
                    jnp.where(has_hi, s[2 * tile :], -1e30),
                ],
                axis=0,
            )
    for b in range(blk):
        for i in range(HEADS // 2):
            s = scores[i, b]
            e = jnp.exp(s - jnp.max(s, axis=0, keepdims=True))
            probs[i, b] = (e * (1.0 / jnp.sum(e, axis=0, keepdims=True))).astype(BF16)
    for b in range(blk):
        for h in range(HEADS):
            head = cols(h, tile=hdim)
            p = probs[h // 2, b, :, cols(h % 2, tile=tile)]
            attn_t[head, cols(b, tile=tile)] = mm(v_t[head, cols(b, 3, tile)], p).astype(BF16)


def arrive(blk, tile, g_prev, rest, one, g_t):
    odd = odd_device()
    for b in range(blk):
        own = cols(b, tile=tile)
        if b == 0:
            part = jnp.where(odd, rest[:, :tile], one[...])
        elif b == blk - 1:
            part = jnp.where(odd, one[...], rest[:, cols(b - 1, tile=tile)])
        else:
            part = jnp.where(odd, rest[:, own], rest[:, cols(b - 1, tile=tile)])
        g_t[:, own] = (g_prev[:, own].astype(F32) + part.astype(F32)).astype(BF16)


def score_grad(i, b, first, count, tile, hdim, v_nat, probs, attn_t, da_t):
    lanes, own = cols(i, tile=2 * hdim), cols(b, tile=tile)
    da = da_t[lanes, own]
    prod = da.astype(F32) * attn_t[lanes, own].astype(F32)
    total = jnp.concatenate(
        [
            jnp.sum(prod[:hdim], axis=0, keepdims=True),
            jnp.sum(prod[hdim:], axis=0, keepdims=True),
        ],
        axis=1,
    )
    dp = mm(v_nat[cols(b + first, count, tile), lanes], halves(da, hdim))
    return (probs[i, b, cols(first, count, tile), :].astype(F32) * (dp - total)).astype(BF16)


def score_grads(blk, tile, hdim, v_nat, probs, attn_t, da_t, ds):
    for b in range(blk):
        for i in range(HEADS // 2):
            ds[i, b] = score_grad(i, b, 0, 3, tile, hdim, v_nat, probs, attn_t, da_t)


def rim_terms(blk, tile, hdim, v_nat, probs, attn_t, q_t, da_t, d_kv):
    width = q_t.shape[0]
    sides = ((0, 0, 0), (1, blk - 1, 2))
    ds = {
        (side, i): score_grad(i, b, j, 1, tile, hdim, v_nat, probs, attn_t, da_t)
        for side, b, j in sides
        for i in range(HEADS // 2)
    }
    for side, b, j in sides:
        own, near, here = cols(b, tile=tile), cols(j, tile=tile), cols(side, tile=tile)
        for i in range(HEADS // 2):
            lanes = cols(i, tile=2 * hdim)
            after = slice(width + i * 2 * hdim, width + (i + 1) * 2 * hdim)
            d_kv[lanes, here] = mm(halves(q_t[lanes, own], hdim), ds[side, i], NT).astype(BF16)
            d_kv[after, here] = mm(
                halves(da_t[lanes, own], hdim), probs[i, b, near, :], NT
            ).astype(BF16)


def value_terms(blk, tile, hdim, first, last, da_t, probs, d_v):
    for i in range(HEADS // 2):
        lanes = cols(i, tile=2 * hdim)
        dv = [None] * (blk + 2)
        for b in range(blk):
            low, high = max(b, first), min(b + 3, last + 1)
            near = slice((low - b) * tile, (high - b) * tile)
            part = mm(halves(da_t[lanes, cols(b, tile=tile)], hdim), probs[i, b, near, :], NT)
            for t in range(low, high):
                more = part[:, cols(t - low, tile=tile)]
                dv[t] = more if dv[t] is None else dv[t] + more
        for t in range(first, last + 1):
            d_v[lanes, cols(t - first, tile=tile)] = dv[t].astype(BF16)


def query_key_terms(blk, tile, hdim, first, last, q_t, k_t, ds, d_qk):
    width = q_t.shape[0]
    for i in range(HEADS // 2):
        lanes = cols(i, tile=2 * hdim)
        dk = [None] * (blk + 2)
        for b in range(blk):
            low, high = max(b, first), min(b + 3, last + 1)
            near = slice((low - b) * tile, (high - b) * tile)
            part = mm(halves(q_t[lanes, cols(b, tile=tile)], hdim), ds[i, b, near, :], NT)
            for t in range(low, high):
                more = part[:, cols(t - low, tile=tile)]
                dk[t] = more if dk[t] is None else dk[t] + more
            for h in (2 * i, 2 * i + 1):
                head = cols(h, tile=hdim)
                d_qk[head, cols(b + 1 - first, tile=tile)] = mm(
                    k_t[head, cols(b, 3, tile)], ds[i, b, :, cols(h % 2, tile=tile)]
                ).astype(BF16)
        for t in range(first, last + 1):
            d_qk[width + i * 2 * hdim : width + (i + 1) * 2 * hdim, cols(t - first, tile=tile)] = dk[
                t
            ].astype(BF16)


def norm_grad(dn, xn, rstd):
    xhat = xn.astype(F32)
    first = jnp.mean(dn, axis=0, keepdims=True)
    second = jnp.mean(dn * xhat, axis=0, keepdims=True)
    return rstd * (dn - first - xhat * second)


def stage_rim_kernel(blk, tile, moved, *refs):
    if moved:
        g_prev, rest, one, *refs = refs
        *refs, g, da_t, c_on, c_off, d_rim = refs
        arrive(blk, tile, g_prev, rest, one, g)
    else:
        g, *refs = refs
        *refs, da_t, c_on, c_off, d_rim = refs
    w_qkv, w_out, xn_t, inv, v_nat, q_t, probs, attn_t = refs
    width = g.shape[0]
    hdim = width // HEADS
    da_t[...] = mm(w_out[...], g[...]).astype(BF16)
    rim_terms(blk, tile, hdim, v_nat, probs, attn_t, q_t, da_t, d_rim)
    dn = mm(w_qkv[:, width:], d_rim[...])
    c_lo, c_hi = (
        norm_grad(dn[:, cols(side, tile=tile)], xn_t[:, cols(t, tile=tile)], inv[0:1, cols(t, tile=tile)])
        for side, t in ((0, 0), (1, blk + 1))
    )
    odd = odd_device()
    c_on[...] = jnp.where(odd, c_lo, c_hi).astype(BF16)
    c_off[...] = jnp.where(odd, c_hi, c_lo).astype(BF16)


def stage_main_kernel(
    blk, tile, g_t, da_t, w_qkv, xn_t, inv, v_nat, k_t, q_t, probs, attn_t, rest, one, ds, d_qkv
):
    width = g_t.shape[0]
    hdim = width // HEADS
    score_grads(blk, tile, hdim, v_nat, probs, attn_t, da_t, ds)
    query_key_terms(blk, tile, hdim, 1, blk, q_t, k_t, ds, d_qkv)
    value_terms(blk, tile, hdim, 1, blk, da_t, probs, d_qkv.at[2 * width :])
    dn = mm(w_qkv[...], d_qkv[...])
    y = []
    for b in range(blk):
        own, here = cols(b, tile=tile), cols(b + 1, tile=tile)
        out = norm_grad(dn[:, own], xn_t[:, here], inv[0:1, here])
        y.append(g_t[:, own].astype(F32) + out)
    odd = odd_device()
    one[...] = jnp.where(odd, y[-1], y[0]).astype(BF16)
    for b in range(blk - 1):
        rest[:, cols(b, tile=tile)] = jnp.where(odd, y[b], y[b + 1]).astype(BF16)


def add_on_kernel(tile, rest, on, out):
    odd = odd_device()
    tiles = rest.shape[1] // tile
    out[...] = rest[...]
    for b, here in ((0, odd), (tiles - 1, jnp.logical_not(odd))):
        own = cols(b, tile=tile)
        more = jnp.where(here, on[...].astype(F32), 0.0)
        out[:, own] = (out[:, own].astype(F32) + more).astype(BF16)


def add_off_kernel(one, off, out):
    out[...] = (one[...].astype(F32) + off[...].astype(F32)).astype(BF16)


def last_terms_kernel(
    blk, tile, chips, g_prev, rest, one, w_out, v_nat, k_t, q_t, probs, attn_t, xn_t,
    g_t, d_qkv, *refs
):
    *give, da_t, ds = refs
    width = g_prev.shape[0]
    hdim = width // HEADS
    arrive(blk, tile, g_prev, rest, one, g_t)
    da_t[...] = mm(w_out[...], g_t[...]).astype(BF16)
    score_grads(blk, tile, hdim, v_nat, probs, attn_t, da_t, ds)
    value_terms(blk, tile, hdim, 0, blk + 1, da_t, probs, d_qkv.at[2 * width :])
    for t in (0, blk + 1):
        d_qkv[:width, cols(t, tile=tile)] = jnp.zeros((width, tile), BF16)
    query_key_terms(blk, tile, hdim, 0, blk + 1, q_t, k_t, ds, d_qkv)
    if give:
        give_rows(chips, [(xn_t, d_qkv), (attn_t, g_t)], *give)


def last_input_kernel(blk, tile, after, g_t, d_qkv, w_qkv, xn_t, inv, y, c_on, c_off):
    dn = mm(w_qkv[...], d_qkv[...])
    outs = [
        norm_grad(dn[:, cols(t, tile=tile)], xn_t[:, cols(t, tile=tile)], inv[0:1, cols(t, tile=tile)])
        for t in range(blk + 2)
    ]
    odd = odd_device()
    c_on[...] = jnp.where(odd, outs[0], outs[-1]).astype(BF16)
    c_off[...] = jnp.where(odd, outs[-1], outs[0]).astype(BF16)
    for b in range(blk):
        own = cols(b, tile=tile)
        y[:, own] = (g_t[:, own].astype(F32) + outs[b + 1]).astype(BF16)


def finish_input_kernel(blk, tile, y_t, on, off, out):
    odd = odd_device()
    from_prev, from_next = jnp.where(odd, on[...], off[...]), jnp.where(odd, off[...], on[...])
    for b in range(blk):
        own = cols(b, tile=tile)
        part = y_t[:, own].astype(F32)
        if b == 0:
            part = part + from_prev.astype(F32)
        if b == blk - 1:
            part = part + from_next.astype(F32)
        out[own, :] = part.T.astype(BF16)


def weight_rows(core, chips, terms):
    def picked(ref):
        rows = ref.shape[0] // (2 * chips)
        starts = [pl.multiple_of((2 * z + core) * rows, rows) for z in range(chips)]
        return jnp.concatenate([ref[pl.ds(s, rows), :] for s in starts], axis=0)

    return [mm(picked(left), right[...], NT) for left, right in terms]


def give_rows(chips, terms, out):
    core = 1 - lax.rem(lax.axis_index("dom"), 2)
    rows, start = out.shape[1], 0
    for part in weight_rows(core, chips, terms):
        across = slice(start, start + part.shape[1])
        for z in range(chips):
            out[z, :, across] = part[z * rows : (z + 1) * rows].astype(BF16)
        start += part.shape[1]


def keep_kernel(chips, steps, got, xn_t, d_qkv, attn_t, g_t, *refs):
    *outs, both = refs
    me = lax.axis_index("dom")
    chip = me // 2
    rows, start = got.shape[1], 0
    for part in weight_rows(lax.rem(me, 2), chips, [(xn_t, d_qkv), (attn_t, g_t)]):
        across = slice(start, start + part.shape[1])
        for z in range(chips):
            both[z, :, across] = part[z * rows : (z + 1) * rows] + got[z, :, across].astype(F32)
        start += part.shape[1]
    half = got.shape[2] // 2
    for n, (first, second) in enumerate(steps):
        give, own = outs[2 * n : 2 * n + 2]
        across = slice(n * half, (n + 1) * half)
        give[0] = both[lax.bitwise_xor(chip, first), :, across].astype(BF16)
        give[1] = both[lax.bitwise_xor(chip, first ^ second), :, across].astype(BF16)
        own[0] = both[chip, :, across]
        own[1] = both[lax.bitwise_xor(chip, second), :, across]


def middle_kernel(own_a, got_a, own_b, got_b, *refs):
    give_a, rest_a, give_b, rest_b = refs[-4:]
    for own, got, give, rest in ((own_b, got_b, give_b, rest_b), (own_a, got_a, give_a, rest_a)):
        rest[...] = own[0] + got[0].astype(F32)
        give[...] = (own[1] + got[1].astype(F32)).astype(BF16)


def total_kernel(rest_a, got_a, rest_b, got_b, qkv_grad, out_grad):
    width = out_grad.shape[1]
    qkv_grad[:, : 2 * width] = rest_a[...] + got_a[...].astype(F32)
    total = rest_b[...] + got_b[...].astype(F32)
    qkv_grad[:, 2 * width :] = total[:, :width]
    out_grad[...] = total[:, width:]


def ring(parts, distance):
    return [(i, (i + distance) % parts) for i in range(parts)]


def other_core(parts):
    return [(i, i ^ 1) for i in range(parts)]


def next_chip(parts):
    return [(i, (i + 1 if i % 2 else i - 1) % parts) for i in range(parts)]


def chips_apart(parts, step):
    return [(i, i ^ (2 * step)) for i in range(parts)]


def local(layer_inputs, top_grad, w_qkv, w_out, neighbours):
    sections = lax.axis_size("section")
    parts = lax.axis_size("dom")
    blk = neighbours.shape[0]
    rows, width = top_grad.shape[1:]
    tile = rows // blk
    ext = rows + 2 * tile
    hdim = width // HEADS
    scale = 1.0 / hdim**0.5
    x = layer_inputs[0, 0]
    w_in, w_back = w_qkv[0], w_out[0]
    x_on, x_off = call(
        functools.partial(pick_kernel, tile), "pick", [((tile, width), BF16)] * 2, [x]
    )
    x_on = lax.ppermute(x_on, "dom", other_core(parts))
    x_off = lax.ppermute(x_off, "dom", next_chip(parts))
    *kept, q_t = call(
        functools.partial(prelude_own_kernel, blk, tile, scale), "prelude_own",
        [
            ((width, rows), BF16), ((8, rows), F32), ((rows, width), BF16), ((rows, width), BF16),
            ((width, rows), BF16), ((width, rows), BF16), ((width, rows), BF16),
        ],
        [x, w_in],
    )
    pair_shape = (HEADS // 2, blk, 3 * tile, 2 * tile)
    xn_t, inv, v_nat, k_t, probs, attn_t, g_t = call(
        functools.partial(prelude_kernel, blk, tile, scale), "prelude",
        [
            ((width, ext), BF16), ((8, ext), F32), ((ext, width), BF16), ((width, ext), BF16),
            (pair_shape, BF16), ((width, rows), BF16), ((width, rows), BF16),
        ],
        [neighbours, x_on, x_off, w_in, *kept, q_t, top_grad[0]],
        scratch=[((ext, width), BF16), ((width, ext), BF16), (pair_shape, F32)], smem=1,
    )
    received = []
    for k in range(sections - 1):
        here = sections - 1 - k
        *new, da_t, c_on, c_off = call(
            functools.partial(stage_rim_kernel, blk, tile, k > 0), "stage_rim",
            [((width, rows), BF16)] * (1 + (k > 0)) + [((width, tile), BF16)] * 2,
            [g_t, *received, w_in, w_back, xn_t, inv, v_nat, q_t, probs, attn_t],
            scratch=[((2 * width, 2 * tile), BF16)],
        )
        if new:
            g_t = new[0]
        off = lax.ppermute(c_off, "dom", next_chip(parts))
        on = lax.ppermute(c_on, "dom", other_core(parts))
        rest, one = call(
            functools.partial(stage_main_kernel, blk, tile), "stage_main",
            [((width, rows - tile), BF16), ((width, tile), BF16)],
            [g_t, da_t, w_in, xn_t, inv, v_nat, k_t, q_t, probs, attn_t],
            scratch=[(pair_shape, BF16), ((3 * width, rows), BF16)],
        )
        rest = call(
            functools.partial(add_on_kernel, tile), "add_on", [((width, rows - tile), BF16)], [rest, on]
        )[0]
        one = call(add_off_kernel, "add_off", [((width, tile), BF16)], [one, off])[0]
        received = [lax.ppermute(part, "section", [(here, here - 1)]) for part in (rest, one)]
    direct = parts == 8
    chips = parts // 2
    every = 4 * width
    row = width // parts
    g_t, d_qkv, *give = call(
        functools.partial(last_terms_kernel, blk, tile, chips), "last_terms",
        [((width, rows), BF16), ((3 * width, ext), BF16)] + [((chips, row, every), BF16)] * direct,
        [g_t, *received, w_back, v_nat, k_t, q_t, probs, attn_t, xn_t],
        scratch=[((width, rows), BF16), (pair_shape, BF16)],
    )
    after = d_qkv
    if direct:
        got = lax.ppermute(give[0], "dom", other_core(parts))
        steps = ((1, 2), (2, 1))
        give_a, own_a, give_b, own_b = call(
            functools.partial(keep_kernel, chips, steps), "keep",
            [((2, row, every // 2), BF16), ((2, row, every // 2), F32)] * 2,
            [got, xn_t, d_qkv, attn_t, g_t], scratch=[((chips, row, every), F32)],
        )
        got_b = lax.ppermute(give_b, "dom", chips_apart(parts, steps[1][0]))
        got_a = lax.ppermute(give_a, "dom", chips_apart(parts, steps[0][0]))
        after = own_a
    y, c_on, c_off = call(
        functools.partial(last_input_kernel, blk, tile), "last_input",
        [((width, rows), BF16), ((width, tile), BF16), ((width, tile), BF16)],
        [after, g_t, d_qkv, w_in, xn_t, inv],
    )
    off = lax.ppermute(c_off, "dom", next_chip(parts))
    on = lax.ppermute(c_on, "dom", other_core(parts))
    if direct:
        give_a, rest_a, give_b, rest_b = call(
            middle_kernel, "middle", [((row, every // 2), BF16), ((row, every // 2), F32)] * 2,
            [own_a, got_a, own_b, got_b, on, off],
        )
        got_b = lax.ppermute(give_b, "dom", chips_apart(parts, steps[1][1]))
        got_a = lax.ppermute(give_a, "dom", chips_apart(parts, steps[0][1]))
    y = call(
        functools.partial(finish_input_kernel, blk, tile), "finish_input", [((rows, width), BF16)],
        [y, on, off],
    )[0]
    if direct:
        qkv_grad, out_grad = call(
            total_kernel, "total", [((row, 3 * width), F32), ((row, width), F32)],
            [rest_a, got_a, rest_b, got_b],
        )
    else:
        term = jnp.concatenate([mm(xn_t, d_qkv, NT), mm(attn_t, g_t, NT)], axis=1)
        total = lax.psum_scatter(term, "dom", scatter_dimension=0, tiled=True)
        qkv_grad, out_grad = total[:, : 3 * width], total[:, 3 * width :]
    return (y[None, None], qkv_grad[None], out_grad[None])


def solution(mesh):
    placed = (
        P("section", None, "dom", None),
        P(None, "dom", None),
        P("section", None, None),
        P("section", None, None),
        P("dom", None),
    )
    return jax.shard_map(
        local,
        mesh=mesh,
        in_specs=placed,
        out_specs=(
            P("section", None, "dom", None),
            P("section", "dom", None),
            P("section", "dom", None),
        ),
        check_vma=False,
    )
```

```python
import functools

import jax
import jax.numpy as jnp
from jax import lax
from jax.experimental import pallas as pl
from jax.experimental.pallas import tpu as pltpu
from jax.sharding import PartitionSpec as P

HEADS = 8
EPS = 1e-05
F32 = jnp.float32
BF16 = jnp.bfloat16
NN = (((1,), (0,)), ((), ()))
NT = (((1,), (1,)), ((), ()))
VMEM_LIMIT = 20 * 1024 * 1024


def mm(a, b, dims=NN):
    return lax.dot_general(a, b, dims, preferred_element_type=F32)


def cols(start, count=1, tile=128):
    return slice(start * tile, (start + count) * tile)


def call(kernel, name, outs, args, scratch=(), smem=0):
    vmem = pl.BlockSpec(memory_space=pltpu.VMEM)
    scalars = pl.BlockSpec(memory_space=pltpu.SMEM)
    return pl.pallas_call(
        kernel,
        in_specs=[scalars] * smem + [vmem] * (len(args) - smem),
        out_specs=[vmem] * len(outs),
        out_shape=[jax.ShapeDtypeStruct(shape, dtype) for shape, dtype in outs],
        scratch_shapes=[pltpu.VMEM(shape, dtype) for shape, dtype in scratch],
        compiler_params=pltpu.CompilerParams(vmem_limit_bytes=VMEM_LIMIT),
        cost_estimate=pl.CostEstimate(flops=1, bytes_accessed=1, transcendentals=0),
        name=name,
    )(*args)


def second_core():
    return lax.rem(lax.axis_index("dom"), 2) == 1


def block_of(b, blk):
    return jnp.where(second_core(), b, blk - 1 - b)


def rows_of(b, blk, tile):
    return pl.ds(pl.multiple_of(block_of(b, blk) * tile, tile), tile)


def halves(pair, hdim):
    zero = jnp.zeros((hdim, pair.shape[1]), pair.dtype)
    return jnp.concatenate(
        [
            jnp.concatenate([pair[:hdim], zero], axis=0),
            jnp.concatenate([zero, pair[hdim:]], axis=0),
        ],
        axis=1,
    )


def normalize(rows):
    xf = rows.astype(F32)
    cent = xf - jnp.mean(xf, axis=-1, keepdims=True)
    rstd = lax.rsqrt(jnp.mean(cent * cent, axis=-1, keepdims=True) + EPS)
    return cent * rstd, rstd


def project_tile(t, tile, scale, rows, w_qkv, xn_t, inv, k_nat, v_nat, k_t, v_t):
    width = rows.shape[1]
    here = cols(t, tile=tile)
    xhat, rstd = normalize(rows)
    xn = xhat.astype(BF16)
    xn_t[:, here] = xhat.T.astype(BF16)
    inv[:, here] = jnp.broadcast_to(rstd, (tile, 128)).T[0:8, :]
    keyval = mm(xn, w_qkv[:, width:])
    k_t[:, here] = (keyval[:, :width].T * scale).astype(BF16)
    v_t[:, here] = keyval[:, width:].T.astype(BF16)
    k_nat[here, :] = keyval[:, :width].astype(BF16)
    v_nat[here, :] = keyval[:, width:].astype(BF16)
    return xn


def pick_kernel(blk, tile, x, x_on, x_off):
    x_on[...] = x[rows_of(0, blk, tile), :]
    x_off[...] = x[rows_of(blk - 1, blk, tile), :]


def prelude_own_kernel(blk, tile, scale, x, w_qkv, xn_t, inv, k_nat, v_nat, k_t, v_t, q_t):
    width = x.shape[1]
    for b in range(blk):
        xn = project_tile(
            b, tile, scale, x[rows_of(b, blk, tile), :], w_qkv, xn_t, inv, k_nat, v_nat, k_t, v_t
        )
        q_t[:, cols(b, tile=tile)] = (mm(xn, w_qkv[:, :width]).T * scale).astype(BF16)


def prelude_kernel(
    blk, tile, scale, neighbours, x_on, x_off, w_qkv,
    xn_own, inv_own, k_own, v_own, kt_own, vt_own, q_t, top,
    xn_t, inv, v_nat, k_t, probs, attn_t, g_rest, g_one, k_nat, v_t, scores,
):
    width = x_on.shape[1]
    hdim = width // HEADS
    ours = cols(1, blk, tile)
    xn_t[:, ours] = xn_own[...]
    inv[:, ours] = inv_own[...]
    k_nat[ours, :] = k_own[...]
    v_nat[ours, :] = v_own[...]
    k_t[:, ours] = kt_own[...]
    v_t[:, ours] = vt_own[...]
    is_last = lax.axis_index("section") == lax.axis_size("section") - 1
    for b in range(blk):
        g = jnp.where(is_last, top[rows_of(b, blk, tile), :].astype(F32).T, 0.0).astype(BF16)
        if b < blk - 1:
            g_rest[:, cols(b, tile=tile)] = g
        else:
            g_one[...] = g
    for t, rows in ((0, x_on), (blk + 1, x_off)):
        project_tile(t, tile, scale, rows[...], w_qkv, xn_t, inv, k_nat, v_nat, k_t, v_t)
    blocks = blk * lax.axis_size("dom")
    second = second_core()
    for b in range(blk):
        place = block_of(b, blk)
        mine = lax.axis_index("dom") * blk + place
        below, above = lax.rem(mine + blocks - 1, blocks), lax.rem(mine + 1, blocks)
        before, after = jnp.where(second, below, above), jnp.where(second, above, below)
        has_before = has_after = False
        for j in range(1, neighbours.shape[1]):
            has_before |= neighbours[place, j] == before
            has_after |= neighbours[place, j] == after
        for i in range(HEADS // 2):
            lanes = cols(i, tile=2 * hdim)
            q = halves(q_t[lanes, cols(b, tile=tile)], hdim)
            s = mm(k_nat[cols(b, 3, tile), lanes], q)
            scores[i, b] = jnp.concatenate(
                [
                    jnp.where(has_before, s[:tile], -1e30),
                    s[tile : 2 * tile],
                    jnp.where(has_after, s[2 * tile :], -1e30),
                ],
                axis=0,
            )
    for b in range(blk):
        for i in range(HEADS // 2):
            s = scores[i, b]
            e = jnp.exp(s - jnp.max(s, axis=0, keepdims=True))
            probs[i, b] = (e * (1.0 / jnp.sum(e, axis=0, keepdims=True))).astype(BF16)
    for b in range(blk):
        for h in range(HEADS):
            head = cols(h, tile=hdim)
            p = probs[h // 2, b, :, cols(h % 2, tile=tile)]
            attn_t[head, cols(b, tile=tile)] = mm(v_t[head, cols(b, 3, tile)], p).astype(BF16)


def score_grad(i, b, first, count, tile, hdim, v_nat, probs, attn_t, da):
    lanes, own = cols(i, tile=2 * hdim), cols(b, tile=tile)
    prod = da.astype(F32) * attn_t[lanes, own].astype(F32)
    total = jnp.concatenate(
        [
            jnp.sum(prod[:hdim], axis=0, keepdims=True),
            jnp.sum(prod[hdim:], axis=0, keepdims=True),
        ],
        axis=1,
    )
    dp = mm(v_nat[cols(b + first, count, tile), lanes], halves(da, hdim))
    return (probs[i, b, cols(first, count, tile), :].astype(F32) * (dp - total)).astype(BF16)


def norm_grad(dn, xn, rstd):
    xhat = xn.astype(F32)
    first = jnp.mean(dn, axis=0, keepdims=True)
    second = jnp.mean(dn * xhat, axis=0, keepdims=True)
    return rstd * (dn - first - xhat * second)


def rim_grad(b, t, tile, hdim, q_t, probs, da, ds, w_qkv, xn_t, inv, d_rim):
    width = q_t.shape[0]
    own, near, here = cols(b, tile=tile), cols(t - b, tile=tile), cols(t, tile=tile)
    for i in range(HEADS // 2):
        lanes = cols(i, tile=2 * hdim)
        after = slice(width + i * 2 * hdim, width + (i + 1) * 2 * hdim)
        d_rim[lanes, :] = mm(halves(q_t[lanes, own], hdim), ds(i), NT).astype(BF16)
        d_rim[after, :] = mm(halves(da(lanes), hdim), probs[i, b, near, :], NT).astype(BF16)
    dn = mm(w_qkv[:, width:], d_rim[...])
    return norm_grad(dn, xn_t[:, here], inv[0:1, here]).astype(BF16)


def add(a, b):
    return (a[...].astype(F32) + b[...].astype(F32)).astype(BF16)


def stage_rest_kernel(blk, tile, moved, rim, *refs):
    if moved:
        g_prev, arrived, *refs = refs
    else:
        g, *refs = refs
    w_out, v_nat, probs, attn_t, *refs = refs
    if rim:
        w_qkv, xn_t, inv, q_t, *refs = refs
        *refs, d_rim = refs
        *refs, c_on = refs
    if moved:
        g, *refs = refs
        g[...] = add(g_prev, arrived)
    da, ds = refs
    hdim = g.shape[0] // HEADS
    da[...] = mm(w_out[...], g[...]).astype(BF16)
    for b in range(blk - 1):
        for i in range(HEADS // 2):
            part = da[cols(i, tile=2 * hdim), cols(b, tile=tile)]
            ds[i, b] = score_grad(i, b, 0, 3, tile, hdim, v_nat, probs, attn_t, part)
    if rim:
        c_on[...] = rim_grad(
            0, 0, tile, hdim, q_t, probs, lambda lanes: da[lanes, :tile],
            lambda i: ds[i, 0, :tile, :], w_qkv, xn_t, inv, d_rim,
        )


def stage_one_kernel(blk, tile, moved, *refs):
    if moved:
        g_prev, arrived, *refs = refs
    else:
        g, *refs = refs
    w_out, v_nat, probs, attn_t, w_qkv, xn_t, inv, q_t, *refs = refs
    if moved:
        g, *refs = refs
        g[...] = add(g_prev, arrived)
    da, c_off, d_rim = refs
    hdim = g.shape[0] // HEADS
    da[...] = mm(w_out[...], g[...]).astype(BF16)
    b = blk - 1
    ds = [
        score_grad(i, b, 2, 1, tile, hdim, v_nat, probs, attn_t, da[cols(i, tile=2 * hdim), :])
        for i in range(HEADS // 2)
    ]
    c_off[...] = rim_grad(
        b, blk + 1, tile, hdim, q_t, probs, lambda lanes: da[lanes, :], lambda i: ds[i],
        w_qkv, xn_t, inv, d_rim,
    )


def own_terms(blk, tile, hdim, first, last, q_t, k_t, probs, da, ds, d_qkv):
    width = q_t.shape[0]
    for i in range(HEADS // 2):
        lanes = cols(i, tile=2 * hdim)
        for n, left, right in (
            (1, lambda b: q_t[lanes, cols(b, tile=tile)], lambda b, near: ds(i, b, near, slice(None))),
            (2, lambda b: da(lanes, b), lambda b, near: probs[i, b, near, :]),
        ):
            total = [None] * (blk + 2)
            for b in range(blk):
                low, high = max(b, first), min(b + 3, last + 1)
                near = slice((low - b) * tile, (high - b) * tile)
                part = mm(halves(left(b), hdim), right(b, near), NT)
                for t in range(low, high):
                    more = part[:, cols(t - low, tile=tile)]
                    total[t] = more if total[t] is None else total[t] + more
            start = n * width + i * 2 * hdim
            for t in range(first, last + 1):
                d_qkv[start : start + 2 * hdim, cols(t - first, tile=tile)] = total[t].astype(BF16)
        for b in range(blk):
            for h in (2 * i, 2 * i + 1):
                head = cols(h, tile=hdim)
                d_qkv[head, cols(b + 1 - first, tile=tile)] = mm(
                    k_t[head, cols(b, 3, tile)],
                    ds(i, b, slice(None), cols(h % 2, tile=tile)),
                ).astype(BF16)


def joined(blk, tile, da_rest, da_one, ds_rest, ds_one):
    def da(lanes, b):
        return da_rest[lanes, cols(b, tile=tile)] if b < blk - 1 else da_one[lanes, :]

    def ds(i, b, near, across):
        return ds_rest[i, b, near, across] if b < blk - 1 else ds_one[i, near, across]

    return da, ds


def stage_main_kernel(
    blk, tile, g_rest, g_one, da_rest, da_one, ds_rest, w_qkv, xn_t, inv, v_nat, k_t, q_t, probs,
    attn_t, rest, one, ds_one, d_qkv,
):
    hdim = g_rest.shape[0] // HEADS
    for i in range(HEADS // 2):
        part = da_one[cols(i, tile=2 * hdim), :]
        ds_one[i] = score_grad(i, blk - 1, 0, 3, tile, hdim, v_nat, probs, attn_t, part)
    da, ds = joined(blk, tile, da_rest, da_one, ds_rest, ds_one)
    own_terms(blk, tile, hdim, 1, blk, q_t, k_t, probs, da, ds, d_qkv)
    dn = mm(w_qkv[...], d_qkv[...])
    for b in range(blk):
        own, here = cols(b, tile=tile), cols(b + 1, tile=tile)
        out = norm_grad(dn[:, own], xn_t[:, here], inv[0:1, here])
        if b < blk - 1:
            rest[:, own] = (g_rest[:, own].astype(F32) + out).astype(BF16)
        else:
            one[...] = (g_one[...].astype(F32) + out).astype(BF16)


def add_on_kernel(tile, rest, on, out):
    out[...] = rest[...]
    out[:, :tile] = (rest[:, :tile].astype(F32) + on[...].astype(F32)).astype(BF16)


def add_off_kernel(one, off, out):
    out[...] = add(one, off)


def last_terms_kernel(
    blk, tile, chips, g_prev, arrived, g_rest, da_rest, ds_rest, w_out, v_nat, k_t, q_t, probs, attn_t,
    xn_t, g_one, d_qkv, *refs
):
    *give, da_one, ds_one = refs
    width = g_prev.shape[0]
    hdim = width // HEADS
    g_one[...] = add(g_prev, arrived)
    da_one[...] = mm(w_out[...], g_one[...]).astype(BF16)
    for i in range(HEADS // 2):
        part = da_one[cols(i, tile=2 * hdim), :]
        ds_one[i] = score_grad(i, blk - 1, 0, 3, tile, hdim, v_nat, probs, attn_t, part)
    for t in (0, blk + 1):
        d_qkv[:width, cols(t, tile=tile)] = jnp.zeros((width, tile), BF16)
    da, ds = joined(blk, tile, da_rest, da_one, ds_rest, ds_one)
    own_terms(blk, tile, hdim, 0, blk + 1, q_t, k_t, probs, da, ds, d_qkv)
    if give:
        core = 1 - lax.rem(lax.axis_index("dom"), 2)
        part = weight_rows(core, chips, xn_t, d_qkv, attn_t, g_rest, g_one)
        rows = width // (2 * chips)
        for z in range(chips):
            here = slice(z * rows, (z + 1) * rows)
            for across, term in part:
                give[0][z, :, across] = term[here].astype(BF16)


def last_input_kernel(
    blk, tile, after, g_rest, g_one, d_qkv, w_qkv, xn_t, inv, y, c_on, c_off
):
    dn = mm(w_qkv[...], d_qkv[...])
    outs = [
        norm_grad(dn[:, cols(t, tile=tile)], xn_t[:, cols(t, tile=tile)], inv[0:1, cols(t, tile=tile)])
        for t in range(blk + 2)
    ]
    c_on[...] = outs[0].astype(BF16)
    c_off[...] = outs[-1].astype(BF16)
    for b in range(blk):
        own = cols(b, tile=tile)
        g = g_rest[:, own] if b < blk - 1 else g_one[...]
        y[:, own] = (g.astype(F32) + outs[b + 1]).astype(BF16)


def finish_input_kernel(blk, tile, y_t, on, off, out):
    for b in range(blk):
        part = y_t[:, cols(b, tile=tile)].astype(F32)
        if b == 0:
            part = part + on[...].astype(F32)
        if b == blk - 1:
            part = part + off[...].astype(F32)
        out[rows_of(b, blk, tile), :] = part.T.astype(BF16)


def weight_rows(core, chips, xn_t, d_qkv, attn_t, g_rest, g_one):
    def picked(ref):
        rows = ref.shape[0] // (2 * chips)
        starts = [pl.multiple_of((2 * z + core) * rows, rows) for z in range(chips)]
        return jnp.concatenate([ref[pl.ds(s, rows), :] for s in starts], axis=0)

    wide, split = d_qkv.shape[0], g_rest.shape[1]
    attn = picked(attn_t)
    out = mm(attn[:, :split], g_rest[...], NT) + mm(attn[:, split:], g_one[...], NT)
    return (
        (slice(0, wide), mm(picked(xn_t), d_qkv[...], NT)),
        (slice(wide, wide + out.shape[1]), out),
    )


def keep_kernel(chips, steps, got, xn_t, d_qkv, attn_t, g_rest, g_one, *refs):
    *outs, both = refs
    me = lax.axis_index("dom")
    chip = me // 2
    rows = got.shape[1]
    for across, term in weight_rows(lax.rem(me, 2), chips, xn_t, d_qkv, attn_t, g_rest, g_one):
        for z in range(chips):
            both[z, :, across] = term[z * rows : (z + 1) * rows] + got[z, :, across].astype(F32)
    half = got.shape[2] // 2
    for n, (first, second) in enumerate(steps):
        give, own = outs[2 * n : 2 * n + 2]
        across = slice(n * half, (n + 1) * half)
        give[0] = both[lax.bitwise_xor(chip, first), :, across].astype(BF16)
        give[1] = both[lax.bitwise_xor(chip, first ^ second), :, across].astype(BF16)
        own[0] = both[chip, :, across]
        own[1] = both[lax.bitwise_xor(chip, second), :, across]


def middle_kernel(own_a, got_a, own_b, got_b, *refs):
    give_a, rest_a, give_b, rest_b = refs[-4:]
    for own, got, give, rest in ((own_b, got_b, give_b, rest_b), (own_a, got_a, give_a, rest_a)):
        rest[...] = own[0] + got[0].astype(F32)
        give[...] = (own[1] + got[1].astype(F32)).astype(BF16)


def total_kernel(rest_a, got_a, rest_b, got_b, qkv_grad, out_grad):
    width = out_grad.shape[1]
    qkv_grad[:, : 2 * width] = rest_a[...] + got_a[...].astype(F32)
    total = rest_b[...] + got_b[...].astype(F32)
    qkv_grad[:, 2 * width :] = total[:, :width]
    out_grad[...] = total[:, width:]


def other_core(parts):
    return [(i, i ^ 1) for i in range(parts)]


def next_chip(parts):
    return [(i, (i + 1 if i % 2 else i - 1) % parts) for i in range(parts)]


def chips_apart(parts, step):
    return [(i, i ^ (2 * step)) for i in range(parts)]


def local(layer_inputs, top_grad, w_qkv, w_out, neighbours):
    sections = lax.axis_size("section")
    parts = lax.axis_size("dom")
    blk = neighbours.shape[0]
    rows, width = top_grad.shape[1:]
    tile = rows // blk
    ext = rows + 2 * tile
    hdim = width // HEADS
    scale = 1.0 / hdim**0.5
    x = layer_inputs[0, 0]
    w_in, w_back = w_qkv[0], w_out[0]
    whole, most, single = ((width, n) for n in (rows, rows - tile, tile))
    pairs = HEADS // 2
    pair_shape = (3 * tile, 2 * tile)
    x_on, x_off = call(
        functools.partial(pick_kernel, blk, tile), "pick", [((tile, width), BF16)] * 2, [x]
    )
    x_on = lax.ppermute(x_on, "dom", other_core(parts))
    x_off = lax.ppermute(x_off, "dom", next_chip(parts))
    *kept, q_t = call(
        functools.partial(prelude_own_kernel, blk, tile, scale), "prelude_own",
        [
            (whole, BF16), ((8, rows), F32), ((rows, width), BF16), ((rows, width), BF16),
            (whole, BF16), (whole, BF16), (whole, BF16),
        ],
        [x, w_in],
    )
    xn_t, inv, v_nat, k_t, probs, attn_t, g_rest, g_one = call(
        functools.partial(prelude_kernel, blk, tile, scale), "prelude",
        [
            ((width, ext), BF16), ((8, ext), F32), ((ext, width), BF16), ((width, ext), BF16),
            ((pairs, blk, *pair_shape), BF16), (whole, BF16), (most, BF16), (single, BF16),
        ],
        [neighbours, x_on, x_off, w_in, *kept, q_t, top_grad[0]],
        scratch=[
            ((ext, width), BF16), ((width, ext), BF16), ((pairs, blk, *pair_shape), F32),
        ],
        smem=1,
    )
    common = [w_back, v_nat, probs, attn_t]
    for_rim = [w_in, xn_t, inv, q_t]
    rim_scratch = [((2 * width, tile), BF16)]
    rest_shape = [(most, BF16), ((pairs, blk - 1, *pair_shape), BF16)]
    rest = one = None
    for k in range(sections - 1):
        here = sections - 1 - k
        moved = k > 0
        *new, da_rest, ds_rest, c_on = call(
            functools.partial(stage_rest_kernel, blk, tile, moved, True), "stage_rest",
            [(most, BF16)] * moved + rest_shape + [(single, BF16)],
            [g_rest, *[rest] * moved, *common, *for_rim], scratch=rim_scratch,
        )
        g_rest = new[0] if moved else g_rest
        on = lax.ppermute(c_on, "dom", other_core(parts))
        *new, da_one, c_off = call(
            functools.partial(stage_one_kernel, blk, tile, moved), "stage_one",
            [(single, BF16)] * (moved + 2),
            [g_one, *[one] * moved, *common, *for_rim], scratch=rim_scratch,
        )
        g_one = new[0] if moved else g_one
        off = lax.ppermute(c_off, "dom", next_chip(parts))
        rest, one = call(
            functools.partial(stage_main_kernel, blk, tile), "stage_main",
            [(most, BF16), (single, BF16)],
            [
                g_rest, g_one, da_rest, da_one, ds_rest, w_in, xn_t, inv, v_nat, k_t, q_t, probs, attn_t
            ],
            scratch=[((pairs, *pair_shape), BF16), ((3 * width, rows), BF16)],
        )
        rest = call(functools.partial(add_on_kernel, tile), "add_on", [(most, BF16)], [rest, on])[0]
        one = call(add_off_kernel, "add_off", [(single, BF16)], [one, off])[0]
        rest, one = (lax.ppermute(part, "section", [(here, here - 1)]) for part in (rest, one))
    direct = parts == 8
    chips = parts // 2
    every = 4 * width
    row = width // parts
    g_rest, da_rest, ds_rest = call(
        functools.partial(stage_rest_kernel, blk, tile, True, False), "last_rest",
        [(most, BF16)] + rest_shape, [g_rest, rest, *common],
    )
    g_one, d_qkv, *give = call(
        functools.partial(last_terms_kernel, blk, tile, chips), "last_terms",
        [(single, BF16), ((3 * width, ext), BF16)] + [((chips, row, every), BF16)] * direct,
        [g_one, one, g_rest, da_rest, ds_rest, w_back, v_nat, k_t, q_t, probs, attn_t, xn_t],
        scratch=[(single, BF16), ((pairs, *pair_shape), BF16)],
    )
    after = d_qkv
    if direct:
        got = lax.ppermute(give[0], "dom", other_core(parts))
        steps = ((1, 2), (2, 1))
        give_a, own_a, give_b, own_b = call(
            functools.partial(keep_kernel, chips, steps), "keep",
            [((2, row, every // 2), BF16), ((2, row, every // 2), F32)] * 2,
            [got, xn_t, d_qkv, attn_t, g_rest, g_one], scratch=[((chips, row, every), F32)],
        )
        got_b = lax.ppermute(give_b, "dom", chips_apart(parts, steps[1][0]))
        got_a = lax.ppermute(give_a, "dom", chips_apart(parts, steps[0][0]))
        after = own_a
    y, c_on, c_off = call(
        functools.partial(last_input_kernel, blk, tile), "last_input",
        [(whole, BF16), (single, BF16), (single, BF16)],
        [after, g_rest, g_one, d_qkv, w_in, xn_t, inv],
    )
    off = lax.ppermute(c_off, "dom", next_chip(parts))
    on = lax.ppermute(c_on, "dom", other_core(parts))
    if direct:
        give_a, rest_a, give_b, rest_b = call(
            middle_kernel, "middle", [((row, every // 2), BF16), ((row, every // 2), F32)] * 2,
            [own_a, got_a, own_b, got_b, on],
        )
        got_b = lax.ppermute(give_b, "dom", chips_apart(parts, steps[1][1]))
        got_a = lax.ppermute(give_a, "dom", chips_apart(parts, steps[0][1]))
    y = call(
        functools.partial(finish_input_kernel, blk, tile), "finish_input", [((rows, width), BF16)],
        [y, on, off],
    )[0]
    if direct:
        qkv_grad, out_grad = call(
            total_kernel, "total", [((row, 3 * width), F32), ((row, width), F32)],
            [rest_a, got_a, rest_b, got_b],
        )
    else:
        g_t = jnp.concatenate([g_rest, g_one], axis=1)
        term = jnp.concatenate([mm(xn_t, d_qkv, NT), mm(attn_t, g_t, NT)], axis=1)
        total = lax.psum_scatter(term, "dom", scatter_dimension=0, tiled=True)
        qkv_grad, out_grad = total[:, : 3 * width], total[:, 3 * width :]
    return (y[None, None], qkv_grad[None], out_grad[None])


def solution(mesh):
    placed = (
        P("section", None, "dom", None),
        P(None, "dom", None),
        P("section", None, None),
        P("section", None, None),
        P("dom", None),
    )
    return jax.shard_map(
        local,
        mesh=mesh,
        in_specs=placed,
        out_specs=(
            P("section", None, "dom", None),
            P("section", "dom", None),
            P("section", "dom", None),
        ),
        check_vma=False,
    )
```

```python
import functools

import jax
import jax.numpy as jnp
from jax import lax
from jax.experimental import pallas as pl
from jax.experimental.pallas import tpu as pltpu
from jax.sharding import PartitionSpec as P

HEADS = 8
EPS = 1e-05
F32 = jnp.float32
BF16 = jnp.bfloat16
NN = (((1,), (0,)), ((), ()))
NT = (((1,), (1,)), ((), ()))
VMEM_LIMIT = 20 * 1024 * 1024


def mm(a, b, dims=NN):
    return lax.dot_general(a, b, dims, preferred_element_type=F32)


def cols(start, count=1, tile=128):
    return slice(start * tile, (start + count) * tile)


def call(kernel, name, outs, args, scratch=(), smem=0):
    vmem = pl.BlockSpec(memory_space=pltpu.VMEM)
    scalars = pl.BlockSpec(memory_space=pltpu.SMEM)
    return pl.pallas_call(
        kernel,
        in_specs=[scalars] * smem + [vmem] * (len(args) - smem),
        out_specs=[vmem] * len(outs),
        out_shape=[jax.ShapeDtypeStruct(shape, dtype) for shape, dtype in outs],
        scratch_shapes=[pltpu.VMEM(shape, dtype) for shape, dtype in scratch],
        compiler_params=pltpu.CompilerParams(vmem_limit_bytes=VMEM_LIMIT),
        cost_estimate=pl.CostEstimate(flops=1, bytes_accessed=1, transcendentals=0),
        name=name,
    )(*args)


def second_core():
    return lax.rem(lax.axis_index("dom"), 2) == 1


def block_of(b, blk):
    return jnp.where(second_core(), b, blk - 1 - b)


def rows_of(b, blk, tile):
    return pl.ds(pl.multiple_of(block_of(b, blk) * tile, tile), tile)


def halves(pair, hdim):
    zero = jnp.zeros((hdim, pair.shape[1]), pair.dtype)
    return jnp.concatenate(
        [
            jnp.concatenate([pair[:hdim], zero], axis=0),
            jnp.concatenate([zero, pair[hdim:]], axis=0),
        ],
        axis=1,
    )


def normalize(rows):
    xf = rows.astype(F32)
    cent = xf - jnp.mean(xf, axis=-1, keepdims=True)
    rstd = lax.rsqrt(jnp.mean(cent * cent, axis=-1, keepdims=True) + EPS)
    return cent * rstd, rstd


def project_tile(t, tile, scale, rows, w_qkv, xn_t, inv, k_nat, v_nat, k_t, v_t):
    width = rows.shape[1]
    here = cols(t, tile=tile)
    xhat, rstd = normalize(rows)
    xn = xhat.astype(BF16)
    xn_t[:, here] = xhat.T.astype(BF16)
    inv[:, here] = jnp.broadcast_to(rstd, (tile, 128)).T[0:8, :]
    keyval = mm(xn, w_qkv[:, width:])
    k_t[:, here] = (keyval[:, :width].T * scale).astype(BF16)
    v_t[:, here] = keyval[:, width:].T.astype(BF16)
    k_nat[here, :] = keyval[:, :width].astype(BF16)
    v_nat[here, :] = keyval[:, width:].astype(BF16)
    return xn


def pick_kernel(blk, tile, x, x_on, x_off):
    x_on[...] = x[rows_of(0, blk, tile), :]
    x_off[...] = x[rows_of(blk - 1, blk, tile), :]


def prelude_own_kernel(blk, tile, scale, x, w_qkv, xn_t, inv, k_nat, v_nat, k_t, v_t, q_t):
    width = x.shape[1]
    for b in range(blk):
        xn = project_tile(
            b, tile, scale, x[rows_of(b, blk, tile), :], w_qkv, xn_t, inv, k_nat, v_nat, k_t, v_t
        )
        q_t[:, cols(b, tile=tile)] = (mm(xn, w_qkv[:, :width]).T * scale).astype(BF16)


def prelude_kernel(
    blk, tile, scale, neighbours, x_on, x_off, w_qkv,
    xn_own, inv_own, k_own, v_own, kt_own, vt_own, q_t, top,
    xn_t, inv, v_nat, k_t, probs, attn_t, g_zero, g_mid, g_one, k_nat, v_t, scores,
):
    width = x_on.shape[1]
    hdim = width // HEADS
    ours = cols(1, blk, tile)
    xn_t[:, ours] = xn_own[...]
    inv[:, ours] = inv_own[...]
    k_nat[ours, :] = k_own[...]
    v_nat[ours, :] = v_own[...]
    k_t[:, ours] = kt_own[...]
    v_t[:, ours] = vt_own[...]
    is_last = lax.axis_index("section") == lax.axis_size("section") - 1
    for b in range(blk):
        g = jnp.where(is_last, top[rows_of(b, blk, tile), :].astype(F32).T, 0.0).astype(BF16)
        if b == 0:
            g_zero[...] = g
        elif b < blk - 1:
            g_mid[:, cols(b - 1, tile=tile)] = g
        else:
            g_one[...] = g
    for t, rows in ((0, x_on), (blk + 1, x_off)):
        project_tile(t, tile, scale, rows[...], w_qkv, xn_t, inv, k_nat, v_nat, k_t, v_t)
    blocks = blk * lax.axis_size("dom")
    second = second_core()
    for b in range(blk):
        place = block_of(b, blk)
        mine = lax.axis_index("dom") * blk + place
        below, above = lax.rem(mine + blocks - 1, blocks), lax.rem(mine + 1, blocks)
        before, after = jnp.where(second, below, above), jnp.where(second, above, below)
        has_before = has_after = False
        for j in range(1, neighbours.shape[1]):
            has_before |= neighbours[place, j] == before
            has_after |= neighbours[place, j] == after
        for i in range(HEADS // 2):
            lanes = cols(i, tile=2 * hdim)
            q = halves(q_t[lanes, cols(b, tile=tile)], hdim)
            s = mm(k_nat[cols(b, 3, tile), lanes], q)
            scores[i, b] = jnp.concatenate(
                [
                    jnp.where(has_before, s[:tile], -1e30),
                    s[tile : 2 * tile],
                    jnp.where(has_after, s[2 * tile :], -1e30),
                ],
                axis=0,
            )
    for b in range(blk):
        for i in range(HEADS // 2):
            s = scores[i, b]
            e = jnp.exp(s - jnp.max(s, axis=0, keepdims=True))
            probs[i, b] = (e * (1.0 / jnp.sum(e, axis=0, keepdims=True))).astype(BF16)
    for b in range(blk):
        for h in range(HEADS):
            head = cols(h, tile=hdim)
            p = probs[h // 2, b, :, cols(h % 2, tile=tile)]
            attn_t[head, cols(b, tile=tile)] = mm(v_t[head, cols(b, 3, tile)], p).astype(BF16)


def score_grad(i, b, first, count, tile, hdim, v_nat, probs, attn_t, da):
    lanes, own = cols(i, tile=2 * hdim), cols(b, tile=tile)
    prod = da.astype(F32) * attn_t[lanes, own].astype(F32)
    total = jnp.concatenate(
        [
            jnp.sum(prod[:hdim], axis=0, keepdims=True),
            jnp.sum(prod[hdim:], axis=0, keepdims=True),
        ],
        axis=1,
    )
    dp = mm(v_nat[cols(b + first, count, tile), lanes], halves(da, hdim))
    return (probs[i, b, cols(first, count, tile), :].astype(F32) * (dp - total)).astype(BF16)


def norm_grad(dn, xn, rstd):
    xhat = xn.astype(F32)
    first = jnp.mean(dn, axis=0, keepdims=True)
    second = jnp.mean(dn * xhat, axis=0, keepdims=True)
    return rstd * (dn - first - xhat * second)


def rim_grad(b, t, tile, hdim, q_t, probs, da, ds, w_qkv, xn_t, inv, d_rim):
    width = q_t.shape[0]
    own, near, here = cols(b, tile=tile), cols(t - b, tile=tile), cols(t, tile=tile)
    for i in range(HEADS // 2):
        lanes = cols(i, tile=2 * hdim)
        after = slice(width + i * 2 * hdim, width + (i + 1) * 2 * hdim)
        d_rim[lanes, :] = mm(halves(q_t[lanes, own], hdim), ds(i), NT).astype(BF16)
        d_rim[after, :] = mm(halves(da(lanes), hdim), probs[i, b, near, :], NT).astype(BF16)
    dn = mm(w_qkv[:, width:], d_rim[...])
    return norm_grad(dn, xn_t[:, here], inv[0:1, here]).astype(BF16)


def add(a, b):
    return (a[...].astype(F32) + b[...].astype(F32)).astype(BF16)


def joined(blk, tile, das, dss):
    def da(lanes, b):
        if b == 0:
            return das[0][lanes, :]
        return das[1][lanes, cols(b - 1, tile=tile)] if b < blk - 1 else das[2][lanes, :]

    def ds(i, b, near, across):
        if b == 0:
            return dss[0][i, near, across]
        return dss[1][i, b - 1, near, across] if b < blk - 1 else dss[2][i, near, across]

    return da, ds


def end_grads(b, tile, hdim, g, w_out, v_nat, probs, attn_t, da, ds):
    da[...] = mm(w_out[...], g[...]).astype(BF16)
    for i in range(HEADS // 2):
        part = da[cols(i, tile=2 * hdim), :]
        ds[i] = score_grad(i, b, 0, 3, tile, hdim, v_nat, probs, attn_t, part)


def mid_grads(blk, tile, hdim, g, w_out, v_nat, probs, attn_t, da, ds):
    da[...] = mm(w_out[...], g[...]).astype(BF16)
    for b in range(1, blk - 1):
        for i in range(HEADS // 2):
            part = da[cols(i, tile=2 * hdim), cols(b - 1, tile=tile)]
            ds[i, b - 1] = score_grad(i, b, 0, 3, tile, hdim, v_nat, probs, attn_t, part)


def own_terms(blk, tile, hdim, first, last, q_t, k_t, probs, da, ds, d_qkv):
    width = q_t.shape[0]
    for i in range(HEADS // 2):
        lanes = cols(i, tile=2 * hdim)
        for n, left, right in (
            (1, lambda b: q_t[lanes, cols(b, tile=tile)], lambda b, near: ds(i, b, near, slice(None))),
            (2, lambda b: da(lanes, b), lambda b, near: probs[i, b, near, :]),
        ):
            total = [None] * (blk + 2)
            for b in range(max(first - 2, 0), min(last + 1, blk)):
                low, high = max(b, first), min(b + 3, last + 1)
                near = slice((low - b) * tile, (high - b) * tile)
                part = mm(halves(left(b), hdim), right(b, near), NT)
                for t in range(low, high):
                    more = part[:, cols(t - low, tile=tile)]
                    total[t] = more if total[t] is None else total[t] + more
            start = n * width + i * 2 * hdim
            for t in range(first, last + 1):
                d_qkv[start : start + 2 * hdim, cols(t - first, tile=tile)] = total[t].astype(BF16)
        for b in range(max(first - 1, 0), min(last, blk)):
            for h in (2 * i, 2 * i + 1):
                head = cols(h, tile=hdim)
                d_qkv[head, cols(b + 1 - first, tile=tile)] = mm(
                    k_t[head, cols(b, 3, tile)],
                    ds(i, b, slice(None), cols(h % 2, tile=tile)),
                ).astype(BF16)


def stage_zero_kernel(blk, tile, moved, *refs):
    if moved:
        g_prev, arrived, *refs = refs
    else:
        g, *refs = refs
    w_out, v_nat, probs, attn_t, w_qkv, xn_t, inv, q_t, *refs = refs
    if moved:
        g, *refs = refs
        g[...] = add(g_prev, arrived)
    da, ds, c_on, d_rim = refs
    hdim = g.shape[0] // HEADS
    end_grads(0, tile, hdim, g, w_out, v_nat, probs, attn_t, da, ds)
    c_on[...] = rim_grad(
        0, 0, tile, hdim, q_t, probs, lambda lanes: da[lanes, :], lambda i: ds[i, :tile, :],
        w_qkv, xn_t, inv, d_rim,
    )


def stage_mid_kernel(blk, tile, moved, *refs):
    if moved:
        g_prev, arrived, *refs = refs
    else:
        g, *refs = refs
    g_zero, da_zero, ds_zero, w_out, v_nat, probs, attn_t, w_qkv, xn_t, inv, q_t, k_t, *refs = refs
    if moved:
        g, *refs = refs
        g[...] = add(g_prev, arrived)
    da, ds, y, d_first = refs
    hdim = g.shape[0] // HEADS
    mid_grads(blk, tile, hdim, g, w_out, v_nat, probs, attn_t, da, ds)
    by_block = joined(blk, tile, (da_zero, da), (ds_zero, ds))
    own_terms(blk, tile, hdim, 1, 1, q_t, k_t, probs, *by_block, d_first)
    dn = mm(w_qkv[...], d_first[...])
    here = cols(1, tile=tile)
    y[...] = (g_zero[...].astype(F32) + norm_grad(dn, xn_t[:, here], inv[0:1, here])).astype(BF16)


def last_mid_kernel(
    blk, tile, g_prev, arrived, da_zero, ds_zero, w_out, v_nat, probs, attn_t, q_t, k_t, g, da, ds, d_low
):
    g[...] = add(g_prev, arrived)
    width = g.shape[0]
    hdim = width // HEADS
    mid_grads(blk, tile, hdim, g, w_out, v_nat, probs, attn_t, da, ds)
    d_low[:width, :tile] = jnp.zeros((width, tile), BF16)
    by_block = joined(blk, tile, (da_zero, da), (ds_zero, ds))
    own_terms(blk, tile, hdim, 0, 1, q_t, k_t, probs, *by_block, d_low)


def stage_one_kernel(blk, tile, moved, *refs):
    if moved:
        g_prev, arrived, *refs = refs
    else:
        g, *refs = refs
    w_out, v_nat, probs, attn_t, w_qkv, xn_t, inv, q_t, *refs = refs
    if moved:
        g, *refs = refs
        g[...] = add(g_prev, arrived)
    da, c_off, d_rim = refs
    hdim = g.shape[0] // HEADS
    da[...] = mm(w_out[...], g[...]).astype(BF16)
    b = blk - 1
    ds = [
        score_grad(i, b, 2, 1, tile, hdim, v_nat, probs, attn_t, da[cols(i, tile=2 * hdim), :])
        for i in range(HEADS // 2)
    ]
    c_off[...] = rim_grad(
        b, blk + 1, tile, hdim, q_t, probs, lambda lanes: da[lanes, :], lambda i: ds[i],
        w_qkv, xn_t, inv, d_rim,
    )


def stage_main_kernel(
    blk, tile, g_mid, g_one, da_zero, da_mid, da_one, ds_zero, ds_mid, w_qkv, xn_t, inv, v_nat, k_t, q_t,
    probs, attn_t, mid, one, ds_one, d_qkv,
):
    hdim = g_mid.shape[0] // HEADS
    for i in range(HEADS // 2):
        part = da_one[cols(i, tile=2 * hdim), :]
        ds_one[i] = score_grad(i, blk - 1, 0, 3, tile, hdim, v_nat, probs, attn_t, part)
    by_block = joined(blk, tile, (da_zero, da_mid, da_one), (ds_zero, ds_mid, ds_one))
    own_terms(blk, tile, hdim, 2, blk, q_t, k_t, probs, *by_block, d_qkv)
    dn = mm(w_qkv[...], d_qkv[...])
    for b in range(1, blk):
        here, place = cols(b + 1, tile=tile), cols(b - 1, tile=tile)
        out = norm_grad(dn[:, place], xn_t[:, here], inv[0:1, here])
        if b < blk - 1:
            mid[:, place] = (g_mid[:, place].astype(F32) + out).astype(BF16)
        else:
            one[...] = (g_one[...].astype(F32) + out).astype(BF16)


def add_rim_kernel(one, rim, out):
    out[...] = add(one, rim)


def last_terms_kernel(
    blk, tile, chips, g_prev, arrived, g_zero, g_mid, da_zero, da_mid, ds_zero, ds_mid, w_out, v_nat, k_t,
    q_t, probs, attn_t, xn_t, d_low, g_one, d_high, *refs
):
    *give, da_one, ds_one = refs
    width = g_prev.shape[0]
    hdim = width // HEADS
    g_one[...] = add(g_prev, arrived)
    end_grads(blk - 1, tile, hdim, g_one, w_out, v_nat, probs, attn_t, da_one, ds_one)
    d_high[:width, cols(blk - 1, tile=tile)] = jnp.zeros((width, tile), BF16)
    by_block = joined(blk, tile, (da_zero, da_mid, da_one), (ds_zero, ds_mid, ds_one))
    own_terms(blk, tile, hdim, 2, blk + 1, q_t, k_t, probs, *by_block, d_high)
    if give:
        core = 1 - lax.rem(lax.axis_index("dom"), 2)
        part = weight_rows(core, chips, xn_t, (d_low, d_high), attn_t, (g_zero, g_mid, g_one))
        rows = width // (2 * chips)
        for z in range(chips):
            here = slice(z * rows, (z + 1) * rows)
            for across, term in part:
                give[0][z, :, across] = term[here].astype(BF16)


def last_input_kernel(
    blk, tile, after, g_zero, g_mid, g_one, d_low, d_high, w_qkv, xn_t, inv, y, c_on, c_off
):
    outs = []
    for part in (d_low, d_high):
        dn = mm(w_qkv[...], part[...])
        for n in range(part.shape[1] // tile):
            here = cols(len(outs), tile=tile)
            outs.append(norm_grad(dn[:, cols(n, tile=tile)], xn_t[:, here], inv[0:1, here]))
    c_on[...] = outs[0].astype(BF16)
    c_off[...] = outs[-1].astype(BF16)
    for b in range(blk):
        own = cols(b, tile=tile)
        g = g_zero[...] if b == 0 else g_mid[:, cols(b - 1, tile=tile)] if b < blk - 1 else g_one[...]
        y[:, own] = (g.astype(F32) + outs[b + 1]).astype(BF16)


def finish_input_kernel(blk, tile, y_t, on, off, out):
    for b in range(blk):
        part = y_t[:, cols(b, tile=tile)].astype(F32)
        if b == 0:
            part = part + on[...].astype(F32)
        if b == blk - 1:
            part = part + off[...].astype(F32)
        out[rows_of(b, blk, tile), :] = part.T.astype(BF16)


def weight_rows(core, chips, xn_t, d_qkv, attn_t, g):
    def picked(ref):
        rows = ref.shape[0] // (2 * chips)
        starts = [pl.multiple_of((2 * z + core) * rows, rows) for z in range(chips)]
        return jnp.concatenate([ref[pl.ds(s, rows), :] for s in starts], axis=0)

    def product(ref, parts):
        left, start, total = picked(ref), 0, None
        for part in parts:
            more = mm(left[:, start : start + part.shape[1]], part[...], NT)
            total = more if total is None else total + more
            start += part.shape[1]
        return total

    wide, width = d_qkv[0].shape[0], g[0].shape[0]
    return (
        (slice(0, wide), product(xn_t, d_qkv)),
        (slice(wide, wide + width), product(attn_t, g)),
    )


def keep_kernel(chips, steps, got, xn_t, d_low, d_high, attn_t, g_zero, g_mid, g_one, *refs):
    *outs, both = refs
    me = lax.axis_index("dom")
    chip = me // 2
    rows = got.shape[1]
    terms = weight_rows(
        lax.rem(me, 2), chips, xn_t, (d_low, d_high), attn_t, (g_zero, g_mid, g_one)
    )
    for across, term in terms:
        for z in range(chips):
            both[z, :, across] = term[z * rows : (z + 1) * rows] + got[z, :, across].astype(F32)
    half = got.shape[2] // 2
    for n, (first, second) in enumerate(steps):
        give, own = outs[2 * n : 2 * n + 2]
        across = slice(n * half, (n + 1) * half)
        give[0] = both[lax.bitwise_xor(chip, first), :, across].astype(BF16)
        give[1] = both[lax.bitwise_xor(chip, first ^ second), :, across].astype(BF16)
        own[0] = both[chip, :, across]
        own[1] = both[lax.bitwise_xor(chip, second), :, across]


def middle_kernel(own_a, got_a, own_b, got_b, *refs):
    give_a, rest_a, give_b, rest_b = refs[-4:]
    for own, got, give, rest in ((own_b, got_b, give_b, rest_b), (own_a, got_a, give_a, rest_a)):
        rest[...] = own[0] + got[0].astype(F32)
        give[...] = (own[1] + got[1].astype(F32)).astype(BF16)


def total_kernel(rest_a, got_a, rest_b, got_b, qkv_grad, out_grad):
    width = out_grad.shape[1]
    qkv_grad[:, : 2 * width] = rest_a[...] + got_a[...].astype(F32)
    total = rest_b[...] + got_b[...].astype(F32)
    qkv_grad[:, 2 * width :] = total[:, :width]
    out_grad[...] = total[:, width:]


def other_core(parts):
    return [(i, i ^ 1) for i in range(parts)]


def next_chip(parts):
    return [(i, (i + 1 if i % 2 else i - 1) % parts) for i in range(parts)]


def chips_apart(parts, step):
    return [(i, i ^ (2 * step)) for i in range(parts)]


def local(layer_inputs, top_grad, w_qkv, w_out, neighbours):
    sections = lax.axis_size("section")
    parts = lax.axis_size("dom")
    blk = neighbours.shape[0]
    rows, width = top_grad.shape[1:]
    tile = rows // blk
    ext = rows + 2 * tile
    hdim = width // HEADS
    scale = 1.0 / hdim**0.5
    x = layer_inputs[0, 0]
    w_in, w_back = w_qkv[0], w_out[0]
    whole, middle, single = ((width, n) for n in (rows, rows - 2 * tile, tile))
    pairs = HEADS // 2
    pair_shape = (3 * tile, 2 * tile)
    x_on, x_off = call(
        functools.partial(pick_kernel, blk, tile), "pick", [((tile, width), BF16)] * 2, [x]
    )
    x_on = lax.ppermute(x_on, "dom", other_core(parts))
    x_off = lax.ppermute(x_off, "dom", next_chip(parts))
    *kept, q_t = call(
        functools.partial(prelude_own_kernel, blk, tile, scale), "prelude_own",
        [
            (whole, BF16), ((8, rows), F32), ((rows, width), BF16), ((rows, width), BF16),
            (whole, BF16), (whole, BF16), (whole, BF16),
        ],
        [x, w_in],
    )
    xn_t, inv, v_nat, k_t, probs, attn_t, g_zero, g_mid, g_one = call(
        functools.partial(prelude_kernel, blk, tile, scale), "prelude",
        [
            ((width, ext), BF16), ((8, ext), F32), ((ext, width), BF16), ((width, ext), BF16),
            ((pairs, blk, *pair_shape), BF16), (whole, BF16), (single, BF16), (middle, BF16),
            (single, BF16),
        ],
        [neighbours, x_on, x_off, w_in, *kept, q_t, top_grad[0]],
        scratch=[
            ((ext, width), BF16), ((width, ext), BF16), ((pairs, blk, *pair_shape), F32),
        ],
        smem=1,
    )
    common = [w_back, v_nat, probs, attn_t]
    for_rim = [w_in, xn_t, inv, q_t]
    others = (width, rows - 2 * tile)
    rim_scratch = [((2 * width, tile), BF16)]
    zero_shape = [(single, BF16), ((pairs, *pair_shape), BF16)]
    mid_shape = [(middle, BF16), ((pairs, blk - 2, *pair_shape), BF16)]
    received = []
    for k in range(sections - 1):
        here = sections - 1 - k
        moved = k > 0
        *new, da_zero, ds_zero, c_on = call(
            functools.partial(stage_zero_kernel, blk, tile, moved), "stage_zero",
            [(single, BF16)] * moved + zero_shape + [(single, BF16)],
            [g_zero, *received[:1], *common, *for_rim], scratch=rim_scratch,
        )
        g_zero = new[0] if moved else g_zero
        on = lax.ppermute(c_on, "dom", other_core(parts))
        *new, da_mid, ds_mid, zero = call(
            functools.partial(stage_mid_kernel, blk, tile, moved), "stage_mid",
            [(middle, BF16)] * moved + mid_shape + [(single, BF16)],
            [g_mid, *received[1:2], g_zero, da_zero, ds_zero, *common, *for_rim, k_t],
            scratch=[((3 * width, tile), BF16)],
        )
        g_mid = new[0] if moved else g_mid
        zero = call(add_rim_kernel, "add_on", [(single, BF16)], [zero, on])[0]
        *new, da_one, c_off = call(
            functools.partial(stage_one_kernel, blk, tile, moved), "stage_one",
            [(single, BF16)] * (moved + 2),
            [g_one, *received[2:], *common, *for_rim], scratch=rim_scratch,
        )
        g_one = new[0] if moved else g_one
        off = lax.ppermute(c_off, "dom", next_chip(parts))
        mid, one = call(
            functools.partial(stage_main_kernel, blk, tile), "stage_main",
            [(middle, BF16), (single, BF16)],
            [
                g_mid, g_one, da_zero, da_mid, da_one, ds_zero, ds_mid, w_in, xn_t, inv, v_nat, k_t, q_t,
                probs, attn_t,
            ],
            scratch=[((pairs, *pair_shape), BF16), ((3 * width, rows - tile), BF16)],
        )
        one = call(add_rim_kernel, "add_off", [(single, BF16)], [one, off])[0]
        received = [lax.ppermute(part, "section", [(here, here - 1)]) for part in (zero, mid, one)]
    direct = parts == 8
    chips = parts // 2
    every = 4 * width
    row = width // parts
    g_zero, da_zero, ds_zero, _ = call(
        functools.partial(stage_zero_kernel, blk, tile, True), "last_zero",
        [(single, BF16)] + zero_shape + [(single, BF16)],
        [g_zero, received[0], *common, *for_rim], scratch=rim_scratch,
    )
    g_mid, da_mid, ds_mid, d_low = call(
        functools.partial(last_mid_kernel, blk, tile), "last_mid",
        [(middle, BF16)] + mid_shape + [((3 * width, 2 * tile), BF16)],
        [g_mid, received[1], da_zero, ds_zero, *common, q_t, k_t],
    )
    g_one, d_high, *give = call(
        functools.partial(last_terms_kernel, blk, tile, chips), "last_terms",
        [(single, BF16), ((3 * width, rows), BF16)] + [((chips, row, every), BF16)] * direct,
        [
            g_one, received[2], g_zero, g_mid, da_zero, da_mid, ds_zero, ds_mid, w_back, v_nat, k_t, q_t,
            probs, attn_t, xn_t, d_low,
        ],
        scratch=[(single, BF16), ((pairs, *pair_shape), BF16)],
    )
    after = d_high
    if direct:
        got = lax.ppermute(give[0], "dom", other_core(parts))
        steps = ((1, 2), (2, 1))
        give_a, own_a, give_b, own_b = call(
            functools.partial(keep_kernel, chips, steps), "keep",
            [((2, row, every // 2), BF16), ((2, row, every // 2), F32)] * 2,
            [got, xn_t, d_low, d_high, attn_t, g_zero, g_mid, g_one], scratch=[((chips, row, every), F32)],
        )
        got_b = lax.ppermute(give_b, "dom", chips_apart(parts, steps[1][0]))
        got_a = lax.ppermute(give_a, "dom", chips_apart(parts, steps[0][0]))
        after = own_a
    y, c_on, c_off = call(
        functools.partial(last_input_kernel, blk, tile), "last_input",
        [(whole, BF16), (single, BF16), (single, BF16)],
        [after, g_zero, g_mid, g_one, d_low, d_high, w_in, xn_t, inv],
    )
    off = lax.ppermute(c_off, "dom", next_chip(parts))
    on = lax.ppermute(c_on, "dom", other_core(parts))
    if direct:
        give_a, rest_a, give_b, rest_b = call(
            middle_kernel, "middle", [((row, every // 2), BF16), ((row, every // 2), F32)] * 2,
            [own_a, got_a, own_b, got_b, on],
        )
        got_b = lax.ppermute(give_b, "dom", chips_apart(parts, steps[1][1]))
        got_a = lax.ppermute(give_a, "dom", chips_apart(parts, steps[0][1]))
    y = call(
        functools.partial(finish_input_kernel, blk, tile), "finish_input", [((rows, width), BF16)],
        [y, on, off],
    )[0]
    if direct:
        qkv_grad, out_grad = call(
            total_kernel, "total", [((row, 3 * width), F32), ((row, width), F32)],
            [rest_a, got_a, rest_b, got_b],
        )
    else:
        g_t = jnp.concatenate([g_zero, g_mid, g_one], axis=1)
        d_qkv = jnp.concatenate([d_low, d_high], axis=1)
        term = jnp.concatenate([mm(xn_t, d_qkv, NT), mm(attn_t, g_t, NT)], axis=1)
        total = lax.psum_scatter(term, "dom", scatter_dimension=0, tiled=True)
        qkv_grad, out_grad = total[:, : 3 * width], total[:, 3 * width :]
    return (y[None, None], qkv_grad[None], out_grad[None])


def solution(mesh):
    placed = (
        P("section", None, "dom", None),
        P(None, "dom", None),
        P("section", None, None),
        P("section", None, None),
        P("dom", None),
    )
    return jax.shard_map(
        local,
        mesh=mesh,
        in_specs=placed,
        out_specs=(
            P("section", None, "dom", None),
            P("section", "dom", None),
            P("section", "dom", None),
        ),
        check_vma=False,
    )
```

```python
import functools

import jax
import jax.numpy as jnp
from jax import lax
from jax.experimental import pallas as pl
from jax.experimental.pallas import tpu as pltpu
from jax.sharding import PartitionSpec as P

HEADS = 8
EPS = 1e-05
F32 = jnp.float32
BF16 = jnp.bfloat16
NN = (((1,), (0,)), ((), ()))
NT = (((1,), (1,)), ((), ()))
VMEM_LIMIT = 20 * 1024 * 1024


def mm(a, b, dims=NN):
    return lax.dot_general(a, b, dims, preferred_element_type=F32)


def cols(start, count=1, tile=128):
    return slice(start * tile, (start + count) * tile)


def call(kernel, name, outs, args, scratch=(), smem=0):
    vmem = pl.BlockSpec(memory_space=pltpu.VMEM)
    scalars = pl.BlockSpec(memory_space=pltpu.SMEM)
    return pl.pallas_call(
        kernel,
        in_specs=[scalars] * smem + [vmem] * (len(args) - smem),
        out_specs=[vmem] * len(outs),
        out_shape=[jax.ShapeDtypeStruct(shape, dtype) for shape, dtype in outs],
        scratch_shapes=[pltpu.VMEM(shape, dtype) for shape, dtype in scratch],
        compiler_params=pltpu.CompilerParams(vmem_limit_bytes=VMEM_LIMIT),
        cost_estimate=pl.CostEstimate(flops=1, bytes_accessed=1, transcendentals=0),
        name=name,
    )(*args)


def second_core():
    return lax.rem(lax.axis_index("dom"), 2) == 1


def block_of(b, blk):
    return jnp.where(second_core(), b, blk - 1 - b)


def rows_of(b, blk, tile):
    return pl.ds(pl.multiple_of(block_of(b, blk) * tile, tile), tile)


def halves(pair, hdim):
    zero = jnp.zeros((hdim, pair.shape[1]), pair.dtype)
    return jnp.concatenate(
        [
            jnp.concatenate([pair[:hdim], zero], axis=0),
            jnp.concatenate([zero, pair[hdim:]], axis=0),
        ],
        axis=1,
    )


def normalize(rows):
    xf = rows.astype(F32)
    cent = xf - jnp.mean(xf, axis=-1, keepdims=True)
    rstd = lax.rsqrt(jnp.mean(cent * cent, axis=-1, keepdims=True) + EPS)
    return cent * rstd, rstd


def project_tile(t, tile, scale, rows, w_qkv, xn_t, inv, k_nat, v_nat, k_t, v_t):
    width = rows.shape[1]
    here = cols(t, tile=tile)
    xhat, rstd = normalize(rows)
    xn = xhat.astype(BF16)
    xn_t[:, here] = xhat.T.astype(BF16)
    inv[:, here] = jnp.broadcast_to(rstd, (tile, 128)).T[0:8, :]
    keyval = mm(xn, w_qkv[:, width:])
    k_t[:, here] = (keyval[:, :width].T * scale).astype(BF16)
    v_t[:, here] = keyval[:, width:].T.astype(BF16)
    k_nat[here, :] = keyval[:, :width].astype(BF16)
    v_nat[here, :] = keyval[:, width:].astype(BF16)
    return xn


def pick_kernel(blk, tile, x, x_on, x_off):
    x_on[...] = x[rows_of(0, blk, tile), :]
    x_off[...] = x[rows_of(blk - 1, blk, tile), :]


def prelude_own_kernel(blk, tile, scale, x, w_qkv, xn_t, inv, k_nat, v_nat, k_t, v_t, q_t):
    width = x.shape[1]
    for b in range(blk):
        xn = project_tile(
            b, tile, scale, x[rows_of(b, blk, tile), :], w_qkv, xn_t, inv, k_nat, v_nat, k_t, v_t
        )
        q_t[:, cols(b, tile=tile)] = (mm(xn, w_qkv[:, :width]).T * scale).astype(BF16)


def prelude_kernel(
    blk, tile, scale, neighbours, x_on, x_off, w_qkv,
    xn_own, inv_own, k_own, v_own, kt_own, vt_own, q_t, top,
    xn_t, inv, v_nat, k_t, probs, attn_t, g_zero, g_mid, g_one, k_nat, v_t, scores,
):
    width = x_on.shape[1]
    hdim = width // HEADS
    ours = cols(1, blk, tile)
    xn_t[:, ours] = xn_own[...]
    inv[:, ours] = inv_own[...]
    k_nat[ours, :] = k_own[...]
    v_nat[ours, :] = v_own[...]
    k_t[:, ours] = kt_own[...]
    v_t[:, ours] = vt_own[...]
    is_last = lax.axis_index("section") == lax.axis_size("section") - 1
    for b in range(blk):
        g = jnp.where(is_last, top[rows_of(b, blk, tile), :].astype(F32).T, 0.0).astype(BF16)
        if b == 0:
            g_zero[...] = g
        elif b < blk - 1:
            g_mid[:, cols(b - 1, tile=tile)] = g
        else:
            g_one[...] = g
    for t, rows in ((0, x_on), (blk + 1, x_off)):
        project_tile(t, tile, scale, rows[...], w_qkv, xn_t, inv, k_nat, v_nat, k_t, v_t)
    blocks = blk * lax.axis_size("dom")
    second = second_core()
    for b in range(blk):
        place = block_of(b, blk)
        mine = lax.axis_index("dom") * blk + place
        below, above = lax.rem(mine + blocks - 1, blocks), lax.rem(mine + 1, blocks)
        before, after = jnp.where(second, below, above), jnp.where(second, above, below)
        has_before = has_after = False
        for j in range(1, neighbours.shape[1]):
            has_before |= neighbours[place, j] == before
            has_after |= neighbours[place, j] == after
        for i in range(HEADS // 2):
            lanes = cols(i, tile=2 * hdim)
            q = halves(q_t[lanes, cols(b, tile=tile)], hdim)
            s = mm(k_nat[cols(b, 3, tile), lanes], q)
            scores[i, b] = jnp.concatenate(
                [
                    jnp.where(has_before, s[:tile], -1e30),
                    s[tile : 2 * tile],
                    jnp.where(has_after, s[2 * tile :], -1e30),
                ],
                axis=0,
            )
    for b in range(blk):
        for i in range(HEADS // 2):
            s = scores[i, b]
            e = jnp.exp(s - jnp.max(s, axis=0, keepdims=True))
            probs[i, b] = (e * (1.0 / jnp.sum(e, axis=0, keepdims=True))).astype(BF16)
    for b in range(blk):
        for h in range(HEADS):
            head = cols(h, tile=hdim)
            p = probs[h // 2, b, :, cols(h % 2, tile=tile)]
            attn_t[head, cols(b, tile=tile)] = mm(v_t[head, cols(b, 3, tile)], p).astype(BF16)


def score_grad(i, b, first, count, tile, hdim, v_nat, probs, attn_t, da):
    lanes, own = cols(i, tile=2 * hdim), cols(b, tile=tile)
    prod = da.astype(F32) * attn_t[lanes, own].astype(F32)
    total = jnp.concatenate(
        [
            jnp.sum(prod[:hdim], axis=0, keepdims=True),
            jnp.sum(prod[hdim:], axis=0, keepdims=True),
        ],
        axis=1,
    )
    dp = mm(v_nat[cols(b + first, count, tile), lanes], halves(da, hdim))
    return (probs[i, b, cols(first, count, tile), :].astype(F32) * (dp - total)).astype(BF16)


def norm_grad(dn, xn, rstd):
    xhat = xn.astype(F32)
    first = jnp.mean(dn, axis=0, keepdims=True)
    second = jnp.mean(dn * xhat, axis=0, keepdims=True)
    return rstd * (dn - first - xhat * second)


def rim_grad(b, t, tile, hdim, q_t, probs, da, ds, w_qkv, xn_t, inv, d_rim):
    width = q_t.shape[0]
    own, near, here = cols(b, tile=tile), cols(t - b, tile=tile), cols(t, tile=tile)
    for i in range(HEADS // 2):
        lanes = cols(i, tile=2 * hdim)
        after = slice(width + i * 2 * hdim, width + (i + 1) * 2 * hdim)
        d_rim[lanes, :] = mm(halves(q_t[lanes, own], hdim), ds(i), NT).astype(BF16)
        d_rim[after, :] = mm(halves(da(lanes), hdim), probs[i, b, near, :], NT).astype(BF16)
    dn = mm(w_qkv[:, width:], d_rim[...])
    return norm_grad(dn, xn_t[:, here], inv[0:1, here]).astype(BF16)


def add(a, b):
    return (a[...].astype(F32) + b[...].astype(F32)).astype(BF16)


def joined(blk, tile, das, dss):
    def da(lanes, b):
        if b == 0:
            return das[0][lanes, :]
        return das[1][lanes, cols(b - 1, tile=tile)] if b < blk - 1 else das[2][lanes, :]

    def ds(i, b, near, across):
        if b == 0:
            return dss[0][i, near, across]
        return dss[1][i, b - 1, near, across] if b < blk - 1 else dss[2][i, near, across]

    return da, ds


def end_grads(b, tile, hdim, g, w_out, v_nat, probs, attn_t, da, ds):
    da[...] = mm(w_out[...], g[...]).astype(BF16)
    for i in range(HEADS // 2):
        part = da[cols(i, tile=2 * hdim), :]
        ds[i] = score_grad(i, b, 0, 3, tile, hdim, v_nat, probs, attn_t, part)


def mid_grads(blk, tile, hdim, g, w_out, v_nat, probs, attn_t, da, ds):
    da[...] = mm(w_out[...], g[...]).astype(BF16)
    for b in range(1, blk - 1):
        for i in range(HEADS // 2):
            part = da[cols(i, tile=2 * hdim), cols(b - 1, tile=tile)]
            ds[i, b - 1] = score_grad(i, b, 0, 3, tile, hdim, v_nat, probs, attn_t, part)


def own_terms(blk, tile, hdim, first, last, q_t, k_t, probs, da, ds, d_qkv):
    width = q_t.shape[0]
    for i in range(HEADS // 2):
        lanes = cols(i, tile=2 * hdim)
        for n, left, right in (
            (1, lambda b: q_t[lanes, cols(b, tile=tile)], lambda b, near: ds(i, b, near, slice(None))),
            (2, lambda b: da(lanes, b), lambda b, near: probs[i, b, near, :]),
        ):
            total = [None] * (blk + 2)
            for b in range(max(first - 2, 0), min(last + 1, blk)):
                low, high = max(b, first), min(b + 3, last + 1)
                near = slice((low - b) * tile, (high - b) * tile)
                part = mm(halves(left(b), hdim), right(b, near), NT)
                for t in range(low, high):
                    more = part[:, cols(t - low, tile=tile)]
                    total[t] = more if total[t] is None else total[t] + more
            start = n * width + i * 2 * hdim
            for t in range(first, last + 1):
                d_qkv[start : start + 2 * hdim, cols(t - first, tile=tile)] = total[t].astype(BF16)
        for b in range(max(first - 1, 0), min(last, blk)):
            for h in (2 * i, 2 * i + 1):
                head = cols(h, tile=hdim)
                d_qkv[head, cols(b + 1 - first, tile=tile)] = mm(
                    k_t[head, cols(b, 3, tile)],
                    ds(i, b, slice(None), cols(h % 2, tile=tile)),
                ).astype(BF16)


def stage_zero_kernel(blk, tile, moved, *refs):
    if moved:
        g_prev, arrived, *refs = refs
    else:
        g, *refs = refs
    w_out, v_nat, probs, attn_t, w_qkv, xn_t, inv, q_t, *refs = refs
    if moved:
        g, *refs = refs
        g[...] = add(g_prev, arrived)
    da, ds, c_on, d_rim = refs
    hdim = g.shape[0] // HEADS
    end_grads(0, tile, hdim, g, w_out, v_nat, probs, attn_t, da, ds)
    c_on[...] = rim_grad(
        0, 0, tile, hdim, q_t, probs, lambda lanes: da[lanes, :], lambda i: ds[i, :tile, :],
        w_qkv, xn_t, inv, d_rim,
    )


def stage_mid_kernel(blk, tile, moved, *refs):
    if moved:
        g_prev, arrived, *refs = refs
    else:
        g, *refs = refs
    g_zero, da_zero, ds_zero, w_out, v_nat, probs, attn_t, w_qkv, xn_t, inv, q_t, k_t, *refs = refs
    if moved:
        g, *refs = refs
        g[...] = add(g_prev, arrived)
    da, ds, y, d_first = refs
    hdim = g.shape[0] // HEADS
    mid_grads(blk, tile, hdim, g, w_out, v_nat, probs, attn_t, da, ds)
    by_block = joined(blk, tile, (da_zero, da), (ds_zero, ds))
    own_terms(blk, tile, hdim, 1, 1, q_t, k_t, probs, *by_block, d_first)
    dn = mm(w_qkv[...], d_first[...])
    here = cols(1, tile=tile)
    y[...] = (g_zero[...].astype(F32) + norm_grad(dn, xn_t[:, here], inv[0:1, here])).astype(BF16)


def last_mid_kernel(
    blk, tile, g_prev, arrived, da_zero, ds_zero, w_out, v_nat, probs, attn_t, q_t, k_t, g, da, ds, d_low
):
    g[...] = add(g_prev, arrived)
    width = g.shape[0]
    hdim = width // HEADS
    mid_grads(blk, tile, hdim, g, w_out, v_nat, probs, attn_t, da, ds)
    d_low[:width, :tile] = jnp.zeros((width, tile), BF16)
    by_block = joined(blk, tile, (da_zero, da), (ds_zero, ds))
    own_terms(blk, tile, hdim, 0, 1, q_t, k_t, probs, *by_block, d_low)


def stage_one_kernel(blk, tile, moved, *refs):
    if moved:
        g_prev, arrived, *refs = refs
    else:
        g, *refs = refs
    w_out, v_nat, probs, attn_t, w_qkv, xn_t, inv, q_t, *refs = refs
    if moved:
        g, *refs = refs
        g[...] = add(g_prev, arrived)
    da, c_off, d_rim = refs
    hdim = g.shape[0] // HEADS
    da[...] = mm(w_out[...], g[...]).astype(BF16)
    b = blk - 1
    ds = [
        score_grad(i, b, 2, 1, tile, hdim, v_nat, probs, attn_t, da[cols(i, tile=2 * hdim), :])
        for i in range(HEADS // 2)
    ]
    c_off[...] = rim_grad(
        b, blk + 1, tile, hdim, q_t, probs, lambda lanes: da[lanes, :], lambda i: ds[i],
        w_qkv, xn_t, inv, d_rim,
    )


def stage_main_kernel(
    blk, tile, g_mid, g_one, da_zero, da_mid, da_one, ds_zero, ds_mid, w_qkv, xn_t, inv, v_nat, k_t, q_t,
    probs, attn_t, mid, one, ds_one, d_qkv,
):
    hdim = g_mid.shape[0] // HEADS
    for i in range(HEADS // 2):
        part = da_one[cols(i, tile=2 * hdim), :]
        ds_one[i] = score_grad(i, blk - 1, 0, 3, tile, hdim, v_nat, probs, attn_t, part)
    by_block = joined(blk, tile, (da_zero, da_mid, da_one), (ds_zero, ds_mid, ds_one))
    own_terms(blk, tile, hdim, 2, blk, q_t, k_t, probs, *by_block, d_qkv)
    dn = mm(w_qkv[...], d_qkv[...])
    for b in range(1, blk):
        here, place = cols(b + 1, tile=tile), cols(b - 1, tile=tile)
        out = norm_grad(dn[:, place], xn_t[:, here], inv[0:1, here])
        if b < blk - 1:
            mid[:, place] = (g_mid[:, place].astype(F32) + out).astype(BF16)
        else:
            one[...] = (g_one[...].astype(F32) + out).astype(BF16)


def add_rim_kernel(one, rim, out):
    out[...] = add(one, rim)


def last_terms_kernel(
    blk, tile, chips, g_prev, arrived, g_zero, g_mid, da_zero, da_mid, ds_zero, ds_mid, w_out, v_nat, k_t,
    q_t, probs, attn_t, xn_t, d_low, g_one, d_high, *refs
):
    *give, da_one, ds_one = refs
    width = g_prev.shape[0]
    hdim = width // HEADS
    g_one[...] = add(g_prev, arrived)
    end_grads(blk - 1, tile, hdim, g_one, w_out, v_nat, probs, attn_t, da_one, ds_one)
    d_high[:width, cols(blk - 1, tile=tile)] = jnp.zeros((width, tile), BF16)
    by_block = joined(blk, tile, (da_zero, da_mid, da_one), (ds_zero, ds_mid, ds_one))
    own_terms(blk, tile, hdim, 2, blk + 1, q_t, k_t, probs, *by_block, d_high)
    if give:
        core = 1 - lax.rem(lax.axis_index("dom"), 2)
        part = weight_rows(core, chips, xn_t, (d_low, d_high), attn_t, (g_zero, g_mid, g_one))
        rows = width // (2 * chips)
        for z in range(chips):
            here = slice(z * rows, (z + 1) * rows)
            for across, term in part:
                give[0][z, :, across] = term[here].astype(BF16)


def last_input_kernel(
    blk, tile, after, g_zero, g_mid, g_one, d_low, d_high, w_qkv, xn_t, inv, y, c_on, c_off
):
    outs = []
    for part in (d_low, d_high):
        dn = mm(w_qkv[...], part[...])
        for n in range(part.shape[1] // tile):
            here = cols(len(outs), tile=tile)
            outs.append(norm_grad(dn[:, cols(n, tile=tile)], xn_t[:, here], inv[0:1, here]))
    c_on[...] = outs[0].astype(BF16)
    c_off[...] = outs[-1].astype(BF16)
    for b in range(blk):
        own = cols(b, tile=tile)
        g = g_zero[...] if b == 0 else g_mid[:, cols(b - 1, tile=tile)] if b < blk - 1 else g_one[...]
        y[:, own] = (g.astype(F32) + outs[b + 1]).astype(BF16)


def finish_input_kernel(blk, tile, y_t, on, off, out):
    for b in range(blk):
        part = y_t[:, cols(b, tile=tile)].astype(F32)
        if b == 0:
            part = part + on[...].astype(F32)
        if b == blk - 1:
            part = part + off[...].astype(F32)
        out[rows_of(b, blk, tile), :] = part.T.astype(BF16)


def weight_rows(core, chips, xn_t, d_qkv, attn_t, g):
    def picked(ref):
        rows = ref.shape[0] // (2 * chips)
        starts = [pl.multiple_of((2 * z + core) * rows, rows) for z in range(chips)]
        return jnp.concatenate([ref[pl.ds(s, rows), :] for s in starts], axis=0)

    def product(ref, parts):
        left, start, total = picked(ref), 0, None
        for part in parts:
            more = mm(left[:, start : start + part.shape[1]], part[...], NT)
            total = more if total is None else total + more
            start += part.shape[1]
        return total

    wide, width = d_qkv[0].shape[0], g[0].shape[0]
    return (
        (slice(0, wide), product(xn_t, d_qkv)),
        (slice(wide, wide + width), product(attn_t, g)),
    )


def mine_kernel(chips, xn_t, d_low, d_high, attn_t, g_zero, g_mid, g_one, both):
    core = lax.rem(lax.axis_index("dom"), 2)
    rows = both.shape[1]
    for across, term in weight_rows(core, chips, xn_t, (d_low, d_high), attn_t, (g_zero, g_mid, g_one)):
        for z in range(chips):
            both[z, :, across] = term[z * rows : (z + 1) * rows]


def keep_kernel(chips, steps, got, both, *outs):
    chip = lax.axis_index("dom") // 2
    half = got.shape[2] // 2
    for n, (first, second) in enumerate(steps):
        give, own = outs[2 * n : 2 * n + 2]
        across = slice(n * half, (n + 1) * half)

        def total(distance):
            z = lax.bitwise_xor(chip, distance)
            return both[z, :, across] + got[z, :, across].astype(F32)

        give[0] = total(first).astype(BF16)
        give[1] = total(first ^ second).astype(BF16)
        own[0] = total(0)
        own[1] = total(second)


def middle_kernel(own_a, got_a, own_b, got_b, *refs):
    give_a, rest_a, give_b, rest_b = refs[-4:]
    for own, got, give, rest in ((own_b, got_b, give_b, rest_b), (own_a, got_a, give_a, rest_a)):
        rest[...] = own[0] + got[0].astype(F32)
        give[...] = (own[1] + got[1].astype(F32)).astype(BF16)


def total_kernel(rest_a, got_a, rest_b, got_b, qkv_grad, out_grad):
    width = out_grad.shape[1]
    qkv_grad[:, : 2 * width] = rest_a[...] + got_a[...].astype(F32)
    total = rest_b[...] + got_b[...].astype(F32)
    qkv_grad[:, 2 * width :] = total[:, :width]
    out_grad[...] = total[:, width:]


def other_core(parts):
    return [(i, i ^ 1) for i in range(parts)]


def next_chip(parts):
    return [(i, (i + 1 if i % 2 else i - 1) % parts) for i in range(parts)]


def chips_apart(parts, step):
    return [(i, i ^ (2 * step)) for i in range(parts)]


def local(layer_inputs, top_grad, w_qkv, w_out, neighbours):
    sections = lax.axis_size("section")
    parts = lax.axis_size("dom")
    blk = neighbours.shape[0]
    rows, width = top_grad.shape[1:]
    tile = rows // blk
    ext = rows + 2 * tile
    hdim = width // HEADS
    scale = 1.0 / hdim**0.5
    x = layer_inputs[0, 0]
    w_in, w_back = w_qkv[0], w_out[0]
    whole, middle, single = ((width, n) for n in (rows, rows - 2 * tile, tile))
    pairs = HEADS // 2
    pair_shape = (3 * tile, 2 * tile)
    x_on, x_off = call(
        functools.partial(pick_kernel, blk, tile), "pick", [((tile, width), BF16)] * 2, [x]
    )
    x_on = lax.ppermute(x_on, "dom", other_core(parts))
    x_off = lax.ppermute(x_off, "dom", next_chip(parts))
    *kept, q_t = call(
        functools.partial(prelude_own_kernel, blk, tile, scale), "prelude_own",
        [
            (whole, BF16), ((8, rows), F32), ((rows, width), BF16), ((rows, width), BF16),
            (whole, BF16), (whole, BF16), (whole, BF16),
        ],
        [x, w_in],
    )
    xn_t, inv, v_nat, k_t, probs, attn_t, g_zero, g_mid, g_one = call(
        functools.partial(prelude_kernel, blk, tile, scale), "prelude",
        [
            ((width, ext), BF16), ((8, ext), F32), ((ext, width), BF16), ((width, ext), BF16),
            ((pairs, blk, *pair_shape), BF16), (whole, BF16), (single, BF16), (middle, BF16),
            (single, BF16),
        ],
        [neighbours, x_on, x_off, w_in, *kept, q_t, top_grad[0]],
        scratch=[
            ((ext, width), BF16), ((width, ext), BF16), ((pairs, blk, *pair_shape), F32),
        ],
        smem=1,
    )
    common = [w_back, v_nat, probs, attn_t]
    for_rim = [w_in, xn_t, inv, q_t]
    others = (width, rows - 2 * tile)
    rim_scratch = [((2 * width, tile), BF16)]
    zero_shape = [(single, BF16), ((pairs, *pair_shape), BF16)]
    mid_shape = [(middle, BF16), ((pairs, blk - 2, *pair_shape), BF16)]
    received = []
    for k in range(sections - 1):
        here = sections - 1 - k
        moved = k > 0
        *new, da_zero, ds_zero, c_on = call(
            functools.partial(stage_zero_kernel, blk, tile, moved), "stage_zero",
            [(single, BF16)] * moved + zero_shape + [(single, BF16)],
            [g_zero, *received[:1], *common, *for_rim], scratch=rim_scratch,
        )
        g_zero = new[0] if moved else g_zero
        on = lax.ppermute(c_on, "dom", other_core(parts))
        *new, da_mid, ds_mid, zero = call(
            functools.partial(stage_mid_kernel, blk, tile, moved), "stage_mid",
            [(middle, BF16)] * moved + mid_shape + [(single, BF16)],
            [g_mid, *received[1:2], g_zero, da_zero, ds_zero, *common, *for_rim, k_t],
            scratch=[((3 * width, tile), BF16)],
        )
        g_mid = new[0] if moved else g_mid
        zero = call(add_rim_kernel, "add_on", [(single, BF16)], [zero, on])[0]
        *new, da_one, c_off = call(
            functools.partial(stage_one_kernel, blk, tile, moved), "stage_one",
            [(single, BF16)] * (moved + 2),
            [g_one, *received[2:], *common, *for_rim], scratch=rim_scratch,
        )
        g_one = new[0] if moved else g_one
        off = lax.ppermute(c_off, "dom", next_chip(parts))
        mid, one = call(
            functools.partial(stage_main_kernel, blk, tile), "stage_main",
            [(middle, BF16), (single, BF16)],
            [
                g_mid, g_one, da_zero, da_mid, da_one, ds_zero, ds_mid, w_in, xn_t, inv, v_nat, k_t, q_t,
                probs, attn_t,
            ],
            scratch=[((pairs, *pair_shape), BF16), ((3 * width, rows - tile), BF16)],
        )
        one = call(add_rim_kernel, "add_off", [(single, BF16)], [one, off])[0]
        received = [lax.ppermute(part, "section", [(here, here - 1)]) for part in (zero, mid, one)]
    direct = parts == 8
    chips = parts // 2
    every = 4 * width
    row = width // parts
    g_zero, da_zero, ds_zero, _ = call(
        functools.partial(stage_zero_kernel, blk, tile, True), "last_zero",
        [(single, BF16)] + zero_shape + [(single, BF16)],
        [g_zero, received[0], *common, *for_rim], scratch=rim_scratch,
    )
    g_mid, da_mid, ds_mid, d_low = call(
        functools.partial(last_mid_kernel, blk, tile), "last_mid",
        [(middle, BF16)] + mid_shape + [((3 * width, 2 * tile), BF16)],
        [g_mid, received[1], da_zero, ds_zero, *common, q_t, k_t],
    )
    g_one, d_high, *give = call(
        functools.partial(last_terms_kernel, blk, tile, chips), "last_terms",
        [(single, BF16), ((3 * width, rows), BF16)] + [((chips, row, every), BF16)] * direct,
        [
            g_one, received[2], g_zero, g_mid, da_zero, da_mid, ds_zero, ds_mid, w_back, v_nat, k_t, q_t,
            probs, attn_t, xn_t, d_low,
        ],
        scratch=[(single, BF16), ((pairs, *pair_shape), BF16)],
    )
    after = d_high
    if direct:
        got = lax.ppermute(give[0], "dom", other_core(parts))
        steps = ((1, 2), (2, 1))
        mine = call(
            functools.partial(mine_kernel, chips), "mine", [((chips, row, every), F32)],
            [xn_t, d_low, d_high, attn_t, g_zero, g_mid, g_one],
        )[0]
        give_a, own_a, give_b, own_b = call(
            functools.partial(keep_kernel, chips, steps), "keep",
            [((2, row, every // 2), BF16), ((2, row, every // 2), F32)] * 2,
            [got, mine],
        )
        got_a = lax.ppermute(give_a, "dom", chips_apart(parts, steps[0][0]))
        got_b = lax.ppermute(give_b, "dom", chips_apart(parts, steps[1][0]))
        after = own_a
    y, c_on, c_off = call(
        functools.partial(last_input_kernel, blk, tile), "last_input",
        [(whole, BF16), (single, BF16), (single, BF16)],
        [after, g_zero, g_mid, g_one, d_low, d_high, w_in, xn_t, inv],
    )
    off = lax.ppermute(c_off, "dom", next_chip(parts))
    on = lax.ppermute(c_on, "dom", other_core(parts))
    if direct:
        give_a, rest_a, give_b, rest_b = call(
            middle_kernel, "middle", [((row, every // 2), BF16), ((row, every // 2), F32)] * 2,
            [own_a, got_a, own_b, got_b, on],
        )
        got_b = lax.ppermute(give_b, "dom", chips_apart(parts, steps[1][1]))
        got_a = lax.ppermute(give_a, "dom", chips_apart(parts, steps[0][1]))
    y = call(
        functools.partial(finish_input_kernel, blk, tile), "finish_input", [((rows, width), BF16)],
        [y, on, off],
    )[0]
    if direct:
        qkv_grad, out_grad = call(
            total_kernel, "total", [((row, 3 * width), F32), ((row, width), F32)],
            [rest_a, got_a, rest_b, got_b],
        )
    else:
        g_t = jnp.concatenate([g_zero, g_mid, g_one], axis=1)
        d_qkv = jnp.concatenate([d_low, d_high], axis=1)
        term = jnp.concatenate([mm(xn_t, d_qkv, NT), mm(attn_t, g_t, NT)], axis=1)
        total = lax.psum_scatter(term, "dom", scatter_dimension=0, tiled=True)
        qkv_grad, out_grad = total[:, : 3 * width], total[:, 3 * width :]
    return (y[None, None], qkv_grad[None], out_grad[None])


def solution(mesh):
    placed = (
        P("section", None, "dom", None),
        P(None, "dom", None),
        P("section", None, None),
        P("section", None, None),
        P("dom", None),
    )
    return jax.shard_map(
        local,
        mesh=mesh,
        in_specs=placed,
        out_specs=(
            P("section", None, "dom", None),
            P("section", "dom", None),
            P("section", "dom", None),
        ),
        check_vma=False,
    )
```

```python
import functools

import jax
import jax.numpy as jnp
from jax import lax
from jax.experimental import pallas as pl
from jax.experimental.pallas import tpu as pltpu
from jax.sharding import PartitionSpec as P

HEADS = 8
EPS = 1e-05
F32 = jnp.float32
BF16 = jnp.bfloat16
NN = (((1,), (0,)), ((), ()))
NT = (((1,), (1,)), ((), ()))
VMEM_LIMIT = 20 * 1024 * 1024


def mm(a, b, dims=NN):
    return lax.dot_general(a, b, dims, preferred_element_type=F32)


def cols(start, count=1, tile=128):
    return slice(start * tile, (start + count) * tile)


def call(kernel, name, outs, args, scratch=(), smem=0):
    vmem = pl.BlockSpec(memory_space=pltpu.VMEM)
    scalars = pl.BlockSpec(memory_space=pltpu.SMEM)
    return pl.pallas_call(
        kernel,
        in_specs=[scalars] * smem + [vmem] * (len(args) - smem),
        out_specs=[vmem] * len(outs),
        out_shape=[jax.ShapeDtypeStruct(shape, dtype) for shape, dtype in outs],
        scratch_shapes=[pltpu.VMEM(shape, dtype) for shape, dtype in scratch],
        compiler_params=pltpu.CompilerParams(vmem_limit_bytes=VMEM_LIMIT),
        cost_estimate=pl.CostEstimate(flops=1, bytes_accessed=1, transcendentals=0),
        name=name,
    )(*args)


def second_core():
    return lax.rem(lax.axis_index("dom"), 2) == 1


def block_of(b, blk):
    return jnp.where(second_core(), b, blk - 1 - b)


def rows_of(b, blk, tile):
    return pl.ds(pl.multiple_of(block_of(b, blk) * tile, tile), tile)


def halves(pair, hdim):
    zero = jnp.zeros((hdim, pair.shape[1]), pair.dtype)
    return jnp.concatenate(
        [
            jnp.concatenate([pair[:hdim], zero], axis=0),
            jnp.concatenate([zero, pair[hdim:]], axis=0),
        ],
        axis=1,
    )


def normalize(rows):
    xf = rows.astype(F32)
    cent = xf - jnp.mean(xf, axis=-1, keepdims=True)
    rstd = lax.rsqrt(jnp.mean(cent * cent, axis=-1, keepdims=True) + EPS)
    return cent * rstd, rstd


def project_tile(t, tile, scale, rows, w_qkv, xn_t, inv, k_nat, v_nat, k_t, v_t):
    width = rows.shape[1]
    here = cols(t, tile=tile)
    xhat, rstd = normalize(rows)
    xn = xhat.astype(BF16)
    xn_t[:, here] = xhat.T.astype(BF16)
    inv[:, here] = jnp.broadcast_to(rstd, (tile, 128)).T[0:8, :]
    keyval = mm(xn, w_qkv[:, width:])
    k_t[:, here] = (keyval[:, :width].T * scale).astype(BF16)
    v_t[:, here] = keyval[:, width:].T.astype(BF16)
    k_nat[here, :] = keyval[:, :width].astype(BF16)
    v_nat[here, :] = keyval[:, width:].astype(BF16)
    return xn


def pick_kernel(blk, tile, x, x_on, x_off):
    x_on[...] = x[rows_of(0, blk, tile), :]
    x_off[...] = x[rows_of(blk - 1, blk, tile), :]


def prelude_own_kernel(blk, tile, scale, x, w_qkv, xn_t, inv, k_nat, v_nat, k_t, v_t, q_t):
    width = x.shape[1]
    for b in range(blk):
        xn = project_tile(
            b, tile, scale, x[rows_of(b, blk, tile), :], w_qkv, xn_t, inv, k_nat, v_nat, k_t, v_t
        )
        q_t[:, cols(b, tile=tile)] = (mm(xn, w_qkv[:, :width]).T * scale).astype(BF16)


def prelude_kernel(
    blk, tile, scale, neighbours, x_on, x_off, w_qkv,
    xn_own, inv_own, k_own, v_own, kt_own, vt_own, q_t, top,
    xn_t, inv, v_nat, k_t, probs, attn_t, g_zero, g_mid, g_one, k_nat, v_t, scores,
):
    width = x_on.shape[1]
    hdim = width // HEADS
    ours = cols(1, blk, tile)
    xn_t[:, ours] = xn_own[...]
    inv[:, ours] = inv_own[...]
    k_nat[ours, :] = k_own[...]
    v_nat[ours, :] = v_own[...]
    k_t[:, ours] = kt_own[...]
    v_t[:, ours] = vt_own[...]
    is_last = lax.axis_index("section") == lax.axis_size("section") - 1
    for b in range(blk):
        g = jnp.where(is_last, top[rows_of(b, blk, tile), :].astype(F32).T, 0.0).astype(BF16)
        if b == 0:
            g_zero[...] = g
        elif b < blk - 1:
            g_mid[:, cols(b - 1, tile=tile)] = g
        else:
            g_one[...] = g
    for t, rows in ((0, x_on), (blk + 1, x_off)):
        project_tile(t, tile, scale, rows[...], w_qkv, xn_t, inv, k_nat, v_nat, k_t, v_t)
    blocks = blk * lax.axis_size("dom")
    second = second_core()
    for b in range(blk):
        place = block_of(b, blk)
        mine = lax.axis_index("dom") * blk + place
        below, above = lax.rem(mine + blocks - 1, blocks), lax.rem(mine + 1, blocks)
        before, after = jnp.where(second, below, above), jnp.where(second, above, below)
        has_before = has_after = False
        for j in range(1, neighbours.shape[1]):
            has_before |= neighbours[place, j] == before
            has_after |= neighbours[place, j] == after
        for i in range(HEADS // 2):
            lanes = cols(i, tile=2 * hdim)
            q = halves(q_t[lanes, cols(b, tile=tile)], hdim)
            s = mm(k_nat[cols(b, 3, tile), lanes], q)
            scores[i, b] = jnp.concatenate(
                [
                    jnp.where(has_before, s[:tile], -1e30),
                    s[tile : 2 * tile],
                    jnp.where(has_after, s[2 * tile :], -1e30),
                ],
                axis=0,
            )
    for b in range(blk):
        for i in range(HEADS // 2):
            s = scores[i, b]
            e = jnp.exp(s - jnp.max(s, axis=0, keepdims=True))
            probs[i, b] = (e * (1.0 / jnp.sum(e, axis=0, keepdims=True))).astype(BF16)
    for b in range(blk):
        for h in range(HEADS):
            head = cols(h, tile=hdim)
            p = probs[h // 2, b, :, cols(h % 2, tile=tile)]
            attn_t[head, cols(b, tile=tile)] = mm(v_t[head, cols(b, 3, tile)], p).astype(BF16)


def score_grad(i, b, first, count, tile, hdim, v_nat, probs, attn_t, da):
    lanes, own = cols(i, tile=2 * hdim), cols(b, tile=tile)
    prod = da.astype(F32) * attn_t[lanes, own].astype(F32)
    total = jnp.concatenate(
        [
            jnp.sum(prod[:hdim], axis=0, keepdims=True),
            jnp.sum(prod[hdim:], axis=0, keepdims=True),
        ],
        axis=1,
    )
    dp = mm(v_nat[cols(b + first, count, tile), lanes], halves(da, hdim))
    return (probs[i, b, cols(first, count, tile), :].astype(F32) * (dp - total)).astype(BF16)


def norm_grad(dn, xn, rstd):
    xhat = xn.astype(F32)
    first = jnp.mean(dn, axis=0, keepdims=True)
    second = jnp.mean(dn * xhat, axis=0, keepdims=True)
    return rstd * (dn - first - xhat * second)


def rim_grad(b, t, tile, hdim, q_t, probs, da, ds, w_qkv, xn_t, inv, d_rim):
    width = q_t.shape[0]
    own, near, here = cols(b, tile=tile), cols(t - b, tile=tile), cols(t, tile=tile)
    for i in range(HEADS // 2):
        lanes = cols(i, tile=2 * hdim)
        after = slice(width + i * 2 * hdim, width + (i + 1) * 2 * hdim)
        d_rim[lanes, :] = mm(halves(q_t[lanes, own], hdim), ds(i), NT).astype(BF16)
        d_rim[after, :] = mm(halves(da(lanes), hdim), probs[i, b, near, :], NT).astype(BF16)
    dn = mm(w_qkv[:, width:], d_rim[...])
    return norm_grad(dn, xn_t[:, here], inv[0:1, here]).astype(BF16)


def add(a, b):
    return (a[...].astype(F32) + b[...].astype(F32)).astype(BF16)


def joined(blk, tile, das, dss):
    def da(lanes, b):
        if b == 0:
            return das[0][lanes, :]
        return das[1][lanes, cols(b - 1, tile=tile)] if b < blk - 1 else das[2][lanes, :]

    def ds(i, b, near, across):
        if b == 0:
            return dss[0][i, near, across]
        return dss[1][i, b - 1, near, across] if b < blk - 1 else dss[2][i, near, across]

    return da, ds


def end_grads(b, tile, hdim, g, w_out, v_nat, probs, attn_t, da, ds):
    da[...] = mm(w_out[...], g[...]).astype(BF16)
    for i in range(HEADS // 2):
        part = da[cols(i, tile=2 * hdim), :]
        ds[i] = score_grad(i, b, 0, 3, tile, hdim, v_nat, probs, attn_t, part)


def mid_grads(blk, tile, hdim, g, w_out, v_nat, probs, attn_t, da, ds):
    da[...] = mm(w_out[...], g[...]).astype(BF16)
    for b in range(1, blk - 1):
        for i in range(HEADS // 2):
            part = da[cols(i, tile=2 * hdim), cols(b - 1, tile=tile)]
            ds[i, b - 1] = score_grad(i, b, 0, 3, tile, hdim, v_nat, probs, attn_t, part)


def own_terms(blk, tile, hdim, first, last, q_t, k_t, probs, da, ds, d_qkv):
    width = q_t.shape[0]
    for i in range(HEADS // 2):
        lanes = cols(i, tile=2 * hdim)
        for n, left, right in (
            (1, lambda b: q_t[lanes, cols(b, tile=tile)], lambda b, near: ds(i, b, near, slice(None))),
            (2, lambda b: da(lanes, b), lambda b, near: probs[i, b, near, :]),
        ):
            total = [None] * (blk + 2)
            for b in range(max(first - 2, 0), min(last + 1, blk)):
                low, high = max(b, first), min(b + 3, last + 1)
                near = slice((low - b) * tile, (high - b) * tile)
                part = mm(halves(left(b), hdim), right(b, near), NT)
                for t in range(low, high):
                    more = part[:, cols(t - low, tile=tile)]
                    total[t] = more if total[t] is None else total[t] + more
            start = n * width + i * 2 * hdim
            for t in range(first, last + 1):
                d_qkv[start : start + 2 * hdim, cols(t - first, tile=tile)] = total[t].astype(BF16)
        for b in range(max(first - 1, 0), min(last, blk)):
            for h in (2 * i, 2 * i + 1):
                head = cols(h, tile=hdim)
                d_qkv[head, cols(b + 1 - first, tile=tile)] = mm(
                    k_t[head, cols(b, 3, tile)],
                    ds(i, b, slice(None), cols(h % 2, tile=tile)),
                ).astype(BF16)


def stage_zero_kernel(blk, tile, moved, *refs):
    if moved:
        g_prev, arrived, *refs = refs
    else:
        g, *refs = refs
    w_out, v_nat, probs, attn_t, w_qkv, xn_t, inv, q_t, *refs = refs
    if moved:
        g, *refs = refs
        g[...] = add(g_prev, arrived)
    da, ds, c_on, d_rim = refs
    hdim = g.shape[0] // HEADS
    end_grads(0, tile, hdim, g, w_out, v_nat, probs, attn_t, da, ds)
    c_on[...] = rim_grad(
        0, 0, tile, hdim, q_t, probs, lambda lanes: da[lanes, :], lambda i: ds[i, :tile, :],
        w_qkv, xn_t, inv, d_rim,
    )


def stage_mid_kernel(blk, tile, moved, *refs):
    if moved:
        g_prev, arrived, *refs = refs
    else:
        g, *refs = refs
    g_zero, da_zero, ds_zero, w_out, v_nat, probs, attn_t, w_qkv, xn_t, inv, q_t, k_t, *refs = refs
    if moved:
        g, *refs = refs
        g[...] = add(g_prev, arrived)
    da, ds, y, d_first = refs
    hdim = g.shape[0] // HEADS
    mid_grads(blk, tile, hdim, g, w_out, v_nat, probs, attn_t, da, ds)
    by_block = joined(blk, tile, (da_zero, da), (ds_zero, ds))
    own_terms(blk, tile, hdim, 1, 1, q_t, k_t, probs, *by_block, d_first)
    dn = mm(w_qkv[...], d_first[...])
    here = cols(1, tile=tile)
    y[...] = (g_zero[...].astype(F32) + norm_grad(dn, xn_t[:, here], inv[0:1, here])).astype(BF16)


def last_mid_kernel(
    blk, tile, g_prev, arrived, da_zero, ds_zero, w_out, v_nat, probs, attn_t, q_t, k_t, g, da, ds, d_low
):
    g[...] = add(g_prev, arrived)
    width = g.shape[0]
    hdim = width // HEADS
    mid_grads(blk, tile, hdim, g, w_out, v_nat, probs, attn_t, da, ds)
    d_low[:width, :tile] = jnp.zeros((width, tile), BF16)
    by_block = joined(blk, tile, (da_zero, da), (ds_zero, ds))
    own_terms(blk, tile, hdim, 0, 1, q_t, k_t, probs, *by_block, d_low)


def stage_one_kernel(blk, tile, moved, *refs):
    if moved:
        g_prev, arrived, *refs = refs
    else:
        g, *refs = refs
    w_out, v_nat, probs, attn_t, w_qkv, xn_t, inv, q_t, *refs = refs
    if moved:
        g, *refs = refs
        g[...] = add(g_prev, arrived)
    da, c_off, d_rim = refs
    hdim = g.shape[0] // HEADS
    da[...] = mm(w_out[...], g[...]).astype(BF16)
    b = blk - 1
    ds = [
        score_grad(i, b, 2, 1, tile, hdim, v_nat, probs, attn_t, da[cols(i, tile=2 * hdim), :])
        for i in range(HEADS // 2)
    ]
    c_off[...] = rim_grad(
        b, blk + 1, tile, hdim, q_t, probs, lambda lanes: da[lanes, :], lambda i: ds[i],
        w_qkv, xn_t, inv, d_rim,
    )


def stage_main_kernel(
    blk, tile, g_mid, g_one, da_zero, da_mid, da_one, ds_zero, ds_mid, w_qkv, xn_t, inv, v_nat, k_t, q_t,
    probs, attn_t, mid, one, ds_one, d_qkv,
):
    hdim = g_mid.shape[0] // HEADS
    for i in range(HEADS // 2):
        part = da_one[cols(i, tile=2 * hdim), :]
        ds_one[i] = score_grad(i, blk - 1, 0, 3, tile, hdim, v_nat, probs, attn_t, part)
    by_block = joined(blk, tile, (da_zero, da_mid, da_one), (ds_zero, ds_mid, ds_one))
    own_terms(blk, tile, hdim, 2, blk, q_t, k_t, probs, *by_block, d_qkv)
    dn = mm(w_qkv[...], d_qkv[...])
    for b in range(1, blk):
        here, place = cols(b + 1, tile=tile), cols(b - 1, tile=tile)
        out = norm_grad(dn[:, place], xn_t[:, here], inv[0:1, here])
        if b < blk - 1:
            mid[:, place] = (g_mid[:, place].astype(F32) + out).astype(BF16)
        else:
            one[...] = (g_one[...].astype(F32) + out).astype(BF16)


def add_rim_kernel(one, rim, out):
    out[...] = add(one, rim)


def last_terms_kernel(
    blk, tile, chips, after, g_prev, arrived, g_zero, g_mid, da_zero, da_mid, ds_zero, ds_mid, w_out, v_nat, k_t,
    q_t, probs, attn_t, xn_t, d_low, g_one, d_high, *refs
):
    *give, da_one, ds_one = refs
    width = g_prev.shape[0]
    hdim = width // HEADS
    g_one[...] = add(g_prev, arrived)
    end_grads(blk - 1, tile, hdim, g_one, w_out, v_nat, probs, attn_t, da_one, ds_one)
    d_high[:width, cols(blk - 1, tile=tile)] = jnp.zeros((width, tile), BF16)
    by_block = joined(blk, tile, (da_zero, da_mid, da_one), (ds_zero, ds_mid, ds_one))
    own_terms(blk, tile, hdim, 2, blk + 1, q_t, k_t, probs, *by_block, d_high)
    if give:
        core = 1 - lax.rem(lax.axis_index("dom"), 2)
        part = weight_rows(core, chips, xn_t, (d_low, d_high), attn_t, (g_zero, g_mid, g_one))
        rows = width // (2 * chips)
        for z in range(chips):
            here = slice(z * rows, (z + 1) * rows)
            for across, term in part:
                give[0][z, :, across] = term[here].astype(BF16)


def last_input_kernel(
    blk, tile, after, g_zero, g_mid, g_one, d_low, d_high, w_qkv, xn_t, inv, y, c_off
):
    outs = []
    for part in (d_low[:, tile:], d_high[...]):
        dn = mm(w_qkv[...], part)
        for n in range(part.shape[1] // tile):
            here = cols(len(outs) + 1, tile=tile)
            outs.append(norm_grad(dn[:, cols(n, tile=tile)], xn_t[:, here], inv[0:1, here]))
    c_off[...] = outs[-1].astype(BF16)
    for b in range(blk):
        own = cols(b, tile=tile)
        g = g_zero[...] if b == 0 else g_mid[:, cols(b - 1, tile=tile)] if b < blk - 1 else g_one[...]
        y[:, own] = (g.astype(F32) + outs[b]).astype(BF16)


def finish_input_kernel(blk, tile, y_t, on, off, out):
    for b in range(blk):
        part = y_t[:, cols(b, tile=tile)].astype(F32)
        if b == 0:
            part = part + on[...].astype(F32)
        if b == blk - 1:
            part = part + off[...].astype(F32)
        out[rows_of(b, blk, tile), :] = part.T.astype(BF16)


def weight_rows(core, chips, xn_t, d_qkv, attn_t, g):
    def picked(ref):
        rows = ref.shape[0] // (2 * chips)
        starts = [pl.multiple_of((2 * z + core) * rows, rows) for z in range(chips)]
        return jnp.concatenate([ref[pl.ds(s, rows), :] for s in starts], axis=0)

    def product(ref, parts):
        left, start, total = picked(ref), 0, None
        for part in parts:
            more = mm(left[:, start : start + part.shape[1]], part[...], NT)
            total = more if total is None else total + more
            start += part.shape[1]
        return total

    wide, width = d_qkv[0].shape[0], g[0].shape[0]
    return (
        (slice(0, wide), product(xn_t, d_qkv)),
        (slice(wide, wide + width), product(attn_t, g)),
    )


def mine_kernel(chips, xn_t, d_low, d_high, attn_t, g_zero, g_mid, g_one, both):
    core = lax.rem(lax.axis_index("dom"), 2)
    rows = both.shape[1]
    for across, term in weight_rows(core, chips, xn_t, (d_low, d_high), attn_t, (g_zero, g_mid, g_one)):
        for z in range(chips):
            both[z, :, across] = term[z * rows : (z + 1) * rows]


def keep_kernel(chips, steps, got, both, *outs):
    chip = lax.axis_index("dom") // 2
    half = got.shape[2] // 2
    for n, (first, second) in enumerate(steps):
        give, own = outs[2 * n : 2 * n + 2]
        across = slice(n * half, (n + 1) * half)

        def total(distance):
            z = lax.bitwise_xor(chip, distance)
            return both[z, :, across] + got[z, :, across].astype(F32)

        give[0] = total(first).astype(BF16)
        give[1] = total(first ^ second).astype(BF16)
        own[0] = total(0)
        own[1] = total(second)


def middle_kernel(own_a, got_a, own_b, got_b, *refs):
    give_a, rest_a, give_b, rest_b = refs[-4:]
    for own, got, give, rest in ((own_b, got_b, give_b, rest_b), (own_a, got_a, give_a, rest_a)):
        rest[...] = own[0] + got[0].astype(F32)
        give[...] = (own[1] + got[1].astype(F32)).astype(BF16)


def total_kernel(rest_a, got_a, rest_b, got_b, qkv_grad, out_grad):
    width = out_grad.shape[1]
    qkv_grad[:, : 2 * width] = rest_a[...] + got_a[...].astype(F32)
    total = rest_b[...] + got_b[...].astype(F32)
    qkv_grad[:, 2 * width :] = total[:, :width]
    out_grad[...] = total[:, width:]


def other_core(parts):
    return [(i, i ^ 1) for i in range(parts)]


def next_chip(parts):
    return [(i, (i + 1 if i % 2 else i - 1) % parts) for i in range(parts)]


def chips_apart(parts, step):
    return [(i, i ^ (2 * step)) for i in range(parts)]


def local(layer_inputs, top_grad, w_qkv, w_out, neighbours):
    sections = lax.axis_size("section")
    parts = lax.axis_size("dom")
    blk = neighbours.shape[0]
    rows, width = top_grad.shape[1:]
    tile = rows // blk
    ext = rows + 2 * tile
    hdim = width // HEADS
    scale = 1.0 / hdim**0.5
    x = layer_inputs[0, 0]
    w_in, w_back = w_qkv[0], w_out[0]
    whole, middle, single = ((width, n) for n in (rows, rows - 2 * tile, tile))
    pairs = HEADS // 2
    pair_shape = (3 * tile, 2 * tile)
    x_on, x_off = call(
        functools.partial(pick_kernel, blk, tile), "pick", [((tile, width), BF16)] * 2, [x]
    )
    x_on = lax.ppermute(x_on, "dom", other_core(parts))
    x_off = lax.ppermute(x_off, "dom", next_chip(parts))
    *kept, q_t = call(
        functools.partial(prelude_own_kernel, blk, tile, scale), "prelude_own",
        [
            (whole, BF16), ((8, rows), F32), ((rows, width), BF16), ((rows, width), BF16),
            (whole, BF16), (whole, BF16), (whole, BF16),
        ],
        [x, w_in],
    )
    xn_t, inv, v_nat, k_t, probs, attn_t, g_zero, g_mid, g_one = call(
        functools.partial(prelude_kernel, blk, tile, scale), "prelude",
        [
            ((width, ext), BF16), ((8, ext), F32), ((ext, width), BF16), ((width, ext), BF16),
            ((pairs, blk, *pair_shape), BF16), (whole, BF16), (single, BF16), (middle, BF16),
            (single, BF16),
        ],
        [neighbours, x_on, x_off, w_in, *kept, q_t, top_grad[0]],
        scratch=[
            ((ext, width), BF16), ((width, ext), BF16), ((pairs, blk, *pair_shape), F32),
        ],
        smem=1,
    )
    common = [w_back, v_nat, probs, attn_t]
    for_rim = [w_in, xn_t, inv, q_t]
    others = (width, rows - 2 * tile)
    rim_scratch = [((2 * width, tile), BF16)]
    zero_shape = [(single, BF16), ((pairs, *pair_shape), BF16)]
    mid_shape = [(middle, BF16), ((pairs, blk - 2, *pair_shape), BF16)]
    received = []
    for k in range(sections - 1):
        here = sections - 1 - k
        moved = k > 0
        *new, da_zero, ds_zero, c_on = call(
            functools.partial(stage_zero_kernel, blk, tile, moved), "stage_zero",
            [(single, BF16)] * moved + zero_shape + [(single, BF16)],
            [g_zero, *received[:1], *common, *for_rim], scratch=rim_scratch,
        )
        g_zero = new[0] if moved else g_zero
        on = lax.ppermute(c_on, "dom", other_core(parts))
        *new, da_mid, ds_mid, zero = call(
            functools.partial(stage_mid_kernel, blk, tile, moved), "stage_mid",
            [(middle, BF16)] * moved + mid_shape + [(single, BF16)],
            [g_mid, *received[1:2], g_zero, da_zero, ds_zero, *common, *for_rim, k_t],
            scratch=[((3 * width, tile), BF16)],
        )
        g_mid = new[0] if moved else g_mid
        zero = call(add_rim_kernel, "add_on", [(single, BF16)], [zero, on])[0]
        *new, da_one, c_off = call(
            functools.partial(stage_one_kernel, blk, tile, moved), "stage_one",
            [(single, BF16)] * (moved + 2),
            [g_one, *received[2:], *common, *for_rim], scratch=rim_scratch,
        )
        g_one = new[0] if moved else g_one
        off = lax.ppermute(c_off, "dom", next_chip(parts))
        mid, one = call(
            functools.partial(stage_main_kernel, blk, tile), "stage_main",
            [(middle, BF16), (single, BF16)],
            [
                g_mid, g_one, da_zero, da_mid, da_one, ds_zero, ds_mid, w_in, xn_t, inv, v_nat, k_t, q_t,
                probs, attn_t,
            ],
            scratch=[((pairs, *pair_shape), BF16), ((3 * width, rows - tile), BF16)],
        )
        one = call(add_rim_kernel, "add_off", [(single, BF16)], [one, off])[0]
        received = [lax.ppermute(part, "section", [(here, here - 1)]) for part in (zero, mid, one)]
    direct = parts == 8
    chips = parts // 2
    every = 4 * width
    row = width // parts
    g_zero, da_zero, ds_zero, c_on = call(
        functools.partial(stage_zero_kernel, blk, tile, True), "last_zero",
        [(single, BF16)] + zero_shape + [(single, BF16)],
        [g_zero, received[0], *common, *for_rim], scratch=rim_scratch,
    )
    on = lax.ppermute(c_on, "dom", other_core(parts))
    g_mid, da_mid, ds_mid, d_low = call(
        functools.partial(last_mid_kernel, blk, tile), "last_mid",
        [(middle, BF16)] + mid_shape + [((3 * width, 2 * tile), BF16)],
        [g_mid, received[1], da_zero, ds_zero, *common, q_t, k_t],
    )
    g_one, d_high, *give = call(
        functools.partial(last_terms_kernel, blk, tile, chips), "last_terms",
        [(single, BF16), ((3 * width, rows), BF16)] + [((chips, row, every), BF16)] * direct,
        [
            on, g_one, received[2], g_zero, g_mid, da_zero, da_mid, ds_zero, ds_mid, w_back, v_nat, k_t, q_t,
            probs, attn_t, xn_t, d_low,
        ],
        scratch=[(single, BF16), ((pairs, *pair_shape), BF16)],
    )
    after = d_high
    if direct:
        got = lax.ppermute(give[0], "dom", other_core(parts))
        steps = ((1, 2), (2, 1))
        mine = call(
            functools.partial(mine_kernel, chips), "mine", [((chips, row, every), F32)],
            [xn_t, d_low, d_high, attn_t, g_zero, g_mid, g_one],
        )[0]
        give_a, own_a, give_b, own_b = call(
            functools.partial(keep_kernel, chips, steps), "keep",
            [((2, row, every // 2), BF16), ((2, row, every // 2), F32)] * 2,
            [got, mine],
        )
        got_a = lax.ppermute(give_a, "dom", chips_apart(parts, steps[0][0]))
        got_b = lax.ppermute(give_b, "dom", chips_apart(parts, steps[1][0]))
        after = own_a
    y, c_off = call(
        functools.partial(last_input_kernel, blk, tile), "last_input",
        [(whole, BF16), (single, BF16)],
        [after, g_zero, g_mid, g_one, d_low, d_high, w_in, xn_t, inv],
    )
    off = lax.ppermute(c_off, "dom", next_chip(parts))
    if direct:
        give_a, rest_a, give_b, rest_b = call(
            middle_kernel, "middle", [((row, every // 2), BF16), ((row, every // 2), F32)] * 2,
            [own_a, got_a, own_b, got_b, c_off],
        )
        got_b = lax.ppermute(give_b, "dom", chips_apart(parts, steps[1][1]))
        got_a = lax.ppermute(give_a, "dom", chips_apart(parts, steps[0][1]))
    y = call(
        functools.partial(finish_input_kernel, blk, tile), "finish_input", [((rows, width), BF16)],
        [y, on, off],
    )[0]
    if direct:
        qkv_grad, out_grad = call(
            total_kernel, "total", [((row, 3 * width), F32), ((row, width), F32)],
            [rest_a, got_a, rest_b, got_b],
        )
    else:
        g_t = jnp.concatenate([g_zero, g_mid, g_one], axis=1)
        d_qkv = jnp.concatenate([d_low, d_high], axis=1)
        term = jnp.concatenate([mm(xn_t, d_qkv, NT), mm(attn_t, g_t, NT)], axis=1)
        total = lax.psum_scatter(term, "dom", scatter_dimension=0, tiled=True)
        qkv_grad, out_grad = total[:, : 3 * width], total[:, 3 * width :]
    return (y[None, None], qkv_grad[None], out_grad[None])


def solution(mesh):
    placed = (
        P("section", None, "dom", None),
        P(None, "dom", None),
        P("section", None, None),
        P("section", None, None),
        P("dom", None),
    )
    return jax.shard_map(
        local,
        mesh=mesh,
        in_specs=placed,
        out_specs=(
            P("section", None, "dom", None),
            P("section", "dom", None),
            P("section", "dom", None),
        ),
        check_vma=False,
    )
```

```python
import functools

import jax
import jax.numpy as jnp
from jax import lax
from jax.experimental import pallas as pl
from jax.experimental.pallas import tpu as pltpu
from jax.sharding import PartitionSpec as P

HEADS = 8
EPS = 1e-05
F32 = jnp.float32
BF16 = jnp.bfloat16
NN = (((1,), (0,)), ((), ()))
NT = (((1,), (1,)), ((), ()))
VMEM_LIMIT = 20 * 1024 * 1024


def mm(a, b, dims=NN):
    return lax.dot_general(a, b, dims, preferred_element_type=F32)


def cols(start, count=1, tile=128):
    return slice(start * tile, (start + count) * tile)


def call(kernel, name, outs, args, scratch=(), smem=0):
    vmem = pl.BlockSpec(memory_space=pltpu.VMEM)
    scalars = pl.BlockSpec(memory_space=pltpu.SMEM)
    return pl.pallas_call(
        kernel,
        in_specs=[scalars] * smem + [vmem] * (len(args) - smem),
        out_specs=[vmem] * len(outs),
        out_shape=[jax.ShapeDtypeStruct(shape, dtype) for shape, dtype in outs],
        scratch_shapes=[pltpu.VMEM(shape, dtype) for shape, dtype in scratch],
        compiler_params=pltpu.CompilerParams(vmem_limit_bytes=VMEM_LIMIT),
        cost_estimate=pl.CostEstimate(flops=1, bytes_accessed=1, transcendentals=0),
        name=name,
    )(*args)


def second_core():
    return lax.rem(lax.axis_index("dom"), 2) == 1


def block_of(b, blk):
    return jnp.where(second_core(), b, blk - 1 - b)


def rows_of(b, blk, tile):
    return pl.ds(pl.multiple_of(block_of(b, blk) * tile, tile), tile)


def halves(pair, hdim):
    zero = jnp.zeros((hdim, pair.shape[1]), pair.dtype)
    return jnp.concatenate(
        [
            jnp.concatenate([pair[:hdim], zero], axis=0),
            jnp.concatenate([zero, pair[hdim:]], axis=0),
        ],
        axis=1,
    )


def normalize(rows):
    xf = rows.astype(F32)
    cent = xf - jnp.mean(xf, axis=-1, keepdims=True)
    rstd = lax.rsqrt(jnp.mean(cent * cent, axis=-1, keepdims=True) + EPS)
    return cent * rstd, rstd


def project_tile(t, tile, scale, rows, w_qkv, xn_t, inv, k_nat, v_nat, k_t, v_t):
    width = rows.shape[1]
    here = cols(t, tile=tile)
    xhat, rstd = normalize(rows)
    xn = xhat.astype(BF16)
    xn_t[:, here] = xhat.T.astype(BF16)
    inv[:, here] = jnp.broadcast_to(rstd, (tile, 128)).T[0:8, :]
    keyval = mm(xn, w_qkv[:, width:])
    k_t[:, here] = (keyval[:, :width].T * scale).astype(BF16)
    v_t[:, here] = keyval[:, width:].T.astype(BF16)
    k_nat[here, :] = keyval[:, :width].astype(BF16)
    v_nat[here, :] = keyval[:, width:].astype(BF16)
    return xn


def pick_kernel(blk, tile, x, x_on, x_off):
    x_on[...] = x[rows_of(0, blk, tile), :]
    x_off[...] = x[rows_of(blk - 1, blk, tile), :]


def prelude_own_kernel(blk, tile, scale, x, w_qkv, xn_t, inv, k_nat, v_nat, k_t, v_t, q_t):
    width = x.shape[1]
    for b in range(blk):
        xn = project_tile(
            b, tile, scale, x[rows_of(b, blk, tile), :], w_qkv, xn_t, inv, k_nat, v_nat, k_t, v_t
        )
        q_t[:, cols(b, tile=tile)] = (mm(xn, w_qkv[:, :width]).T * scale).astype(BF16)


def prelude_kernel(
    blk, tile, scale, neighbours, x_on, x_off, w_qkv,
    xn_own, inv_own, k_own, v_own, kt_own, vt_own, q_t, top,
    xn_t, inv, v_nat, k_t, probs, attn_t, g_zero, g_mid, g_one, k_nat, v_t, scores,
):
    width = x_on.shape[1]
    hdim = width // HEADS
    ours = cols(1, blk, tile)
    xn_t[:, ours] = xn_own[...]
    inv[:, ours] = inv_own[...]
    k_nat[ours, :] = k_own[...]
    v_nat[ours, :] = v_own[...]
    k_t[:, ours] = kt_own[...]
    v_t[:, ours] = vt_own[...]
    is_last = lax.axis_index("section") == lax.axis_size("section") - 1
    for b in range(blk):
        g = jnp.where(is_last, top[rows_of(b, blk, tile), :].astype(F32).T, 0.0).astype(BF16)
        if b == 0:
            g_zero[...] = g
        elif b < blk - 1:
            g_mid[:, cols(b - 1, tile=tile)] = g
        else:
            g_one[...] = g
    for t, rows in ((0, x_on), (blk + 1, x_off)):
        project_tile(t, tile, scale, rows[...], w_qkv, xn_t, inv, k_nat, v_nat, k_t, v_t)
    blocks = blk * lax.axis_size("dom")
    second = second_core()
    for b in range(blk):
        place = block_of(b, blk)
        mine = lax.axis_index("dom") * blk + place
        below, above = lax.rem(mine + blocks - 1, blocks), lax.rem(mine + 1, blocks)
        before, after = jnp.where(second, below, above), jnp.where(second, above, below)
        has_before = has_after = False
        for j in range(1, neighbours.shape[1]):
            has_before |= neighbours[place, j] == before
            has_after |= neighbours[place, j] == after
        for i in range(HEADS // 2):
            lanes = cols(i, tile=2 * hdim)
            q = halves(q_t[lanes, cols(b, tile=tile)], hdim)
            s = mm(k_nat[cols(b, 3, tile), lanes], q)
            scores[i, b] = jnp.concatenate(
                [
                    jnp.where(has_before, s[:tile], -1e30),
                    s[tile : 2 * tile],
                    jnp.where(has_after, s[2 * tile :], -1e30),
                ],
                axis=0,
            )
    for b in range(blk):
        for i in range(HEADS // 2):
            s = scores[i, b]
            e = jnp.exp(s - jnp.max(s, axis=0, keepdims=True))
            probs[i, b] = (e * (1.0 / jnp.sum(e, axis=0, keepdims=True))).astype(BF16)
    for b in range(blk):
        for h in range(HEADS):
            head = cols(h, tile=hdim)
            p = probs[h // 2, b, :, cols(h % 2, tile=tile)]
            attn_t[head, cols(b, tile=tile)] = mm(v_t[head, cols(b, 3, tile)], p).astype(BF16)


def score_grad(i, b, first, count, tile, hdim, v_nat, probs, attn_t, da):
    lanes, own = cols(i, tile=2 * hdim), cols(b, tile=tile)
    prod = da.astype(F32) * attn_t[lanes, own].astype(F32)
    total = jnp.concatenate(
        [
            jnp.sum(prod[:hdim], axis=0, keepdims=True),
            jnp.sum(prod[hdim:], axis=0, keepdims=True),
        ],
        axis=1,
    )
    dp = mm(v_nat[cols(b + first, count, tile), lanes], halves(da, hdim))
    return (probs[i, b, cols(first, count, tile), :].astype(F32) * (dp - total)).astype(BF16)


def norm_grad(dn, xn, rstd):
    xhat = xn.astype(F32)
    first = jnp.mean(dn, axis=0, keepdims=True)
    second = jnp.mean(dn * xhat, axis=0, keepdims=True)
    return rstd * (dn - first - xhat * second)


def rim_grad(b, t, tile, hdim, q_t, probs, da, ds, w_qkv, xn_t, inv, d_rim):
    width = q_t.shape[0]
    own, near, here = cols(b, tile=tile), cols(t - b, tile=tile), cols(t, tile=tile)
    for i in range(HEADS // 2):
        lanes = cols(i, tile=2 * hdim)
        after = slice(width + i * 2 * hdim, width + (i + 1) * 2 * hdim)
        d_rim[lanes, :] = mm(halves(q_t[lanes, own], hdim), ds(i), NT).astype(BF16)
        d_rim[after, :] = mm(halves(da(lanes), hdim), probs[i, b, near, :], NT).astype(BF16)
    dn = mm(w_qkv[:, width:], d_rim[...])
    return norm_grad(dn, xn_t[:, here], inv[0:1, here]).astype(BF16)


def add(a, b):
    return (a[...].astype(F32) + b[...].astype(F32)).astype(BF16)


def joined(blk, tile, das, dss):
    def da(lanes, b):
        if b == 0:
            return das[0][lanes, :]
        return das[1][lanes, cols(b - 1, tile=tile)] if b < blk - 1 else das[2][lanes, :]

    def ds(i, b, near, across):
        if b == 0:
            return dss[0][i, near, across]
        return dss[1][i, b - 1, near, across] if b < blk - 1 else dss[2][i, near, across]

    return da, ds


def end_grads(b, tile, hdim, g, w_out, v_nat, probs, attn_t, da, ds):
    da[...] = mm(w_out[...], g[...]).astype(BF16)
    for i in range(HEADS // 2):
        part = da[cols(i, tile=2 * hdim), :]
        ds[i] = score_grad(i, b, 0, 3, tile, hdim, v_nat, probs, attn_t, part)


def mid_grads(blk, tile, hdim, g, w_out, v_nat, probs, attn_t, da, ds):
    da[...] = mm(w_out[...], g[...]).astype(BF16)
    for b in range(1, blk - 1):
        for i in range(HEADS // 2):
            part = da[cols(i, tile=2 * hdim), cols(b - 1, tile=tile)]
            ds[i, b - 1] = score_grad(i, b, 0, 3, tile, hdim, v_nat, probs, attn_t, part)


def own_terms(blk, tile, hdim, first, last, q_t, k_t, probs, da, ds, d_qkv):
    width = q_t.shape[0]
    for i in range(HEADS // 2):
        lanes = cols(i, tile=2 * hdim)
        for n, left, right in (
            (1, lambda b: q_t[lanes, cols(b, tile=tile)], lambda b, near: ds(i, b, near, slice(None))),
            (2, lambda b: da(lanes, b), lambda b, near: probs[i, b, near, :]),
        ):
            total = [None] * (blk + 2)
            for b in range(max(first - 2, 0), min(last + 1, blk)):
                low, high = max(b, first), min(b + 3, last + 1)
                near = slice((low - b) * tile, (high - b) * tile)
                part = mm(halves(left(b), hdim), right(b, near), NT)
                for t in range(low, high):
                    more = part[:, cols(t - low, tile=tile)]
                    total[t] = more if total[t] is None else total[t] + more
            start = n * width + i * 2 * hdim
            for t in range(first, last + 1):
                d_qkv[start : start + 2 * hdim, cols(t - first, tile=tile)] = total[t].astype(BF16)
        for b in range(max(first - 1, 0), min(last, blk)):
            for h in (2 * i, 2 * i + 1):
                head = cols(h, tile=hdim)
                d_qkv[head, cols(b + 1 - first, tile=tile)] = mm(
                    k_t[head, cols(b, 3, tile)],
                    ds(i, b, slice(None), cols(h % 2, tile=tile)),
                ).astype(BF16)


def stage_zero_kernel(blk, tile, moved, *refs):
    if moved:
        g_prev, arrived, *refs = refs
    else:
        g, *refs = refs
    w_out, v_nat, probs, attn_t, w_qkv, xn_t, inv, q_t, *refs = refs
    if moved:
        g, *refs = refs
        g[...] = add(g_prev, arrived)
    da, ds, c_on, d_rim = refs
    hdim = g.shape[0] // HEADS
    end_grads(0, tile, hdim, g, w_out, v_nat, probs, attn_t, da, ds)
    c_on[...] = rim_grad(
        0, 0, tile, hdim, q_t, probs, lambda lanes: da[lanes, :], lambda i: ds[i, :tile, :],
        w_qkv, xn_t, inv, d_rim,
    )


def stage_mid_kernel(blk, tile, moved, *refs):
    if moved:
        g_prev, arrived, *refs = refs
    else:
        g, *refs = refs
    g_zero, da_zero, ds_zero, w_out, v_nat, probs, attn_t, w_qkv, xn_t, inv, q_t, k_t, *refs = refs
    if moved:
        g, *refs = refs
        g[...] = add(g_prev, arrived)
    da, ds, y, d_first = refs
    hdim = g.shape[0] // HEADS
    mid_grads(blk, tile, hdim, g, w_out, v_nat, probs, attn_t, da, ds)
    by_block = joined(blk, tile, (da_zero, da), (ds_zero, ds))
    own_terms(blk, tile, hdim, 1, 1, q_t, k_t, probs, *by_block, d_first)
    dn = mm(w_qkv[...], d_first[...])
    here = cols(1, tile=tile)
    y[...] = (g_zero[...].astype(F32) + norm_grad(dn, xn_t[:, here], inv[0:1, here])).astype(BF16)


def last_mid_kernel(
    blk, tile, g_prev, arrived, da_zero, ds_zero, w_out, v_nat, probs, attn_t, q_t, k_t, g, da, ds, d_low
):
    g[...] = add(g_prev, arrived)
    width = g.shape[0]
    hdim = width // HEADS
    mid_grads(blk, tile, hdim, g, w_out, v_nat, probs, attn_t, da, ds)
    d_low[:width, :tile] = jnp.zeros((width, tile), BF16)
    by_block = joined(blk, tile, (da_zero, da), (ds_zero, ds))
    own_terms(blk, tile, hdim, 0, 1, q_t, k_t, probs, *by_block, d_low)


def stage_one_kernel(blk, tile, moved, *refs):
    if moved:
        g_prev, arrived, *refs = refs
    else:
        g, *refs = refs
    w_out, v_nat, probs, attn_t, w_qkv, xn_t, inv, q_t, *refs = refs
    if moved:
        g, *refs = refs
        g[...] = add(g_prev, arrived)
    da, c_off, d_rim = refs
    hdim = g.shape[0] // HEADS
    da[...] = mm(w_out[...], g[...]).astype(BF16)
    b = blk - 1
    ds = [
        score_grad(i, b, 2, 1, tile, hdim, v_nat, probs, attn_t, da[cols(i, tile=2 * hdim), :])
        for i in range(HEADS // 2)
    ]
    c_off[...] = rim_grad(
        b, blk + 1, tile, hdim, q_t, probs, lambda lanes: da[lanes, :], lambda i: ds[i],
        w_qkv, xn_t, inv, d_rim,
    )


def stage_start_kernel(
    blk, tile, g_zero, g_mid, g_one, w_out, v_nat, probs, attn_t, w_qkv, xn_t, inv, q_t, k_t,
    da_zero, ds_zero, c_on, da_one, c_off, da_mid, ds_mid, zero, d_rim, d_rim_too, d_first,
):
    common = (w_out, v_nat, probs, attn_t, w_qkv, xn_t, inv, q_t)
    stage_zero_kernel(blk, tile, False, g_zero, *common, da_zero, ds_zero, c_on, d_rim)
    stage_one_kernel(blk, tile, False, g_one, *common, da_one, c_off, d_rim_too)
    stage_mid_kernel(
        blk, tile, False, g_mid, g_zero, da_zero, ds_zero, *common, k_t, da_mid, ds_mid, zero, d_first
    )


def stage_main_kernel(
    blk, tile, g_mid, g_one, da_zero, da_mid, da_one, ds_zero, ds_mid, w_qkv, xn_t, inv, v_nat, k_t, q_t,
    probs, attn_t, mid, one, ds_one, d_qkv,
):
    hdim = g_mid.shape[0] // HEADS
    for i in range(HEADS // 2):
        part = da_one[cols(i, tile=2 * hdim), :]
        ds_one[i] = score_grad(i, blk - 1, 0, 3, tile, hdim, v_nat, probs, attn_t, part)
    by_block = joined(blk, tile, (da_zero, da_mid, da_one), (ds_zero, ds_mid, ds_one))
    own_terms(blk, tile, hdim, 2, blk, q_t, k_t, probs, *by_block, d_qkv)
    dn = mm(w_qkv[...], d_qkv[...])
    for b in range(1, blk):
        here, place = cols(b + 1, tile=tile), cols(b - 1, tile=tile)
        out = norm_grad(dn[:, place], xn_t[:, here], inv[0:1, here])
        if b < blk - 1:
            mid[:, place] = (g_mid[:, place].astype(F32) + out).astype(BF16)
        else:
            one[...] = (g_one[...].astype(F32) + out).astype(BF16)


def add_rim_kernel(one, rim, out):
    out[...] = add(one, rim)


def last_terms_kernel(
    blk, tile, chips, after, g_prev, arrived, g_zero, g_mid, da_zero, da_mid, ds_zero, ds_mid, w_out, v_nat, k_t,
    q_t, probs, attn_t, xn_t, d_low, g_one, d_high, *refs
):
    *give, da_one, ds_one = refs
    width = g_prev.shape[0]
    hdim = width // HEADS
    g_one[...] = add(g_prev, arrived)
    end_grads(blk - 1, tile, hdim, g_one, w_out, v_nat, probs, attn_t, da_one, ds_one)
    d_high[:width, cols(blk - 1, tile=tile)] = jnp.zeros((width, tile), BF16)
    by_block = joined(blk, tile, (da_zero, da_mid, da_one), (ds_zero, ds_mid, ds_one))
    own_terms(blk, tile, hdim, 2, blk + 1, q_t, k_t, probs, *by_block, d_high)
    if give:
        core = 1 - lax.rem(lax.axis_index("dom"), 2)
        part = weight_rows(core, chips, xn_t, (d_low, d_high), attn_t, (g_zero, g_mid, g_one))
        rows = width // (2 * chips)
        for z in range(chips):
            here = slice(z * rows, (z + 1) * rows)
            for across, term in part:
                give[0][z, :, across] = term[here].astype(BF16)


def last_input_kernel(
    blk, tile, after, g_zero, g_mid, g_one, d_low, d_high, w_qkv, xn_t, inv, y, c_off
):
    outs = []
    for part in (d_low[:, tile:], d_high[...]):
        dn = mm(w_qkv[...], part)
        for n in range(part.shape[1] // tile):
            here = cols(len(outs) + 1, tile=tile)
            outs.append(norm_grad(dn[:, cols(n, tile=tile)], xn_t[:, here], inv[0:1, here]))
    c_off[...] = outs[-1].astype(BF16)
    for b in range(blk):
        own = cols(b, tile=tile)
        g = g_zero[...] if b == 0 else g_mid[:, cols(b - 1, tile=tile)] if b < blk - 1 else g_one[...]
        y[:, own] = (g.astype(F32) + outs[b]).astype(BF16)


def finish_input_kernel(blk, tile, y_t, on, off, out):
    for b in range(blk):
        part = y_t[:, cols(b, tile=tile)].astype(F32)
        if b == 0:
            part = part + on[...].astype(F32)
        if b == blk - 1:
            part = part + off[...].astype(F32)
        out[rows_of(b, blk, tile), :] = part.T.astype(BF16)


def weight_rows(core, chips, xn_t, d_qkv, attn_t, g):
    def picked(ref):
        rows = ref.shape[0] // (2 * chips)
        starts = [pl.multiple_of((2 * z + core) * rows, rows) for z in range(chips)]
        return jnp.concatenate([ref[pl.ds(s, rows), :] for s in starts], axis=0)

    def product(ref, parts):
        left, start, total = picked(ref), 0, None
        for part in parts:
            more = mm(left[:, start : start + part.shape[1]], part[...], NT)
            total = more if total is None else total + more
            start += part.shape[1]
        return total

    wide, width = d_qkv[0].shape[0], g[0].shape[0]
    return (
        (slice(0, wide), product(xn_t, d_qkv)),
        (slice(wide, wide + width), product(attn_t, g)),
    )


def mine_kernel(chips, xn_t, d_low, d_high, attn_t, g_zero, g_mid, g_one, both):
    core = lax.rem(lax.axis_index("dom"), 2)
    rows = both.shape[1]
    for across, term in weight_rows(core, chips, xn_t, (d_low, d_high), attn_t, (g_zero, g_mid, g_one)):
        for z in range(chips):
            both[z, :, across] = term[z * rows : (z + 1) * rows]


def keep_kernel(chips, steps, got, both, *outs):
    chip = lax.axis_index("dom") // 2
    half = got.shape[2] // 2
    for n, (first, second) in enumerate(steps):
        give, own = outs[2 * n : 2 * n + 2]
        across = slice(n * half, (n + 1) * half)

        def total(distance):
            z = lax.bitwise_xor(chip, distance)
            return both[z, :, across] + got[z, :, across].astype(F32)

        give[0] = total(first).astype(BF16)
        give[1] = total(first ^ second).astype(BF16)
        own[0] = total(0)
        own[1] = total(second)


def middle_kernel(own_a, got_a, own_b, got_b, *refs):
    give_a, rest_a, give_b, rest_b = refs[-4:]
    for own, got, give, rest in ((own_b, got_b, give_b, rest_b), (own_a, got_a, give_a, rest_a)):
        rest[...] = own[0] + got[0].astype(F32)
        give[...] = (own[1] + got[1].astype(F32)).astype(BF16)


def total_kernel(rest_a, got_a, rest_b, got_b, qkv_grad, out_grad):
    width = out_grad.shape[1]
    qkv_grad[:, : 2 * width] = rest_a[...] + got_a[...].astype(F32)
    total = rest_b[...] + got_b[...].astype(F32)
    qkv_grad[:, 2 * width :] = total[:, :width]
    out_grad[...] = total[:, width:]


def other_core(parts):
    return [(i, i ^ 1) for i in range(parts)]


def next_chip(parts):
    return [(i, (i + 1 if i % 2 else i - 1) % parts) for i in range(parts)]


def chips_apart(parts, step):
    return [(i, i ^ (2 * step)) for i in range(parts)]


def local(layer_inputs, top_grad, w_qkv, w_out, neighbours):
    sections = lax.axis_size("section")
    parts = lax.axis_size("dom")
    blk = neighbours.shape[0]
    rows, width = top_grad.shape[1:]
    tile = rows // blk
    ext = rows + 2 * tile
    hdim = width // HEADS
    scale = 1.0 / hdim**0.5
    x = layer_inputs[0, 0]
    w_in, w_back = w_qkv[0], w_out[0]
    whole, middle, single = ((width, n) for n in (rows, rows - 2 * tile, tile))
    pairs = HEADS // 2
    pair_shape = (3 * tile, 2 * tile)
    x_on, x_off = call(
        functools.partial(pick_kernel, blk, tile), "pick", [((tile, width), BF16)] * 2, [x]
    )
    x_on = lax.ppermute(x_on, "dom", other_core(parts))
    x_off = lax.ppermute(x_off, "dom", next_chip(parts))
    *kept, q_t = call(
        functools.partial(prelude_own_kernel, blk, tile, scale), "prelude_own",
        [
            (whole, BF16), ((8, rows), F32), ((rows, width), BF16), ((rows, width), BF16),
            (whole, BF16), (whole, BF16), (whole, BF16),
        ],
        [x, w_in],
    )
    xn_t, inv, v_nat, k_t, probs, attn_t, g_zero, g_mid, g_one = call(
        functools.partial(prelude_kernel, blk, tile, scale), "prelude",
        [
            ((width, ext), BF16), ((8, ext), F32), ((ext, width), BF16), ((width, ext), BF16),
            ((pairs, blk, *pair_shape), BF16), (whole, BF16), (single, BF16), (middle, BF16),
            (single, BF16),
        ],
        [neighbours, x_on, x_off, w_in, *kept, q_t, top_grad[0]],
        scratch=[
            ((ext, width), BF16), ((width, ext), BF16), ((pairs, blk, *pair_shape), F32),
        ],
        smem=1,
    )
    common = [w_back, v_nat, probs, attn_t]
    for_rim = [w_in, xn_t, inv, q_t]
    others = (width, rows - 2 * tile)
    rim_scratch = [((2 * width, tile), BF16)]
    zero_shape = [(single, BF16), ((pairs, *pair_shape), BF16)]
    mid_shape = [(middle, BF16), ((pairs, blk - 2, *pair_shape), BF16)]
    received = []
    for k in range(sections - 1):
        here = sections - 1 - k
        if k == 0:
            da_zero, ds_zero, c_on, da_one, c_off, da_mid, ds_mid, zero = call(
                functools.partial(stage_start_kernel, blk, tile), "stage_start",
                zero_shape + [(single, BF16)] * 3 + mid_shape + [(single, BF16)],
                [g_zero, g_mid, g_one, *common, *for_rim, k_t],
                scratch=rim_scratch * 2 + [((3 * width, tile), BF16)],
            )
            on = lax.ppermute(c_on, "dom", other_core(parts))
        else:
            g_zero, da_zero, ds_zero, c_on = call(
                functools.partial(stage_zero_kernel, blk, tile, True), "stage_zero",
                [(single, BF16)]  + zero_shape + [(single, BF16)],
                [g_zero, received[0], *common, *for_rim], scratch=rim_scratch,
            )
            on = lax.ppermute(c_on, "dom", other_core(parts))
            g_mid, da_mid, ds_mid, zero = call(
                functools.partial(stage_mid_kernel, blk, tile, True), "stage_mid",
                [(middle, BF16)]  + mid_shape + [(single, BF16)],
                [g_mid, received[1], g_zero, da_zero, ds_zero, *common, *for_rim, k_t],
                scratch=[((3 * width, tile), BF16)],
            )
            g_one, da_one, c_off = call(
                functools.partial(stage_one_kernel, blk, tile, True), "stage_one",
                [(single, BF16)] * 3,
                [g_one, received[2], *common, *for_rim], scratch=rim_scratch,
            )
        zero = call(add_rim_kernel, "add_on", [(single, BF16)], [zero, on])[0]
        off = lax.ppermute(c_off, "dom", next_chip(parts))
        mid, one = call(
            functools.partial(stage_main_kernel, blk, tile), "stage_main",
            [(middle, BF16), (single, BF16)],
            [
                g_mid, g_one, da_zero, da_mid, da_one, ds_zero, ds_mid, w_in, xn_t, inv, v_nat, k_t, q_t,
                probs, attn_t,
            ],
            scratch=[((pairs, *pair_shape), BF16), ((3 * width, rows - tile), BF16)],
        )
        one = call(add_rim_kernel, "add_off", [(single, BF16)], [one, off])[0]
        received = [lax.ppermute(part, "section", [(here, here - 1)]) for part in (zero, mid, one)]
    direct = parts == 8
    chips = parts // 2
    every = 4 * width
    row = width // parts
    g_zero, da_zero, ds_zero, c_on = call(
        functools.partial(stage_zero_kernel, blk, tile, True), "last_zero",
        [(single, BF16)] + zero_shape + [(single, BF16)],
        [g_zero, received[0], *common, *for_rim], scratch=rim_scratch,
    )
    on = lax.ppermute(c_on, "dom", other_core(parts))
    g_mid, da_mid, ds_mid, d_low = call(
        functools.partial(last_mid_kernel, blk, tile), "last_mid",
        [(middle, BF16)] + mid_shape + [((3 * width, 2 * tile), BF16)],
        [g_mid, received[1], da_zero, ds_zero, *common, q_t, k_t],
    )
    g_one, d_high, *give = call(
        functools.partial(last_terms_kernel, blk, tile, chips), "last_terms",
        [(single, BF16), ((3 * width, rows), BF16)] + [((chips, row, every), BF16)] * direct,
        [
            on, g_one, received[2], g_zero, g_mid, da_zero, da_mid, ds_zero, ds_mid, w_back, v_nat, k_t, q_t,
            probs, attn_t, xn_t, d_low,
        ],
        scratch=[(single, BF16), ((pairs, *pair_shape), BF16)],
    )
    after = d_high
    if direct:
        got = lax.ppermute(give[0], "dom", other_core(parts))
        steps = ((1, 2), (2, 1))
        mine = call(
            functools.partial(mine_kernel, chips), "mine", [((chips, row, every), F32)],
            [xn_t, d_low, d_high, attn_t, g_zero, g_mid, g_one],
        )[0]
        give_a, own_a, give_b, own_b = call(
            functools.partial(keep_kernel, chips, steps), "keep",
            [((2, row, every // 2), BF16), ((2, row, every // 2), F32)] * 2,
            [got, mine],
        )
        got_a = lax.ppermute(give_a, "dom", chips_apart(parts, steps[0][0]))
        got_b = lax.ppermute(give_b, "dom", chips_apart(parts, steps[1][0]))
        after = own_a
    y, c_off = call(
        functools.partial(last_input_kernel, blk, tile), "last_input",
        [(whole, BF16), (single, BF16)],
        [after, g_zero, g_mid, g_one, d_low, d_high, w_in, xn_t, inv],
    )
    off = lax.ppermute(c_off, "dom", next_chip(parts))
    if direct:
        give_a, rest_a, give_b, rest_b = call(
            middle_kernel, "middle", [((row, every // 2), BF16), ((row, every // 2), F32)] * 2,
            [own_a, got_a, own_b, got_b, c_off],
        )
        got_b = lax.ppermute(give_b, "dom", chips_apart(parts, steps[1][1]))
        got_a = lax.ppermute(give_a, "dom", chips_apart(parts, steps[0][1]))
    y = call(
        functools.partial(finish_input_kernel, blk, tile), "finish_input", [((rows, width), BF16)],
        [y, on, off],
    )[0]
    if direct:
        qkv_grad, out_grad = call(
            total_kernel, "total", [((row, 3 * width), F32), ((row, width), F32)],
            [rest_a, got_a, rest_b, got_b],
        )
    else:
        g_t = jnp.concatenate([g_zero, g_mid, g_one], axis=1)
        d_qkv = jnp.concatenate([d_low, d_high], axis=1)
        term = jnp.concatenate([mm(xn_t, d_qkv, NT), mm(attn_t, g_t, NT)], axis=1)
        total = lax.psum_scatter(term, "dom", scatter_dimension=0, tiled=True)
        qkv_grad, out_grad = total[:, : 3 * width], total[:, 3 * width :]
    return (y[None, None], qkv_grad[None], out_grad[None])


def solution(mesh):
    placed = (
        P("section", None, "dom", None),
        P(None, "dom", None),
        P("section", None, None),
        P("section", None, None),
        P("dom", None),
    )
    return jax.shard_map(
        local,
        mesh=mesh,
        in_specs=placed,
        out_specs=(
            P("section", None, "dom", None),
            P("section", "dom", None),
            P("section", "dom", None),
        ),
        check_vma=False,
    )
```

```python
import functools

import jax
import jax.numpy as jnp
from jax import lax
from jax.experimental import pallas as pl
from jax.experimental.pallas import tpu as pltpu
from jax.sharding import PartitionSpec as P

HEADS = 8
EPS = 1e-05
F32 = jnp.float32
BF16 = jnp.bfloat16
NN = (((1,), (0,)), ((), ()))
NT = (((1,), (1,)), ((), ()))
VMEM_LIMIT = 20 * 1024 * 1024


def mm(a, b, dims=NN):
    return lax.dot_general(a, b, dims, preferred_element_type=F32)


def cols(start, count=1, tile=128):
    return slice(start * tile, (start + count) * tile)


def call(kernel, name, outs, args, scratch=(), smem=0):
    vmem = pl.BlockSpec(memory_space=pltpu.VMEM)
    scalars = pl.BlockSpec(memory_space=pltpu.SMEM)
    return pl.pallas_call(
        kernel,
        in_specs=[scalars] * smem + [vmem] * (len(args) - smem),
        out_specs=[vmem] * len(outs),
        out_shape=[jax.ShapeDtypeStruct(shape, dtype) for shape, dtype in outs],
        scratch_shapes=[pltpu.VMEM(shape, dtype) for shape, dtype in scratch],
        compiler_params=pltpu.CompilerParams(vmem_limit_bytes=VMEM_LIMIT),
        cost_estimate=pl.CostEstimate(flops=1, bytes_accessed=1, transcendentals=0),
        name=name,
    )(*args)


def second_core():
    return lax.rem(lax.axis_index("dom"), 2) == 1


def block_of(b, blk):
    return jnp.where(second_core(), b, blk - 1 - b)


def rows_of(b, blk, tile):
    return pl.ds(pl.multiple_of(block_of(b, blk) * tile, tile), tile)


def halves(pair, hdim):
    zero = jnp.zeros((hdim, pair.shape[1]), pair.dtype)
    return jnp.concatenate(
        [
            jnp.concatenate([pair[:hdim], zero], axis=0),
            jnp.concatenate([zero, pair[hdim:]], axis=0),
        ],
        axis=1,
    )


def normalize(rows):
    xf = rows.astype(F32)
    cent = xf - jnp.mean(xf, axis=-1, keepdims=True)
    rstd = lax.rsqrt(jnp.mean(cent * cent, axis=-1, keepdims=True) + EPS)
    return cent * rstd, rstd


def project_tile(t, tile, scale, rows, w_qkv, xn_t, inv, k_nat, v_nat, k_t, v_t):
    width = rows.shape[1]
    here = cols(t, tile=tile)
    xhat, rstd = normalize(rows)
    xn = xhat.astype(BF16)
    xn_t[:, here] = xhat.T.astype(BF16)
    inv[:, here] = jnp.broadcast_to(rstd, (tile, 128)).T[0:8, :]
    keyval = mm(xn, w_qkv[:, width:])
    k_t[:, here] = (keyval[:, :width].T * scale).astype(BF16)
    v_t[:, here] = keyval[:, width:].T.astype(BF16)
    k_nat[here, :] = keyval[:, :width].astype(BF16)
    v_nat[here, :] = keyval[:, width:].astype(BF16)
    return xn


def pick_kernel(blk, tile, x, x_on, x_off):
    x_on[...] = x[rows_of(0, blk, tile), :]
    x_off[...] = x[rows_of(blk - 1, blk, tile), :]


def prelude_own_kernel(blk, tile, scale, x, w_qkv, xn_t, inv, k_nat, v_nat, k_t, v_t, q_t):
    width = x.shape[1]
    for b in range(blk):
        xn = project_tile(
            b, tile, scale, x[rows_of(b, blk, tile), :], w_qkv, xn_t, inv, k_nat, v_nat, k_t, v_t
        )
        q_t[:, cols(b, tile=tile)] = (mm(xn, w_qkv[:, :width]).T * scale).astype(BF16)


def prelude_kernel(
    blk, tile, scale, neighbours, x_on, x_off, w_qkv,
    xn_own, inv_own, k_own, v_own, kt_own, vt_own, q_t, top,
    xn_t, inv, v_nat, k_t, probs, attn_t, g_zero, g_mid, g_one, k_nat, v_t, scores,
):
    width = x_on.shape[1]
    hdim = width // HEADS
    ours = cols(1, blk, tile)
    xn_t[:, ours] = xn_own[...]
    inv[:, ours] = inv_own[...]
    k_nat[ours, :] = k_own[...]
    v_nat[ours, :] = v_own[...]
    k_t[:, ours] = kt_own[...]
    v_t[:, ours] = vt_own[...]
    is_last = lax.axis_index("section") == lax.axis_size("section") - 1
    for b in range(blk):
        g = jnp.where(is_last, top[rows_of(b, blk, tile), :].astype(F32).T, 0.0).astype(BF16)
        if b == 0:
            g_zero[...] = g
        elif b < blk - 1:
            g_mid[:, cols(b - 1, tile=tile)] = g
        else:
            g_one[...] = g
    for t, rows in ((0, x_on), (blk + 1, x_off)):
        project_tile(t, tile, scale, rows[...], w_qkv, xn_t, inv, k_nat, v_nat, k_t, v_t)
    blocks = blk * lax.axis_size("dom")
    second = second_core()
    for b in range(blk):
        place = block_of(b, blk)
        mine = lax.axis_index("dom") * blk + place
        below, above = lax.rem(mine + blocks - 1, blocks), lax.rem(mine + 1, blocks)
        before, after = jnp.where(second, below, above), jnp.where(second, above, below)
        has_before = has_after = False
        for j in range(1, neighbours.shape[1]):
            has_before |= neighbours[place, j] == before
            has_after |= neighbours[place, j] == after
        for i in range(HEADS // 2):
            lanes = cols(i, tile=2 * hdim)
            q = halves(q_t[lanes, cols(b, tile=tile)], hdim)
            s = mm(k_nat[cols(b, 3, tile), lanes], q)
            scores[i, b] = jnp.concatenate(
                [
                    jnp.where(has_before, s[:tile], -1e30),
                    s[tile : 2 * tile],
                    jnp.where(has_after, s[2 * tile :], -1e30),
                ],
                axis=0,
            )
    for b in range(blk):
        for i in range(HEADS // 2):
            s = scores[i, b]
            e = jnp.exp(s - jnp.max(s, axis=0, keepdims=True))
            probs[i, b] = (e * (1.0 / jnp.sum(e, axis=0, keepdims=True))).astype(BF16)
    for b in range(blk):
        for h in range(HEADS):
            head = cols(h, tile=hdim)
            p = probs[h // 2, b, :, cols(h % 2, tile=tile)]
            attn_t[head, cols(b, tile=tile)] = mm(v_t[head, cols(b, 3, tile)], p).astype(BF16)


def score_grad(i, b, first, count, tile, hdim, v_nat, probs, attn_t, da):
    lanes, own = cols(i, tile=2 * hdim), cols(b, tile=tile)
    prod = da.astype(F32) * attn_t[lanes, own].astype(F32)
    total = jnp.concatenate(
        [
            jnp.sum(prod[:hdim], axis=0, keepdims=True),
            jnp.sum(prod[hdim:], axis=0, keepdims=True),
        ],
        axis=1,
    )
    dp = mm(v_nat[cols(b + first, count, tile), lanes], halves(da, hdim))
    return (probs[i, b, cols(first, count, tile), :].astype(F32) * (dp - total)).astype(BF16)


def norm_grad(dn, xn, rstd):
    xhat = xn.astype(F32)
    first = jnp.mean(dn, axis=0, keepdims=True)
    second = jnp.mean(dn * xhat, axis=0, keepdims=True)
    return rstd * (dn - first - xhat * second)


def rim_grad(b, t, tile, hdim, q_t, probs, da, ds, w_qkv, xn_t, inv, d_rim):
    width = q_t.shape[0]
    own, near, here = cols(b, tile=tile), cols(t - b, tile=tile), cols(t, tile=tile)
    for i in range(HEADS // 2):
        lanes = cols(i, tile=2 * hdim)
        after = slice(width + i * 2 * hdim, width + (i + 1) * 2 * hdim)
        d_rim[lanes, :] = mm(halves(q_t[lanes, own], hdim), ds(i), NT).astype(BF16)
        d_rim[after, :] = mm(halves(da(lanes), hdim), probs[i, b, near, :], NT).astype(BF16)
    dn = mm(w_qkv[:, width:], d_rim[...])
    return norm_grad(dn, xn_t[:, here], inv[0:1, here]).astype(BF16)


def add(a, b):
    return (a[...].astype(F32) + b[...].astype(F32)).astype(BF16)


def joined(blk, tile, das, dss):
    def da(lanes, b):
        if b == 0:
            return das[0][lanes, :]
        return das[1][lanes, cols(b - 1, tile=tile)] if b < blk - 1 else das[2][lanes, :]

    def ds(i, b, near, across):
        if b == 0:
            return dss[0][i, near, across]
        return dss[1][i, b - 1, near, across] if b < blk - 1 else dss[2][i, near, across]

    return da, ds


def end_grads(b, tile, hdim, g, w_out, v_nat, probs, attn_t, da, ds):
    da[...] = mm(w_out[...], g[...]).astype(BF16)
    for i in range(HEADS // 2):
        part = da[cols(i, tile=2 * hdim), :]
        ds[i] = score_grad(i, b, 0, 3, tile, hdim, v_nat, probs, attn_t, part)


def mid_grads(blk, tile, hdim, g, w_out, v_nat, probs, attn_t, da, ds):
    da[...] = mm(w_out[...], g[...]).astype(BF16)
    for b in range(1, blk - 1):
        for i in range(HEADS // 2):
            part = da[cols(i, tile=2 * hdim), cols(b - 1, tile=tile)]
            ds[i, b - 1] = score_grad(i, b, 0, 3, tile, hdim, v_nat, probs, attn_t, part)


def own_terms(blk, tile, hdim, first, last, q_t, k_t, probs, da, ds, d_qkv):
    width = q_t.shape[0]
    for i in range(HEADS // 2):
        lanes = cols(i, tile=2 * hdim)
        for n, left, right in (
            (1, lambda b: q_t[lanes, cols(b, tile=tile)], lambda b, near: ds(i, b, near, slice(None))),
            (2, lambda b: da(lanes, b), lambda b, near: probs[i, b, near, :]),
        ):
            total = [None] * (blk + 2)
            for b in range(max(first - 2, 0), min(last + 1, blk)):
                low, high = max(b, first), min(b + 3, last + 1)
                near = slice((low - b) * tile, (high - b) * tile)
                part = mm(halves(left(b), hdim), right(b, near), NT)
                for t in range(low, high):
                    more = part[:, cols(t - low, tile=tile)]
                    total[t] = more if total[t] is None else total[t] + more
            start = n * width + i * 2 * hdim
            for t in range(first, last + 1):
                d_qkv[start : start + 2 * hdim, cols(t - first, tile=tile)] = total[t].astype(BF16)
        for b in range(max(first - 1, 0), min(last, blk)):
            for h in (2 * i, 2 * i + 1):
                head = cols(h, tile=hdim)
                d_qkv[head, cols(b + 1 - first, tile=tile)] = mm(
                    k_t[head, cols(b, 3, tile)],
                    ds(i, b, slice(None), cols(h % 2, tile=tile)),
                ).astype(BF16)


def stage_zero_kernel(blk, tile, moved, *refs):
    if moved:
        g_prev, arrived, *refs = refs
    else:
        g, *refs = refs
    w_out, v_nat, probs, attn_t, w_qkv, xn_t, inv, q_t, *refs = refs
    if moved:
        g, *refs = refs
        g[...] = add(g_prev, arrived)
    da, ds, c_on, d_rim = refs
    hdim = g.shape[0] // HEADS
    end_grads(0, tile, hdim, g, w_out, v_nat, probs, attn_t, da, ds)
    c_on[...] = rim_grad(
        0, 0, tile, hdim, q_t, probs, lambda lanes: da[lanes, :], lambda i: ds[i, :tile, :],
        w_qkv, xn_t, inv, d_rim,
    )


def stage_mid_kernel(blk, tile, moved, *refs):
    if moved:
        g_prev, arrived, *refs = refs
    else:
        g, *refs = refs
    g_zero, da_zero, ds_zero, w_out, v_nat, probs, attn_t, w_qkv, xn_t, inv, q_t, k_t, *refs = refs
    if moved:
        g, *refs = refs
        g[...] = add(g_prev, arrived)
    da, ds, y, d_first = refs
    hdim = g.shape[0] // HEADS
    mid_grads(blk, tile, hdim, g, w_out, v_nat, probs, attn_t, da, ds)
    by_block = joined(blk, tile, (da_zero, da), (ds_zero, ds))
    own_terms(blk, tile, hdim, 1, 1, q_t, k_t, probs, *by_block, d_first)
    dn = mm(w_qkv[...], d_first[...])
    here = cols(1, tile=tile)
    y[...] = (g_zero[...].astype(F32) + norm_grad(dn, xn_t[:, here], inv[0:1, here])).astype(BF16)


def last_mid_kernel(
    blk, tile, g_prev, arrived, da_zero, ds_zero, w_out, v_nat, probs, attn_t, q_t, k_t, g, da, ds, d_low
):
    g[...] = add(g_prev, arrived)
    width = g.shape[0]
    hdim = width // HEADS
    mid_grads(blk, tile, hdim, g, w_out, v_nat, probs, attn_t, da, ds)
    d_low[:width, :tile] = jnp.zeros((width, tile), BF16)
    by_block = joined(blk, tile, (da_zero, da), (ds_zero, ds))
    own_terms(blk, tile, hdim, 0, 1, q_t, k_t, probs, *by_block, d_low)


def stage_one_kernel(blk, tile, moved, *refs):
    if moved:
        g_prev, arrived, *refs = refs
    else:
        g, *refs = refs
    w_out, v_nat, probs, attn_t, w_qkv, xn_t, inv, q_t, *refs = refs
    if moved:
        g, *refs = refs
        g[...] = add(g_prev, arrived)
    da, c_off, d_rim = refs
    hdim = g.shape[0] // HEADS
    da[...] = mm(w_out[...], g[...]).astype(BF16)
    b = blk - 1
    ds = [
        score_grad(i, b, 2, 1, tile, hdim, v_nat, probs, attn_t, da[cols(i, tile=2 * hdim), :])
        for i in range(HEADS // 2)
    ]
    c_off[...] = rim_grad(
        b, blk + 1, tile, hdim, q_t, probs, lambda lanes: da[lanes, :], lambda i: ds[i],
        w_qkv, xn_t, inv, d_rim,
    )


def stage_start_kernel(
    blk, tile, g_zero, g_mid, g_one, w_out, v_nat, probs, attn_t, w_qkv, xn_t, inv, q_t, k_t,
    da_zero, ds_zero, c_on, da_one, c_off, da_mid, ds_mid, zero, d_rim, d_rim_too, d_first,
):
    common = (w_out, v_nat, probs, attn_t, w_qkv, xn_t, inv, q_t)
    stage_zero_kernel(blk, tile, False, g_zero, *common, da_zero, ds_zero, c_on, d_rim)
    stage_one_kernel(blk, tile, False, g_one, *common, da_one, c_off, d_rim_too)
    stage_mid_kernel(
        blk, tile, False, g_mid, g_zero, da_zero, ds_zero, *common, k_t, da_mid, ds_mid, zero, d_first
    )


def stage_main_kernel(
    blk, tile, g_mid, g_one, da_zero, da_mid, da_one, ds_zero, ds_mid, w_qkv, xn_t, inv, v_nat, k_t, q_t,
    probs, attn_t, mid, one, ds_one, d_qkv,
):
    hdim = g_mid.shape[0] // HEADS
    for i in range(HEADS // 2):
        part = da_one[cols(i, tile=2 * hdim), :]
        ds_one[i] = score_grad(i, blk - 1, 0, 3, tile, hdim, v_nat, probs, attn_t, part)
    by_block = joined(blk, tile, (da_zero, da_mid, da_one), (ds_zero, ds_mid, ds_one))
    own_terms(blk, tile, hdim, 2, blk, q_t, k_t, probs, *by_block, d_qkv)
    dn = mm(w_qkv[...], d_qkv[...])
    for b in range(1, blk):
        here, place = cols(b + 1, tile=tile), cols(b - 1, tile=tile)
        out = norm_grad(dn[:, place], xn_t[:, here], inv[0:1, here])
        if b < blk - 1:
            mid[:, place] = (g_mid[:, place].astype(F32) + out).astype(BF16)
        else:
            one[...] = (g_one[...].astype(F32) + out).astype(BF16)


def add_rim_kernel(one, rim, out):
    out[...] = add(one, rim)


def last_terms_kernel(
    blk, tile, chips, after, g_prev, arrived, g_zero, g_mid, da_zero, da_mid, ds_zero, ds_mid, w_out, v_nat, k_t,
    q_t, probs, attn_t, xn_t, d_low, g_one, d_high, *refs
):
    *give, da_one, ds_one = refs
    width = g_prev.shape[0]
    hdim = width // HEADS
    g_one[...] = add(g_prev, arrived)
    end_grads(blk - 1, tile, hdim, g_one, w_out, v_nat, probs, attn_t, da_one, ds_one)
    d_high[:width, cols(blk - 1, tile=tile)] = jnp.zeros((width, tile), BF16)
    by_block = joined(blk, tile, (da_zero, da_mid, da_one), (ds_zero, ds_mid, ds_one))
    own_terms(blk, tile, hdim, 2, blk + 1, q_t, k_t, probs, *by_block, d_high)
    if give:
        core = 1 - lax.rem(lax.axis_index("dom"), 2)
        part = weight_rows(core, chips, xn_t, (d_low, d_high), attn_t, (g_zero, g_mid, g_one))
        rows = width // (2 * chips)
        for z in range(chips):
            here = slice(z * rows, (z + 1) * rows)
            for across, term in part:
                give[0][z, :, across] = term[here].astype(BF16)


def last_input_kernel(
    blk, tile, after, g_zero, g_mid, g_one, d_low, d_high, w_qkv, xn_t, inv, y, c_off
):
    outs = []
    for part in (d_low[:, tile:], d_high[...]):
        dn = mm(w_qkv[...], part)
        for n in range(part.shape[1] // tile):
            here = cols(len(outs) + 1, tile=tile)
            outs.append(norm_grad(dn[:, cols(n, tile=tile)], xn_t[:, here], inv[0:1, here]))
    c_off[...] = outs[-1].astype(BF16)
    for b in range(blk):
        own = cols(b, tile=tile)
        g = g_zero[...] if b == 0 else g_mid[:, cols(b - 1, tile=tile)] if b < blk - 1 else g_one[...]
        y[:, own] = (g.astype(F32) + outs[b]).astype(BF16)


def finish_input_kernel(blk, tile, y_t, on, off, out):
    for b in range(blk):
        part = y_t[:, cols(b, tile=tile)].astype(F32)
        if b == 0:
            part = part + on[...].astype(F32)
        if b == blk - 1:
            part = part + off[...].astype(F32)
        out[rows_of(b, blk, tile), :] = part.T.astype(BF16)


def weight_rows(core, chips, xn_t, d_qkv, attn_t, g):
    def picked(ref):
        rows = ref.shape[0] // (2 * chips)
        starts = [pl.multiple_of((2 * z + core) * rows, rows) for z in range(chips)]
        return jnp.concatenate([ref[pl.ds(s, rows), :] for s in starts], axis=0)

    def product(ref, parts):
        left, start, total = picked(ref), 0, None
        for part in parts:
            more = mm(left[:, start : start + part.shape[1]], part[...], NT)
            total = more if total is None else total + more
            start += part.shape[1]
        return total

    wide, width = d_qkv[0].shape[0], g[0].shape[0]
    return (
        (slice(0, wide), product(xn_t, d_qkv)),
        (slice(wide, wide + width), product(attn_t, g)),
    )


def mine_kernel(chips, xn_t, d_low, d_high, attn_t, g_zero, g_mid, g_one, both):
    core = lax.rem(lax.axis_index("dom"), 2)
    rows = both.shape[1]
    for across, term in weight_rows(core, chips, xn_t, (d_low, d_high), attn_t, (g_zero, g_mid, g_one)):
        for z in range(chips):
            both[z, :, across] = term[z * rows : (z + 1) * rows]


def keep_kernel(chips, steps, got, both, *outs):
    chip = lax.axis_index("dom") // 2
    start = 0
    for n, (first, second) in enumerate(steps):
        give, own = outs[2 * n : 2 * n + 2]
        across = slice(start, start + own.shape[2])
        start += own.shape[2]

        def total(distance):
            z = lax.bitwise_xor(chip, distance)
            return both[z, :, across] + got[z, :, across].astype(F32)

        give[0] = total(first).astype(BF16)
        give[1] = total(first ^ second).astype(BF16)
        own[0] = total(0)
        own[1] = total(second)


def middle_kernel(own_a, got_a, own_b, got_b, *refs):
    give_a, rest_a, give_b, rest_b = refs[-4:]
    for own, got, give, rest in ((own_b, got_b, give_b, rest_b), (own_a, got_a, give_a, rest_a)):
        rest[...] = own[0] + got[0].astype(F32)
        give[...] = (own[1] + got[1].astype(F32)).astype(BF16)


def total_kernel(rest_a, got_a, rest_b, got_b, qkv_grad, out_grad):
    width = out_grad.shape[1]
    split = rest_a.shape[1]
    qkv_grad[:, :split] = rest_a[...] + got_a[...].astype(F32)
    total = rest_b[...] + got_b[...].astype(F32)
    qkv_grad[:, split:] = total[:, : total.shape[1] - width]
    out_grad[...] = total[:, total.shape[1] - width :]


def other_core(parts):
    return [(i, i ^ 1) for i in range(parts)]


def next_chip(parts):
    return [(i, (i + 1 if i % 2 else i - 1) % parts) for i in range(parts)]


def chips_apart(parts, step):
    return [(i, i ^ (2 * step)) for i in range(parts)]


def local(layer_inputs, top_grad, w_qkv, w_out, neighbours):
    sections = lax.axis_size("section")
    parts = lax.axis_size("dom")
    blk = neighbours.shape[0]
    rows, width = top_grad.shape[1:]
    tile = rows // blk
    ext = rows + 2 * tile
    hdim = width // HEADS
    scale = 1.0 / hdim**0.5
    x = layer_inputs[0, 0]
    w_in, w_back = w_qkv[0], w_out[0]
    whole, middle, single = ((width, n) for n in (rows, rows - 2 * tile, tile))
    pairs = HEADS // 2
    pair_shape = (3 * tile, 2 * tile)
    x_on, x_off = call(
        functools.partial(pick_kernel, blk, tile), "pick", [((tile, width), BF16)] * 2, [x]
    )
    x_on = lax.ppermute(x_on, "dom", other_core(parts))
    x_off = lax.ppermute(x_off, "dom", next_chip(parts))
    *kept, q_t = call(
        functools.partial(prelude_own_kernel, blk, tile, scale), "prelude_own",
        [
            (whole, BF16), ((8, rows), F32), ((rows, width), BF16), ((rows, width), BF16),
            (whole, BF16), (whole, BF16), (whole, BF16),
        ],
        [x, w_in],
    )
    xn_t, inv, v_nat, k_t, probs, attn_t, g_zero, g_mid, g_one = call(
        functools.partial(prelude_kernel, blk, tile, scale), "prelude",
        [
            ((width, ext), BF16), ((8, ext), F32), ((ext, width), BF16), ((width, ext), BF16),
            ((pairs, blk, *pair_shape), BF16), (whole, BF16), (single, BF16), (middle, BF16),
            (single, BF16),
        ],
        [neighbours, x_on, x_off, w_in, *kept, q_t, top_grad[0]],
        scratch=[
            ((ext, width), BF16), ((width, ext), BF16), ((pairs, blk, *pair_shape), F32),
        ],
        smem=1,
    )
    common = [w_back, v_nat, probs, attn_t]
    for_rim = [w_in, xn_t, inv, q_t]
    others = (width, rows - 2 * tile)
    rim_scratch = [((2 * width, tile), BF16)]
    zero_shape = [(single, BF16), ((pairs, *pair_shape), BF16)]
    mid_shape = [(middle, BF16), ((pairs, blk - 2, *pair_shape), BF16)]
    received = []
    for k in range(sections - 1):
        here = sections - 1 - k
        if k == 0:
            da_zero, ds_zero, c_on, da_one, c_off, da_mid, ds_mid, zero = call(
                functools.partial(stage_start_kernel, blk, tile), "stage_start",
                zero_shape + [(single, BF16)] * 3 + mid_shape + [(single, BF16)],
                [g_zero, g_mid, g_one, *common, *for_rim, k_t],
                scratch=rim_scratch * 2 + [((3 * width, tile), BF16)],
            )
            on = lax.ppermute(c_on, "dom", other_core(parts))
        else:
            g_zero, da_zero, ds_zero, c_on = call(
                functools.partial(stage_zero_kernel, blk, tile, True), "stage_zero",
                [(single, BF16)]  + zero_shape + [(single, BF16)],
                [g_zero, received[0], *common, *for_rim], scratch=rim_scratch,
            )
            on = lax.ppermute(c_on, "dom", other_core(parts))
            g_mid, da_mid, ds_mid, zero = call(
                functools.partial(stage_mid_kernel, blk, tile, True), "stage_mid",
                [(middle, BF16)]  + mid_shape + [(single, BF16)],
                [g_mid, received[1], g_zero, da_zero, ds_zero, *common, *for_rim, k_t],
                scratch=[((3 * width, tile), BF16)],
            )
            g_one, da_one, c_off = call(
                functools.partial(stage_one_kernel, blk, tile, True), "stage_one",
                [(single, BF16)] * 3,
                [g_one, received[2], *common, *for_rim], scratch=rim_scratch,
            )
        zero = call(add_rim_kernel, "add_on", [(single, BF16)], [zero, on])[0]
        off = lax.ppermute(c_off, "dom", next_chip(parts))
        mid, one = call(
            functools.partial(stage_main_kernel, blk, tile), "stage_main",
            [(middle, BF16), (single, BF16)],
            [
                g_mid, g_one, da_zero, da_mid, da_one, ds_zero, ds_mid, w_in, xn_t, inv, v_nat, k_t, q_t,
                probs, attn_t,
            ],
            scratch=[((pairs, *pair_shape), BF16), ((3 * width, rows - tile), BF16)],
        )
        one = call(add_rim_kernel, "add_off", [(single, BF16)], [one, off])[0]
        received = [lax.ppermute(part, "section", [(here, here - 1)]) for part in (zero, mid, one)]
    direct = parts == 8
    chips = parts // 2
    every = 4 * width
    row = width // parts
    g_zero, da_zero, ds_zero, c_on = call(
        functools.partial(stage_zero_kernel, blk, tile, True), "last_zero",
        [(single, BF16)] + zero_shape + [(single, BF16)],
        [g_zero, received[0], *common, *for_rim], scratch=rim_scratch,
    )
    on = lax.ppermute(c_on, "dom", other_core(parts))
    g_mid, da_mid, ds_mid, d_low = call(
        functools.partial(last_mid_kernel, blk, tile), "last_mid",
        [(middle, BF16)] + mid_shape + [((3 * width, 2 * tile), BF16)],
        [g_mid, received[1], da_zero, ds_zero, *common, q_t, k_t],
    )
    g_one, d_high, *give = call(
        functools.partial(last_terms_kernel, blk, tile, chips), "last_terms",
        [(single, BF16), ((3 * width, rows), BF16)] + [((chips, row, every), BF16)] * direct,
        [
            on, g_one, received[2], g_zero, g_mid, da_zero, da_mid, ds_zero, ds_mid, w_back, v_nat, k_t, q_t,
            probs, attn_t, xn_t, d_low,
        ],
        scratch=[(single, BF16), ((pairs, *pair_shape), BF16)],
    )
    after = d_high
    if direct:
        got = lax.ppermute(give[0], "dom", other_core(parts))
        steps = ((1, 2), (2, 1))
        shares = (every // 2 + width // 4, every // 2 - width // 4)
        mine = call(
            functools.partial(mine_kernel, chips), "mine", [((chips, row, every), F32)],
            [xn_t, d_low, d_high, attn_t, g_zero, g_mid, g_one],
        )[0]
        give_a, own_a, give_b, own_b = call(
            functools.partial(keep_kernel, chips, steps), "keep",
            [((2, row, n), dtype) for n in shares for dtype in (BF16, F32)],
            [got, mine],
        )
        got_a = lax.ppermute(give_a, "dom", chips_apart(parts, steps[0][0]))
        got_b = lax.ppermute(give_b, "dom", chips_apart(parts, steps[1][0]))
        after = own_a
    y, c_off = call(
        functools.partial(last_input_kernel, blk, tile), "last_input",
        [(whole, BF16), (single, BF16)],
        [after, g_zero, g_mid, g_one, d_low, d_high, w_in, xn_t, inv],
    )
    off = lax.ppermute(c_off, "dom", next_chip(parts))
    if direct:
        give_a, rest_a, give_b, rest_b = call(
            middle_kernel, "middle", [((row, n), dtype) for n in shares for dtype in (BF16, F32)],
            [own_a, got_a, own_b, got_b, c_off],
        )
        got_b = lax.ppermute(give_b, "dom", chips_apart(parts, steps[1][1]))
        got_a = lax.ppermute(give_a, "dom", chips_apart(parts, steps[0][1]))
    y = call(
        functools.partial(finish_input_kernel, blk, tile), "finish_input", [((rows, width), BF16)],
        [y, on, off],
    )[0]
    if direct:
        qkv_grad, out_grad = call(
            total_kernel, "total", [((row, 3 * width), F32), ((row, width), F32)],
            [rest_a, got_a, rest_b, got_b],
        )
    else:
        g_t = jnp.concatenate([g_zero, g_mid, g_one], axis=1)
        d_qkv = jnp.concatenate([d_low, d_high], axis=1)
        term = jnp.concatenate([mm(xn_t, d_qkv, NT), mm(attn_t, g_t, NT)], axis=1)
        total = lax.psum_scatter(term, "dom", scatter_dimension=0, tiled=True)
        qkv_grad, out_grad = total[:, : 3 * width], total[:, 3 * width :]
    return (y[None, None], qkv_grad[None], out_grad[None])


def solution(mesh):
    placed = (
        P("section", None, "dom", None),
        P(None, "dom", None),
        P("section", None, None),
        P("section", None, None),
        P("dom", None),
    )
    return jax.shard_map(
        local,
        mesh=mesh,
        in_specs=placed,
        out_specs=(
            P("section", None, "dom", None),
            P("section", "dom", None),
            P("section", "dom", None),
        ),
        check_vma=False,
    )
```
